32 devices in a mesh: tm: 8 (over z, x), lm: 4 (over y, core).
Axes of the slice: x: 2, y: 2, z: 4, core: 2. Of those that a mesh axis runs over, the one named last changes fastest.
Arguments:
- camera_poses: float32 [6, 8192], P(None, 'tm'), may hold values from -1.5 to 1.5
- landmarks: float32 [3, 16384], P(None, ('tm', 'lm')), may hold values from -5 to 5
- odometry: float32 [6, 8192], P(None, 'tm'), may hold values from -1.5 to 1.5
- odometry_info: float32 [8192], P('tm'), may hold values from 100 to 3000
- observations: bfloat16 [3072, 3, 64, 64], P(('tm', 'lm')), may hold values from -6 to 6
- tile_frame: int32 [3072], P(('tm', 'lm')), may hold values from 0 to 15, as said below
- tile_block: int32 [3072], P(('tm', 'lm')), may hold values from 0 to 31, as said below
- tile_count: int32 [32], P(('tm', 'lm')), may hold values from 38 to 96, as said below
- block_slot: int32 [8, 32], P('tm'), may hold values from 0 to 31, each once within a row
Outputs:
- refined_poses: float32 [6, 8192], P(None, 'tm')
- refined_points: float32 [3, 16384], P(None, ('tm', 'lm'))
The draws below stay inside these ranges and needn't reach their ends.
Inputs may be any that keep to these rules, and one draw needn't show every extreme that they name: `tile_frame`: frame blocks of the slot's own time shard. `tile_block`: landmark block ids of the slot's own time shard. `tile_count`: slots from this count on hold no live tile; some device is full. `block_slot`: each row is a permutation of the 32 block ids.
All inputs are finite; a program needn't handle non-finite values.
Results may differ from the reference program's by a relative error of at most 0.0003.
Values sent between devices are 32-bit elements; how exact they have to be, the bound alone decides.
A program may use at most 64 MiB of HBM per device.

```python
import math
import jax
import jax.numpy as jnp
from jax import lax

TILE = 64
FRM_DEV = 1024
TILE_CAP = 96
ITERS = 2
FBLK_DEV = 16
FRAMES = 8192
LB_ROW = 32
LANDMARKS = 16384
TILES = 3072
N_TM = 8
N_LM = 4
DEVICES = 32


def tile_lists(key):
    base_key = jax.random.fold_in(key, 17)
    first_key, second_key = jax.random.split(base_key)
    frame_ids = jax.random.randint(first_key, (TILES,), 0, FBLK_DEV)
    spread = max(LB_ROW // FBLK_DEV, 1)
    further = jax.random.randint(second_key, (TILES,), 0, 2 * spread)
    block_ids = (frame_ids * LB_ROW // FBLK_DEV + further) % LB_ROW
    return (frame_ids.astype(jnp.int32), block_ids.astype(jnp.int32))


def draw_tile_frame(key, part):
    return tile_lists(key)[0]


def draw_tile_block(key, part):
    return tile_lists(key)[1]


def draw_tile_count(key, part):
    base_key = jax.random.fold_in(key, 29)
    first_key, second_key = jax.random.split(base_key)
    counts = jax.random.randint(first_key, (DEVICES,), TILE_CAP * 2 // 5, TILE_CAP + 1)
    busiest = jax.random.randint(second_key, (), 0, DEVICES)
    return jnp.where(jnp.arange(DEVICES) == busiest, TILE_CAP, counts).astype(jnp.int32)


def levels(rng, extent, cuts, least, high):
    def one(position, blocks):
        draws = jax.random.uniform(jax.random.fold_in(jax.random.fold_in(rng, 6), position), (blocks,), jnp.float32, least / len(cuts), high / len(cuts))
        return jnp.repeat(jnp.exp(draws), extent[position] // blocks).reshape((-1,) + (1,) * (len(extent) - position - 1))

    level = one(*cuts[0])
    for cut in cuts[1:]:
        level = level * one(*cut)
    return level


def bell_draw(key, dims, deviation, bound, cuts=(), kind=jnp.bfloat16):
    gain = levels(key, dims, cuts, -0.22, 0.18) if cuts else 1.0
    entries = jax.random.normal(key, dims, jnp.float32) * deviation * gain
    return jnp.minimum(jnp.maximum(entries, -bound), bound).astype(kind)


def setup_inputs(seed: int = 0) -> dict:
    splits = jax.random.split(jax.random.key(seed), 10)
    camera_poses = bell_draw(splits[0], (6, FRAMES), 0.3, 1.5, ((1, 8),), jnp.float32)
    landmarks = bell_draw(splits[1], (3, LANDMARKS), 1.0, 5.0, ((1, 32),), jnp.float32)
    odometry = bell_draw(splits[2], (6, FRAMES), 0.3, 1.5, ((1, 8),), jnp.float32)
    odometry_info = jnp.clip(jnp.exp(math.log(3000.0) - 3.4011974 * jax.random.uniform(splits[3], (FRAMES,), jnp.float32) ** levels(splits[3], (FRAMES,), ((0, 8),), -0.2, 0.2)), 100.0, 3000.0)
    observations = bell_draw(splits[4], (TILES, 3, TILE, TILE), 1.0, 6.0, ((0, 32),))
    tile_frame = draw_tile_frame(jax.random.fold_in(splits[9], 71), 0)
    tile_block = draw_tile_block(jax.random.fold_in(splits[9], 71), 0)
    tile_count = draw_tile_count(jax.random.fold_in(splits[9], 71), 0)
    block_slot = jax.vmap(lambda own: jax.random.permutation(own, LB_ROW))(jax.random.split(splits[8], N_TM)).reshape((N_TM, LB_ROW)).astype(jnp.int32)
    return dict(camera_poses=camera_poses, landmarks=landmarks, odometry=odometry, odometry_info=odometry_info, observations=observations, tile_frame=tile_frame, tile_block=tile_block, tile_count=tile_count, block_slot=block_slot)


robust_scale = 4.0
damping = 1.0
moment_pairs = ((0, 0), (1, 1), (2, 2), (0, 1), (0, 2), (1, 2))

def cross_product(left, right):
    return [left[1] * right[2] - left[2] * right[1], left[2] * right[0] - left[0] * right[2], left[0] * right[1] - left[1] * right[0]]

def tile_terms(rotation, offset, points, measured_tiles, live_mask):
    rotation_rows = [rotation[k][:, :, None] for k in range(3)]
    offset_rows = [offset[k][:, :, None] for k in range(3)]
    point_columns = [points[k][:, None, :] for k in range(3)]
    measured = measured_tiles.astype(jnp.float32)
    turned = cross_product(rotation_rows, point_columns)
    residual = [point_columns[k] + turned[k] + offset_rows[k] - measured[:, k] for k in range(3)]
    squared = residual[0] * residual[0] + residual[1] * residual[1] + residual[2] * residual[2]
    weight = live_mask[:, None, None] / (1.0 + squared / robust_scale)
    weighted = [weight * residual[k] for k in range(3)]
    lever = cross_product(point_columns, weighted)
    frame_terms = [lax.optimization_barrier(jnp.sum(lever[k], axis=2)) for k in range(3)]
    frame_terms += [lax.optimization_barrier(jnp.sum(weighted[k], axis=2)) for k in range(3)]
    frame_terms += [lax.optimization_barrier(jnp.sum(weight, axis=2))]
    frame_terms += [lax.optimization_barrier(jnp.sum(weight * point_columns[k], axis=2)) for k in range(3)]
    frame_terms += [lax.optimization_barrier(jnp.sum(weight * (point_columns[a] * point_columns[b]), axis=2)) for a, b in moment_pairs]
    spun = cross_product(rotation_rows, weighted)
    point_terms = [lax.optimization_barrier(jnp.sum(weighted[k] - spun[k], axis=1)) for k in range(3)]
    rotation_square = rotation_rows[0] * rotation_rows[0] + rotation_rows[1] * rotation_rows[1] + rotation_rows[2] * rotation_rows[2]
    point_terms += [lax.optimization_barrier(jnp.sum(weight * (1.0 + rotation_square), axis=1))]
    point_terms += [lax.optimization_barrier(jnp.sum(weight * (rotation_rows[a] * rotation_rows[b]), axis=1)) for a, b in moment_pairs]
    return (jnp.stack(frame_terms, axis=1), jnp.stack(point_terms, axis=1))

def block_solve(matrix, vector):
    dimension = len(vector)
    factor = [[None] * dimension for i in range(dimension)]
    inverse_diag = [None] * dimension
    for i in range(dimension):
        for j in range(i + 1):
            running = matrix[i][j]
            for k in range(j):
                running = running - factor[i][k] * factor[j][k]
            if i == j:
                factor[i][i] = jnp.sqrt(running)
                inverse_diag[i] = 1.0 / factor[i][i]
            else:
                factor[i][j] = running * inverse_diag[j]
    forward = [None] * dimension
    for i in range(dimension):
        running = vector[i]
        for k in range(i):
            running = running - factor[i][k] * forward[k]
        forward[i] = running * inverse_diag[i]
    solution = [None] * dimension
    for i in reversed(range(dimension)):
        running = forward[i]
        for k in range(i + 1, dimension):
            running = running - factor[k][i] * solution[k]
        solution[i] = running * inverse_diag[i]
    return solution

def pose_step(sums, current, link_grad, link_diag):
    moments = [sums[10 + m] for m in range(6)]
    centroid = [sums[7 + m] for m in range(3)]
    counted = sums[6]
    diagonal_add = link_diag + damping
    zero_entry = jnp.zeros_like(counted)
    rotation_block = [[moments[1] + moments[2] + diagonal_add, -moments[3], -moments[4]], [-moments[3], moments[0] + moments[2] + diagonal_add, -moments[5]], [-moments[4], -moments[5], moments[0] + moments[1] + diagonal_add]]
    cross_block = [[zero_entry, -centroid[2], centroid[1]], [centroid[2], zero_entry, -centroid[0]], [-centroid[1], centroid[0], zero_entry]]
    matrix = []
    for i in range(3):
        matrix.append(rotation_block[i] + cross_block[i])
    for i in range(3):
        offset_row = [counted + diagonal_add if i == k else zero_entry for k in range(3)]
        matrix.append([cross_block[k][i] for k in range(3)] + offset_row)
    gradient = [sums[k] + link_grad[k] for k in range(6)]
    solution = block_solve(matrix, gradient)
    return current - jnp.stack(solution)

def point_step(sums, current):
    diagonal = sums[3] + damping
    outer = [sums[4 + m] for m in range(6)]
    matrix = [[diagonal - outer[0], -outer[3], -outer[4]], [-outer[3], diagonal - outer[1], -outer[5]], [-outer[4], -outer[5], diagonal - outer[2]]]
    solution = block_solve(matrix, [sums[0], sums[1], sums[2]])
    return current - jnp.stack(solution)

def reference(camera_poses, landmarks, odometry, odometry_info, observations, tile_frame, tile_block, tile_count, block_slot):
    device_tiles = observations.reshape(DEVICES, TILE_CAP, 3, TILE, TILE)
    device_frames = tile_frame.reshape(DEVICES, TILE_CAP)
    device_blocks = tile_block.reshape(DEVICES, TILE_CAP)
    time_rows = (jnp.arange(DEVICES) // N_LM).astype(jnp.int32)
    poses = camera_poses
    points = landmarks
    for iteration in range(ITERS):

        def device_terms(carry, inputs):
            frame_total, point_total = carry
            tiles_here, frames_here, blocks_here, count_here, time_row = inputs
            frame_start = (time_row * FRM_DEV).astype(jnp.int32)
            point_start = (time_row * (LB_ROW * TILE)).astype(jnp.int32)
            pose_shard = lax.dynamic_slice_in_dim(poses, frame_start, FRM_DEV, 1).reshape(6, FBLK_DEV, TILE)
            picked = jnp.take(pose_shard, frames_here, axis=1)
            window = lax.dynamic_slice_in_dim(points, point_start, LB_ROW * TILE, 1).reshape(3, LB_ROW, TILE)
            slot_table = lax.dynamic_index_in_dim(block_slot, time_row, 0, keepdims=False)
            positions = jnp.take(slot_table, blocks_here).astype(jnp.int32)
            seen_points = jnp.take(window, positions, axis=1)
            live_mask = (jnp.arange(TILE_CAP) < count_here).astype(jnp.float32)
            frame_part, point_part = tile_terms(picked[0:3], picked[3:6], seen_points, tiles_here, live_mask)
            frame_onehot = (frames_here[:, None] == jnp.arange(FBLK_DEV)[None, :]).astype(jnp.float32)
            point_onehot = (positions[:, None] == jnp.arange(LB_ROW)[None, :]).astype(jnp.float32)
            frame_sum = jnp.einsum('tf,tqi->qfi', frame_onehot, frame_part, precision=lax.Precision.HIGHEST).reshape(16, FRM_DEV)
            point_sum = jnp.einsum('tp,tqi->qpi', point_onehot, point_part, precision=lax.Precision.HIGHEST).reshape(10, LB_ROW * TILE)
            frame_total = lax.dynamic_update_slice_in_dim(frame_total, lax.dynamic_slice_in_dim(frame_total, frame_start, FRM_DEV, 1) + frame_sum, frame_start, 1)
            point_total = lax.dynamic_update_slice_in_dim(point_total, lax.dynamic_slice_in_dim(point_total, point_start, LB_ROW * TILE, 1) + point_sum, point_start, 1)
            return ((frame_total, point_total), None)
        starting = (jnp.zeros((16, FRAMES), jnp.float32), jnp.zeros((10, LANDMARKS), jnp.float32))
        totals = lax.scan(device_terms, starting, (device_tiles, device_frames, device_blocks, tile_count, time_rows))[0]
        link_gap = poses[:, 1:] - poses[:, :-1] - odometry[:, :-1]
        link_weight = odometry_info[:-1]
        weighted_gap = link_weight[None, :] * link_gap
        zero_column = jnp.zeros((6, 1), jnp.float32)
        link_grad = jnp.concatenate([-weighted_gap, zero_column], axis=1) + jnp.concatenate([zero_column, weighted_gap], axis=1)
        zero_single = jnp.zeros((1,), jnp.float32)
        link_diag = jnp.concatenate([link_weight, zero_single]) + jnp.concatenate([zero_single, link_weight])
        next_poses = pose_step(totals[0], poses, link_grad, link_diag)
        points = point_step(totals[1], points)
        poses = next_poses
    return (poses, points)
```

```python
import functools

import jax
import jax.numpy as jnp
from jax import lax
from jax.experimental import pallas as pl
from jax.experimental.pallas import tpu as pltpu
from jax.sharding import PartitionSpec as P

TILE = 64
HALF = 32
ITERS = 2
MESH = pl.DeviceIdType.MESH

robust_scale = 4.0
damping = 1.0
moment_pairs = ((0, 0), (1, 1), (2, 2), (0, 1), (0, 2), (1, 2))


def cross_product(left, right):
    return [
        left[1] * right[2] - left[2] * right[1],
        left[2] * right[0] - left[0] * right[2],
        left[0] * right[1] - left[1] * right[0],
    ]


def block_solve(matrix, vector):
    dimension = len(vector)
    factor = [[None] * dimension for i in range(dimension)]
    inverse_diag = [None] * dimension
    for i in range(dimension):
        for j in range(i + 1):
            running = matrix[i][j]
            for k in range(j):
                running = running - factor[i][k] * factor[j][k]
            if i == j:
                factor[i][i] = jnp.sqrt(running)
                inverse_diag[i] = 1.0 / factor[i][i]
            else:
                factor[i][j] = running * inverse_diag[j]
    forward = [None] * dimension
    for i in range(dimension):
        running = vector[i]
        for k in range(i):
            running = running - factor[i][k] * forward[k]
        forward[i] = running * inverse_diag[i]
    solution = [None] * dimension
    for i in reversed(range(dimension)):
        running = forward[i]
        for k in range(i + 1, dimension):
            running = running - factor[k][i] * solution[k]
        solution[i] = running * inverse_diag[i]
    return solution


def split_rows(value):
    high = value.astype(jnp.bfloat16)
    low = (value - high.astype(jnp.float32)).astype(jnp.bfloat16)
    return high, low


def tiles_kernel(
    tile_frame,
    tile_block,
    tile_count,
    block_slot,
    poses,
    window,
    obs,
    frame_out,
    point_out,
    pose_wide,
    point_wide,
    frame_feat,
    point_feat,
    build_frame,
    build_point,
    frame_acc,
    point_acc,
):
    step = pl.program_id(0)
    frame_blocks = poses.shape[0]
    point_blocks = window.shape[0]
    step_tiles = obs.shape[0]
    lane = lax.broadcasted_iota(jnp.int32, (1, 128), 1)
    upper = lane >= TILE

    @pl.when(step == 0)
    def _():
        frame_acc[...] = jnp.zeros_like(frame_acc)
        point_acc[...] = jnp.zeros_like(point_acc)
        build_frame[...] = jnp.zeros_like(build_frame)
        build_point[...] = jnp.zeros_like(build_point)

        @pl.loop(0, frame_blocks)
        def _(block):
            columns = jnp.transpose(poses[block, 0:8, :])
            for k in range(6):
                column = columns[:, k : k + 1]
                pose_wide[block, k] = jnp.where(
                    upper,
                    jnp.broadcast_to(column[HALF:], (HALF, 128)),
                    jnp.broadcast_to(column[:HALF], (HALF, 128)),
                )

        image = lane // HALF
        for half in range(2):
            value = []
            for k in range(6):
                part = poses[:, k, :][:, half * HALF : (half + 1) * HALF]
                value.append(jnp.concatenate([part] * 4, axis=1))
            w, t = value[0:3], value[3:6]
            turned = cross_product(w, t)
            zero = jnp.zeros_like(w[0])
            rows = []
            for m in range(3):
                a, b = (m + 1) % 3, (m + 2) % 3
                coefs = [t[m] - turned[m], zero, zero, zero]
                coefs[1 + m] = zero - 1.0
                coefs[1 + b] = w[a]
                coefs[1 + a] = -w[b]
                row = coefs[0]
                for g in range(1, 4):
                    row = jnp.where(image == g, coefs[g], row)
                rows.append(row)
            first = image == 0
            square = w[0] * w[0] + w[1] * w[1] + w[2] * w[2]
            rows.append(jnp.where(first, 1.0 + square, 0.0))
            for a, b in moment_pairs:
                rows.append(jnp.where(first, w[a] * w[b], 0.0))
            for q, row in enumerate(rows):
                build_frame[:, half * 16 + q, :] = row

        spread = []
        for k in range(3):
            part = window[:, k, :]
            spread.append(jnp.concatenate([part, part], axis=1))
            point_wide[:, k, :] = spread[k]
        one = jnp.ones_like(spread[0])
        features = [one] + spread
        moments = [spread[a] * spread[b] for a, b in moment_pairs]
        for half in range(2):
            mine = upper if half else jnp.logical_not(upper)
            for f, feature in enumerate(features):
                build_point[:, half * 20 + f, :] = jnp.where(mine, feature, 0.0)
            for f, feature in enumerate(moments):
                build_point[:, half * 16 + 8 + f, :] = jnp.where(mine, feature, 0.0)

        @pl.loop(0, frame_blocks)
        def _(block):
            high, low = split_rows(build_frame[block])
            frame_feat[block, 0:32, :] = high
            frame_feat[block, 32:64, :] = low

        @pl.loop(0, point_blocks)
        def _(block):
            high, low = split_rows(build_point[block])
            point_feat[block, 0:32, :] = high
            point_feat[block, 32:64, :] = low

    def one_tile(t, slot):
        f = tile_frame[slot]
        p = block_slot[0, tile_block[slot]]
        measured = obs[t]
        measured = jnp.concatenate(
            [measured[:, :HALF, :], measured[:, HALF:, :]], axis=2
        ).astype(jnp.float32)
        x = [point_wide[p, k : k + 1, :] for k in range(3)]
        w = [pose_wide[f, k] for k in range(3)]
        turned = cross_product(w, x)
        residual = [
            x[k] + turned[k] + pose_wide[f, 3 + k] - measured[k] for k in range(3)
        ]
        squared = (
            residual[0] * residual[0] + residual[1] * residual[1] + residual[2] * residual[2]
        )
        weight = 1.0 / (1.0 + squared * (1.0 / robust_scale))
        images = jnp.concatenate(
            [weight] + [weight * measured[k] for k in range(3)], axis=0
        )
        high, low = split_rows(images)
        g = frame_feat[f]
        with_high = lax.dot_general(
            g, high, (((1,), (0,)), ((), ())), preferred_element_type=jnp.float32
        )
        with_low = lax.dot_general(
            g[0:32], low, (((1,), (0,)), ((), ())), preferred_element_type=jnp.float32
        )
        point_acc[p] += with_high[0:32] + with_high[32:64] + with_low
        h = point_feat[p]
        with_high = lax.dot_general(
            h, high, (((1,), (1,)), ((), ())), preferred_element_type=jnp.float32
        )
        with_low = lax.dot_general(
            h[0:32], low, (((1,), (1,)), ((), ())), preferred_element_type=jnp.float32
        )
        frame_acc[f] += with_high[0:32] + with_high[32:64] + with_low

    here = jnp.clip(tile_count[0] - step * step_tiles, 0, step_tiles)

    @pl.loop(0, here)
    def _(t):
        one_tile(t, step * step_tiles + t)

    @pl.when(step == pl.num_programs(0) - 1)
    def _():
        @pl.loop(0, frame_blocks)
        def _(block):
            total = frame_acc[block]
            frame_out[block, 0:8, :] = total[0:8] + total[16:24]
            frame_out[block, 8:16, :] = jnp.where(
                lane < HALF, total[8:16], pltpu.roll(total[24:32], HALF, 1)
            )

        @pl.loop(0, point_blocks)
        def _(block):
            total = point_acc[block]
            point_out[block] = jnp.where(
                upper,
                pltpu.roll(total[8:16], TILE, 1) + total[24:32],
                total[0:8] + pltpu.roll(total[16:24], TILE, 1),
            )


def tile_sums(poses, window, observations, tile_frame, tile_block, tile_count, block_slot):
    slots = observations.shape[0]
    frame_blocks, point_blocks = poses.shape[0], window.shape[0]
    steps = 4
    while slots % steps:
        steps -= 1
    whole = lambda shape: pl.BlockSpec(shape, lambda s, *_: (0,) * len(shape))
    grid_spec = pltpu.PrefetchScalarGridSpec(
        num_scalar_prefetch=4,
        grid=(steps,),
        in_specs=[
            whole(poses.shape),
            whole(window.shape),
            pl.BlockSpec((slots // steps, 3, TILE, TILE), lambda s, *_: (s, 0, 0, 0)),
        ],
        out_specs=[whole((frame_blocks, 16, 128)), whole((point_blocks, 8, 128))],
        scratch_shapes=[
            pltpu.VMEM((frame_blocks, 6, HALF, 128), jnp.float32),
            pltpu.VMEM((point_blocks, 8, 128), jnp.float32),
            pltpu.VMEM((frame_blocks, 64, 128), jnp.bfloat16),
            pltpu.VMEM((point_blocks, 64, 128), jnp.bfloat16),
            pltpu.VMEM((frame_blocks, 32, 128), jnp.float32),
            pltpu.VMEM((point_blocks, 32, 128), jnp.float32),
            pltpu.VMEM((frame_blocks, 32, 128), jnp.float32),
            pltpu.VMEM((point_blocks, 32, 128), jnp.float32),
        ],
    )
    return pl.pallas_call(
        tiles_kernel,
        grid_spec=grid_spec,
        out_shape=[
            jax.ShapeDtypeStruct((frame_blocks, 16, 128), jnp.float32),
            jax.ShapeDtypeStruct((point_blocks, 8, 128), jnp.float32),
        ],
        compiler_params=pltpu.CompilerParams(vmem_limit_bytes=48 * 1024 * 1024),
        name="tile_sums",
    )(tile_frame, tile_block, tile_count, block_slot, poses, window, observations)


def ring_peers(count):
    me = lax.axis_index("lm")
    return me, [lax.rem(me + d, count) for d in range(1, count)]


def greet(peers, row, rows):
    barrier = pltpu.get_barrier_semaphore()
    for peer in peers:
        pl.semaphore_signal(barrier, inc=1, device_id=(row, peer), device_id_type=MESH)
    if rows is None:
        pl.semaphore_wait(barrier, len(peers))
        return
    me = lax.axis_index("lm")

    @pl.when(row > 0)
    def _():
        pl.semaphore_signal(barrier, inc=1, device_id=(row - 1, me), device_id_type=MESH)

    @pl.when(row < rows - 1)
    def _():
        pl.semaphore_signal(barrier, inc=1, device_id=(row + 1, me), device_id_type=MESH)

    edges = jnp.minimum(row, 1) + jnp.minimum(rows - 1 - row, 1)
    pl.semaphore_wait(barrier, len(peers) + edges)


def gather_kernel(count, own, window, send_sem, recv_sem):
    row = lax.axis_index("tm")
    me, peers = ring_peers(count)
    blocks = own.shape[0]
    greet(peers, row, None)
    copies = []
    for d, peer in enumerate(peers):
        copies.append(
            pltpu.make_async_remote_copy(
                src_ref=own,
                dst_ref=window.at[pl.ds(me * blocks, blocks)],
                send_sem=send_sem.at[d],
                recv_sem=recv_sem.at[d],
                device_id=(row, peer),
                device_id_type=MESH,
            )
        )
        copies[-1].start()
    window[pl.ds(me * blocks, blocks)] = own[...]
    for copy in copies:
        copy.wait()


def gather_points(own, count):
    blocks = own.shape[0]
    vmem = pl.BlockSpec(memory_space=pltpu.VMEM)
    return pl.pallas_call(
        functools.partial(gather_kernel, count),
        out_shape=jax.ShapeDtypeStruct((blocks * count,) + own.shape[1:], jnp.float32),
        in_specs=[vmem],
        out_specs=vmem,
        scratch_shapes=[
            pltpu.SemaphoreType.DMA((count - 1,)),
            pltpu.SemaphoreType.DMA((count - 1,)),
        ],
        compiler_params=pltpu.CompilerParams(collective_id=0, has_side_effects=True),
        name="gather_points",
    )(own)


def pose_update(total, state, before, after, final):
    def both(row_low, row_high, start):
        return jnp.concatenate(
            [total[:, row_low, start : start + HALF], total[:, row_high, start : start + HALF]],
            axis=1,
        )

    counted = both(0, 4, 0)
    centroid = [both(1 + k, 5 + k, 0) for k in range(3)]
    moments = [total[:, 8 + m, 0:TILE] for m in range(6)]
    seen = [both(0, 4, HALF * (1 + k)) for k in range(3)]

    def lever(a, k):
        return both(1 + a, 5 + a, HALF * (1 + k))

    current = [state[:, k, :] for k in range(6)]
    w, t = current[0:3], current[3:6]
    turned = cross_product(w, centroid)
    grad_off = [centroid[k] + turned[k] + t[k] * counted - seen[k] for k in range(3)]
    matrix_rows = [
        [moments[0], moments[3], moments[4]],
        [moments[3], moments[1], moments[5]],
        [moments[4], moments[5], moments[2]],
    ]
    trace = moments[0] + moments[1] + moments[2]
    pushed = cross_product(centroid, t)
    grad_rot = []
    for k in range(3):
        a, b = (k + 1) % 3, (k + 2) % 3
        product = (
            matrix_rows[k][0] * w[0] + matrix_rows[k][1] * w[1] + matrix_rows[k][2] * w[2]
        )
        grad_rot.append(trace * w[k] - product + pushed[k] - (lever(a, b) - lever(b, a)))

    weight_before = before[:, 12, :]
    weight_after = jnp.where(final, 0.0, state[:, 12, :])
    link_grad = []
    for k in range(6):
        ahead = after[:, k, :] - current[k] - state[:, 6 + k, :]
        behind = current[k] - before[:, k, :] - before[:, 6 + k, :]
        link_grad.append(weight_before * behind - weight_after * ahead)
    diagonal_add = weight_after + weight_before + damping

    zero_entry = jnp.zeros_like(counted)
    rotation_block = [
        [moments[1] + moments[2] + diagonal_add, -moments[3], -moments[4]],
        [-moments[3], moments[0] + moments[2] + diagonal_add, -moments[5]],
        [-moments[4], -moments[5], moments[0] + moments[1] + diagonal_add],
    ]
    cross_block = [
        [zero_entry, -centroid[2], centroid[1]],
        [centroid[2], zero_entry, -centroid[0]],
        [-centroid[1], centroid[0], zero_entry],
    ]
    matrix = [rotation_block[i] + cross_block[i] for i in range(3)]
    for i in range(3):
        offset_row = [counted + diagonal_add if i == k else zero_entry for k in range(3)]
        matrix.append([cross_block[k][i] for k in range(3)] + offset_row)
    sums = grad_rot + grad_off
    step = block_solve(matrix, [sums[k] + link_grad[k] for k in range(6)])
    return [current[k] - step[k] for k in range(6)]


def point_update(total, own):
    x = [own[:, k, :] for k in range(3)]
    spread = total[:, 3, 0:TILE]
    outer = [total[:, 4 + m, 0:TILE] for m in range(4)]
    outer += [total[:, m, TILE:] for m in range(2)]
    rows = [
        [outer[0], outer[3], outer[4]],
        [outer[3], outer[1], outer[5]],
        [outer[4], outer[5], outer[2]],
    ]
    gradient = [
        total[:, k, 0:TILE]
        + spread * x[k]
        - (rows[k][0] * x[0] + rows[k][1] * x[1] + rows[k][2] * x[2])
        for k in range(3)
    ]
    diagonal = spread + damping
    matrix = [
        [diagonal - outer[0], -outer[3], -outer[4]],
        [-outer[3], diagonal - outer[1], -outer[5]],
        [-outer[4], -outer[5], diagonal - outer[2]],
    ]
    step = block_solve(matrix, gradient)
    return [x[k] - step[k] for k in range(3)]


def exchange_kernel(
    count,
    rows,
    last,
    frame_sums,
    point_sums,
    state,
    own,
    new_state,
    new_points,
    frame_in,
    point_in,
    edge_in,
    extended,
    send_sem,
    recv_sem,
    edge_send,
    edge_recv,
):
    row = lax.axis_index("tm")
    me, peers = ring_peers(count)
    frame_blocks = state.shape[0]
    share = frame_blocks // count
    own_blocks = own.shape[0]
    greet(peers, row, rows)

    def send(group, d, peer, source, target):
        copy = pltpu.make_async_remote_copy(
            src_ref=source,
            dst_ref=target,
            send_sem=send_sem.at[group, d],
            recv_sem=recv_sem.at[group, d],
            device_id=(row, peer),
            device_id_type=MESH,
        )
        copy.start()
        return copy

    def edge(side, target_row):
        block = frame_blocks - 1 if side == 0 else 0
        return pltpu.make_async_remote_copy(
            src_ref=state.at[block],
            dst_ref=edge_in.at[side],
            send_sem=edge_send.at[side],
            recv_sem=edge_recv.at[side],
            device_id=(target_row, me),
            device_id_type=MESH,
        )

    frame_copies = [
        send(0, d, peer, frame_sums.at[pl.ds(peer * share, share)], frame_in.at[d])
        for d, peer in enumerate(peers)
    ]

    @pl.when(row < rows - 1)
    def _():
        edge(0, row + 1).start()

    @pl.when(row > 0)
    def _():
        edge(1, row - 1).start()

    point_copies = [
        send(1, d, peer, point_sums.at[pl.ds(peer * own_blocks, own_blocks)], point_in.at[d])
        for d, peer in enumerate(peers)
    ]

    extended[pl.ds(1, frame_blocks)] = state[...]
    extended[0] = jnp.zeros_like(extended[0])
    extended[frame_blocks + 1] = jnp.zeros_like(extended[0])

    @pl.when(row > 0)
    def _():
        edge(0, row - 1).wait_recv()
        extended[0] = edge_in[0]

    @pl.when(row < rows - 1)
    def _():
        edge(1, row + 1).wait_recv()
        extended[frame_blocks + 1] = edge_in[1]

    first = me * share
    mine = state[pl.ds(first, share)]
    ahead = extended[pl.ds(first + 2, share)]
    behind = extended[pl.ds(first, share)]
    after = jnp.concatenate([mine[:, :, 1:], ahead[:, :, :1]], axis=2)
    before = jnp.concatenate([behind[:, :, TILE - 1 :], mine[:, :, : TILE - 1]], axis=2)
    block_index = lax.broadcasted_iota(jnp.int32, (share, TILE), 0) + first
    lane = lax.broadcasted_iota(jnp.int32, (share, TILE), 1)
    final = (block_index * TILE + lane) == jnp.where(
        row == rows - 1, frame_blocks * TILE - 1, -1
    )

    total = frame_sums[pl.ds(first, share)]
    for d, copy in enumerate(frame_copies):
        copy.wait_recv()
        total = total + frame_in[d]
    poses = pose_update(total, mine, before, after, final)
    here = pl.ds(first, share)
    new_state[here] = mine
    for k in range(6):
        new_state[here, k, :] = poses[k]
    pose_copies = [
        send(2, d, peer, new_state.at[here], new_state.at[here])
        for d, peer in enumerate(peers)
    ]

    total = point_sums[pl.ds(me * own_blocks, own_blocks)]
    for d, copy in enumerate(point_copies):
        copy.wait_recv()
        total = total + point_in[d]
    points = point_update(total, own[...])
    if last:
        for k in range(3):
            new_points[:, k, :] = points[k]
        window_copies = []
    else:
        here_points = pl.ds(me * own_blocks, own_blocks)
        new_points[here_points] = own[...]
        for k in range(3):
            new_points[here_points, k, :] = points[k]
        window_copies = [
            send(3, d, peer, new_points.at[here_points], new_points.at[here_points])
            for d, peer in enumerate(peers)
        ]

    for copy in frame_copies + point_copies:
        copy.wait_send()
    for copy in pose_copies + window_copies:
        copy.wait()

    @pl.when(row < rows - 1)
    def _():
        edge(0, row + 1).wait_send()

    @pl.when(row > 0)
    def _():
        edge(1, row - 1).wait_send()


def exchange(frame_sums, point_sums, state, own, count, rows, last):
    frame_blocks = state.shape[0]
    own_blocks = own.shape[0]
    share = frame_blocks // count
    vmem = pl.BlockSpec(memory_space=pltpu.VMEM)
    point_blocks = own_blocks if last else own_blocks * count
    return pl.pallas_call(
        functools.partial(exchange_kernel, count, rows, last),
        out_shape=[
            jax.ShapeDtypeStruct(state.shape, jnp.float32),
            jax.ShapeDtypeStruct((point_blocks,) + own.shape[1:], jnp.float32),
        ],
        in_specs=[vmem] * 4,
        out_specs=[vmem] * 2,
        scratch_shapes=[
            pltpu.VMEM((count - 1, share, 16, 128), jnp.float32),
            pltpu.VMEM((count - 1, own_blocks, 8, 128), jnp.float32),
            pltpu.VMEM((2, 16, TILE), jnp.float32),
            pltpu.VMEM((frame_blocks + 2, 16, TILE), jnp.float32),
            pltpu.SemaphoreType.DMA((4, count - 1)),
            pltpu.SemaphoreType.DMA((4, count - 1)),
            pltpu.SemaphoreType.DMA((2,)),
            pltpu.SemaphoreType.DMA((2,)),
        ],
        compiler_params=pltpu.CompilerParams(
            collective_id=2 if last else 1, has_side_effects=True
        ),
        name="exchange_last" if last else "exchange_first",
    )(frame_sums, point_sums, state, own)


def on_device(
    camera_poses,
    landmarks,
    odometry,
    odometry_info,
    observations,
    tile_frame,
    tile_block,
    tile_count,
    block_slot,
):
    frames = camera_poses.shape[1]
    blocks = frames // TILE
    rows, count = lax.axis_size("tm"), lax.axis_size("lm")
    own_blocks = landmarks.shape[1] // TILE
    packed = jnp.concatenate(
        [camera_poses, odometry, odometry_info[None, :], jnp.zeros((3, frames), jnp.float32)],
        axis=0,
    )
    state = jnp.transpose(packed.reshape(16, blocks, TILE), (1, 0, 2))
    own = jnp.concatenate([landmarks, jnp.zeros((5, own_blocks * TILE), jnp.float32)], axis=0)
    own = jnp.transpose(own.reshape(8, own_blocks, TILE), (1, 0, 2))
    window = gather_points(own, count)
    for iteration in range(ITERS):
        last = iteration == ITERS - 1
        frame_sums, point_sums = tile_sums(
            state, window, observations, tile_frame, tile_block, tile_count, block_slot
        )
        state, window = exchange(frame_sums, point_sums, state, own, count, rows, last)
        if not last:
            own = lax.dynamic_slice_in_dim(
                window, lax.axis_index("lm") * own_blocks, own_blocks, 0
            )
    poses = jnp.transpose(state[:, 0:6, :], (1, 0, 2)).reshape(6, frames)
    points = jnp.transpose(window[:, 0:3, :], (1, 0, 2)).reshape(3, own_blocks * TILE)
    return (poses, points)


def solution(mesh):
    return jax.shard_map(
        on_device,
        mesh=mesh,
        in_specs=(
            P(None, "tm"),
            P(None, ("tm", "lm")),
            P(None, "tm"),
            P("tm"),
            P(("tm", "lm"), None, None, None),
            P(("tm", "lm")),
            P(("tm", "lm")),
            P(("tm", "lm")),
            P("tm", None),
        ),
        out_specs=(P(None, "tm"), P(None, ("tm", "lm"))),
        check_vma=False,
    )
```

```python
import functools

import jax
import jax.numpy as jnp
from jax import lax
from jax.experimental import pallas as pl
from jax.experimental.pallas import tpu as pltpu
from jax.sharding import PartitionSpec as P

TILE = 64
HALF = 32
ITERS = 2
MESH = pl.DeviceIdType.MESH

robust_scale = 4.0
damping = 1.0
moment_pairs = ((0, 0), (1, 1), (2, 2), (0, 1), (0, 2), (1, 2))


def cross_product(left, right):
    return [
        left[1] * right[2] - left[2] * right[1],
        left[2] * right[0] - left[0] * right[2],
        left[0] * right[1] - left[1] * right[0],
    ]


def block_solve(matrix, vector):
    dimension = len(vector)
    factor = [[None] * dimension for i in range(dimension)]
    inverse_diag = [None] * dimension
    for i in range(dimension):
        for j in range(i + 1):
            running = matrix[i][j]
            for k in range(j):
                running = running - factor[i][k] * factor[j][k]
            if i == j:
                factor[i][i] = jnp.sqrt(running)
                inverse_diag[i] = 1.0 / factor[i][i]
            else:
                factor[i][j] = running * inverse_diag[j]
    forward = [None] * dimension
    for i in range(dimension):
        running = vector[i]
        for k in range(i):
            running = running - factor[i][k] * forward[k]
        forward[i] = running * inverse_diag[i]
    solution = [None] * dimension
    for i in reversed(range(dimension)):
        running = forward[i]
        for k in range(i + 1, dimension):
            running = running - factor[k][i] * solution[k]
        solution[i] = running * inverse_diag[i]
    return solution


def split_rows(value):
    high = value.astype(jnp.bfloat16)
    low = (value - high.astype(jnp.float32)).astype(jnp.bfloat16)
    return high, low


def repack_kernel(obs, packed):
    part = pl.program_id(0)
    slots = obs.shape[3]
    images = packed.shape[0] // slots
    row = lax.broadcasted_iota(jnp.int32, (slots, slots), 0)
    column = lax.broadcasted_iota(jnp.int32, (slots, slots), 1)
    identity = jnp.where(row == column, 1.0, 0.0).astype(jnp.bfloat16)

    @pl.loop(0, HALF, step=4)
    def _(start):
        for u in range(4):
            i = start + u
            pairs = jnp.concatenate([obs[0, i], obs[0, i + HALF]], axis=0)
            turned = lax.dot_general(
                identity, pairs, (((1,), (1,)), ((), ())), preferred_element_type=jnp.float32
            )
            packed[pl.ds(part * HALF + i, slots, stride=images), :] = turned


def repack(observations):
    slots = observations.shape[0]
    by_tile = jnp.transpose(observations, (1, 2, 3, 0))
    packed = pl.pallas_call(
        repack_kernel,
        grid=(3,),
        in_specs=[pl.BlockSpec((1, TILE, TILE, slots), lambda s: (s, 0, 0, 0))],
        out_specs=pl.BlockSpec((slots * 3 * HALF, 128), lambda s: (0, 0)),
        out_shape=jax.ShapeDtypeStruct((slots * 3 * HALF, 128), jnp.float32),
        compiler_params=pltpu.CompilerParams(vmem_limit_bytes=48 * 1024 * 1024),
        name="repack",
    )(by_tile)
    return packed.reshape(slots, 3 * HALF, 128)


def tiles_kernel(
    unroll,
    tile_frame,
    tile_block,
    tile_count,
    block_slot,
    poses,
    window,
    obs,
    frame_out,
    point_out,
    pose_wide,
    point_wide,
    frame_feat,
    point_feat,
    build_frame,
    build_point,
    frame_acc,
    point_acc,
):
    step = pl.program_id(0)
    frame_blocks = poses.shape[0]
    point_blocks = window.shape[0]
    step_tiles = obs.shape[0]
    lane = lax.broadcasted_iota(jnp.int32, (1, 128), 1)
    upper = lane >= TILE

    @pl.when(step == 0)
    def _():
        frame_acc[...] = jnp.zeros_like(frame_acc)
        point_acc[...] = jnp.zeros_like(point_acc)
        build_frame[...] = jnp.zeros_like(build_frame)
        build_point[...] = jnp.zeros_like(build_point)

        @pl.loop(0, frame_blocks)
        def _(block):
            columns = jnp.transpose(poses[block, 0:8, :])
            for k in range(6):
                column = columns[:, k : k + 1]
                pose_wide[block, k] = jnp.where(
                    upper,
                    jnp.broadcast_to(column[HALF:], (HALF, 128)),
                    jnp.broadcast_to(column[:HALF], (HALF, 128)),
                )

        image = lane // HALF
        for half in range(2):
            value = []
            for k in range(6):
                part = poses[:, k, :][:, half * HALF : (half + 1) * HALF]
                value.append(jnp.concatenate([part] * 4, axis=1))
            w, t = value[0:3], value[3:6]
            turned = cross_product(w, t)
            zero = jnp.zeros_like(w[0])
            rows = []
            for m in range(3):
                a, b = (m + 1) % 3, (m + 2) % 3
                coefs = [t[m] - turned[m], zero, zero, zero]
                coefs[1 + m] = zero - 1.0
                coefs[1 + b] = w[a]
                coefs[1 + a] = -w[b]
                row = coefs[0]
                for g in range(1, 4):
                    row = jnp.where(image == g, coefs[g], row)
                rows.append(row)
            first = image == 0
            square = w[0] * w[0] + w[1] * w[1] + w[2] * w[2]
            rows.append(jnp.where(first, 1.0 + square, 0.0))
            for a, b in moment_pairs:
                rows.append(jnp.where(first, w[a] * w[b], 0.0))
            for q, row in enumerate(rows):
                build_frame[:, half * 16 + q, :] = row

        spread = []
        for k in range(3):
            part = window[:, k, :]
            spread.append(jnp.concatenate([part, part], axis=1))
            point_wide[:, k, :] = spread[k]
        one = jnp.ones_like(spread[0])
        features = [one] + spread
        moments = [spread[a] * spread[b] for a, b in moment_pairs]
        for half in range(2):
            mine = upper if half else jnp.logical_not(upper)
            for f, feature in enumerate(features):
                build_point[:, half * 20 + f, :] = jnp.where(mine, feature, 0.0)
            for f, feature in enumerate(moments):
                build_point[:, half * 16 + 8 + f, :] = jnp.where(mine, feature, 0.0)

        @pl.loop(0, frame_blocks)
        def _(block):
            high, low = split_rows(build_frame[block])
            frame_feat[block, 0:32, :] = high
            frame_feat[block, 32:64, :] = low

        @pl.loop(0, point_blocks)
        def _(block):
            high, low = split_rows(build_point[block])
            point_feat[block, 0:32, :] = high
            point_feat[block, 32:64, :] = low

    def one_tile(t, slot):
        live = slot < tile_count[0]
        f = jnp.where(live, tile_frame[slot], 0)
        p = jnp.where(live, block_slot[0, tile_block[slot]], 0)
        measured = [obs[t, k * HALF : (k + 1) * HALF, :] for k in range(3)]
        x = [point_wide[p, k : k + 1, :] for k in range(3)]
        w = [pose_wide[f, k] for k in range(3)]
        turned = cross_product(w, x)
        residual = [
            x[k] + turned[k] + pose_wide[f, 3 + k] - measured[k] for k in range(3)
        ]
        squared = (
            residual[0] * residual[0] + residual[1] * residual[1] + residual[2] * residual[2]
        )
        weight = jnp.where(live, 1.0, 0.0) / (1.0 + squared * (1.0 / robust_scale))
        images = jnp.concatenate(
            [weight] + [weight * measured[k] for k in range(3)], axis=0
        )
        high, low = split_rows(images)
        sums = []
        for features, dims in ((frame_feat[f], (1, 0)), (point_feat[p], (1, 1))):
            dims = (((dims[0],), (dims[1],)), ((), ()))
            with_high = lax.dot_general(
                features, high, dims, preferred_element_type=jnp.float32
            )
            with_low = lax.dot_general(
                features[0:32], low, dims, preferred_element_type=jnp.float32
            )
            sums.append(with_high[0:32] + with_high[32:64] + with_low)
        return f, p, sums

    here = jnp.clip(tile_count[0] - step * step_tiles, 0, step_tiles)

    @pl.loop(0, (here + unroll - 1) // unroll)
    def _(group):
        done = []
        for u in range(unroll):
            t = group * unroll + u
            done.append(one_tile(t, step * step_tiles + t))
        for f, p, sums in done:
            point_acc[p] += sums[0]
            frame_acc[f] += sums[1]

    @pl.when(step == pl.num_programs(0) - 1)
    def _():
        @pl.loop(0, frame_blocks)
        def _(block):
            total = frame_acc[block]
            frame_out[block, 0:8, :] = total[0:8] + total[16:24]
            frame_out[block, 8:16, :] = jnp.where(
                lane < HALF, total[8:16], pltpu.roll(total[24:32], HALF, 1)
            )

        @pl.loop(0, point_blocks)
        def _(block):
            total = point_acc[block]
            point_out[block] = jnp.where(
                upper,
                pltpu.roll(total[8:16], TILE, 1) + total[24:32],
                total[0:8] + pltpu.roll(total[16:24], TILE, 1),
            )


def tile_sums(poses, window, observations, tile_frame, tile_block, tile_count, block_slot):
    slots = observations.shape[0]
    frame_blocks, point_blocks = poses.shape[0], window.shape[0]
    steps = 2 if slots % 2 == 0 else 1
    unroll = max(u for u in (1, 2, 3, 4) if slots // steps % u == 0)
    whole = lambda shape: pl.BlockSpec(shape, lambda s, *_: (0,) * len(shape))
    grid_spec = pltpu.PrefetchScalarGridSpec(
        num_scalar_prefetch=4,
        grid=(steps,),
        in_specs=[
            whole(poses.shape),
            whole(window.shape),
            pl.BlockSpec((slots // steps, 3 * HALF, 128), lambda s, *_: (s, 0, 0)),
        ],
        out_specs=[whole((frame_blocks, 16, 128)), whole((point_blocks, 8, 128))],
        scratch_shapes=[
            pltpu.VMEM((frame_blocks, 6, HALF, 128), jnp.float32),
            pltpu.VMEM((point_blocks, 8, 128), jnp.float32),
            pltpu.VMEM((frame_blocks, 64, 128), jnp.bfloat16),
            pltpu.VMEM((point_blocks, 64, 128), jnp.bfloat16),
            pltpu.VMEM((frame_blocks, 32, 128), jnp.float32),
            pltpu.VMEM((point_blocks, 32, 128), jnp.float32),
            pltpu.VMEM((frame_blocks, 32, 128), jnp.float32),
            pltpu.VMEM((point_blocks, 32, 128), jnp.float32),
        ],
    )
    return pl.pallas_call(
        functools.partial(tiles_kernel, unroll),
        grid_spec=grid_spec,
        out_shape=[
            jax.ShapeDtypeStruct((frame_blocks, 16, 128), jnp.float32),
            jax.ShapeDtypeStruct((point_blocks, 8, 128), jnp.float32),
        ],
        compiler_params=pltpu.CompilerParams(vmem_limit_bytes=48 * 1024 * 1024),
        name="tile_sums",
    )(tile_frame, tile_block, tile_count, block_slot, poses, window, observations)


def ring_peers(count):
    me = lax.axis_index("lm")
    return me, [lax.rem(me + d, count) for d in range(1, count)]


def greet(peers, row, rows):
    barrier = pltpu.get_barrier_semaphore()
    for peer in peers:
        pl.semaphore_signal(barrier, inc=1, device_id=(row, peer), device_id_type=MESH)
    if rows is None:
        pl.semaphore_wait(barrier, len(peers))
        return
    me = lax.axis_index("lm")

    @pl.when(row > 0)
    def _():
        pl.semaphore_signal(barrier, inc=1, device_id=(row - 1, me), device_id_type=MESH)

    @pl.when(row < rows - 1)
    def _():
        pl.semaphore_signal(barrier, inc=1, device_id=(row + 1, me), device_id_type=MESH)

    edges = jnp.minimum(row, 1) + jnp.minimum(rows - 1 - row, 1)
    pl.semaphore_wait(barrier, len(peers) + edges)


def gather_kernel(count, own, window, send_sem, recv_sem):
    row = lax.axis_index("tm")
    me, peers = ring_peers(count)
    blocks = own.shape[0]
    greet(peers, row, None)
    copies = []
    for d, peer in enumerate(peers):
        copies.append(
            pltpu.make_async_remote_copy(
                src_ref=own,
                dst_ref=window.at[pl.ds(me * blocks, blocks)],
                send_sem=send_sem.at[d],
                recv_sem=recv_sem.at[d],
                device_id=(row, peer),
                device_id_type=MESH,
            )
        )
        copies[-1].start()
    window[pl.ds(me * blocks, blocks)] = own[...]
    for copy in copies:
        copy.wait()


def gather_points(own, count):
    blocks = own.shape[0]
    vmem = pl.BlockSpec(memory_space=pltpu.VMEM)
    return pl.pallas_call(
        functools.partial(gather_kernel, count),
        out_shape=jax.ShapeDtypeStruct((blocks * count,) + own.shape[1:], jnp.float32),
        in_specs=[vmem],
        out_specs=vmem,
        scratch_shapes=[
            pltpu.SemaphoreType.DMA((count - 1,)),
            pltpu.SemaphoreType.DMA((count - 1,)),
        ],
        compiler_params=pltpu.CompilerParams(collective_id=0, has_side_effects=True),
        name="gather_points",
    )(own)


def pose_update(total, state, before, after, final):
    def both(row_low, row_high, start):
        return jnp.concatenate(
            [total[:, row_low, start : start + HALF], total[:, row_high, start : start + HALF]],
            axis=1,
        )

    counted = both(0, 4, 0)
    centroid = [both(1 + k, 5 + k, 0) for k in range(3)]
    moments = [total[:, 8 + m, 0:TILE] for m in range(6)]
    seen = [both(0, 4, HALF * (1 + k)) for k in range(3)]

    def lever(a, k):
        return both(1 + a, 5 + a, HALF * (1 + k))

    current = [state[:, k, :] for k in range(6)]
    w, t = current[0:3], current[3:6]
    turned = cross_product(w, centroid)
    grad_off = [centroid[k] + turned[k] + t[k] * counted - seen[k] for k in range(3)]
    matrix_rows = [
        [moments[0], moments[3], moments[4]],
        [moments[3], moments[1], moments[5]],
        [moments[4], moments[5], moments[2]],
    ]
    trace = moments[0] + moments[1] + moments[2]
    pushed = cross_product(centroid, t)
    grad_rot = []
    for k in range(3):
        a, b = (k + 1) % 3, (k + 2) % 3
        product = (
            matrix_rows[k][0] * w[0] + matrix_rows[k][1] * w[1] + matrix_rows[k][2] * w[2]
        )
        grad_rot.append(trace * w[k] - product + pushed[k] - (lever(a, b) - lever(b, a)))

    weight_before = before[:, 12, :]
    weight_after = jnp.where(final, 0.0, state[:, 12, :])
    link_grad = []
    for k in range(6):
        ahead = after[:, k, :] - current[k] - state[:, 6 + k, :]
        behind = current[k] - before[:, k, :] - before[:, 6 + k, :]
        link_grad.append(weight_before * behind - weight_after * ahead)
    diagonal_add = weight_after + weight_before + damping

    zero_entry = jnp.zeros_like(counted)
    rotation_block = [
        [moments[1] + moments[2] + diagonal_add, -moments[3], -moments[4]],
        [-moments[3], moments[0] + moments[2] + diagonal_add, -moments[5]],
        [-moments[4], -moments[5], moments[0] + moments[1] + diagonal_add],
    ]
    cross_block = [
        [zero_entry, -centroid[2], centroid[1]],
        [centroid[2], zero_entry, -centroid[0]],
        [-centroid[1], centroid[0], zero_entry],
    ]
    matrix = [rotation_block[i] + cross_block[i] for i in range(3)]
    for i in range(3):
        offset_row = [counted + diagonal_add if i == k else zero_entry for k in range(3)]
        matrix.append([cross_block[k][i] for k in range(3)] + offset_row)
    sums = grad_rot + grad_off
    step = block_solve(matrix, [sums[k] + link_grad[k] for k in range(6)])
    return [current[k] - step[k] for k in range(6)]


def point_update(total, own):
    x = [own[:, k, :] for k in range(3)]
    spread = total[:, 3, 0:TILE]
    outer = [total[:, 4 + m, 0:TILE] for m in range(4)]
    outer += [total[:, m, TILE:] for m in range(2)]
    rows = [
        [outer[0], outer[3], outer[4]],
        [outer[3], outer[1], outer[5]],
        [outer[4], outer[5], outer[2]],
    ]
    gradient = [
        total[:, k, 0:TILE]
        + spread * x[k]
        - (rows[k][0] * x[0] + rows[k][1] * x[1] + rows[k][2] * x[2])
        for k in range(3)
    ]
    diagonal = spread + damping
    matrix = [
        [diagonal - outer[0], -outer[3], -outer[4]],
        [-outer[3], diagonal - outer[1], -outer[5]],
        [-outer[4], -outer[5], diagonal - outer[2]],
    ]
    step = block_solve(matrix, gradient)
    return [x[k] - step[k] for k in range(3)]


def exchange_kernel(
    count,
    rows,
    last,
    frame_sums,
    point_sums,
    state,
    own,
    new_state,
    new_own,
    new_window,
    frame_in,
    point_in,
    edge_in,
    extended,
    send_sem,
    recv_sem,
    edge_send,
    edge_recv,
):
    row = lax.axis_index("tm")
    me, peers = ring_peers(count)
    frame_blocks = state.shape[0]
    share = frame_blocks // count
    own_blocks = own.shape[0]
    greet(peers, row, rows)

    def send(group, d, peer, source, target):
        copy = pltpu.make_async_remote_copy(
            src_ref=source,
            dst_ref=target,
            send_sem=send_sem.at[group, d],
            recv_sem=recv_sem.at[group, d],
            device_id=(row, peer),
            device_id_type=MESH,
        )
        copy.start()
        return copy

    def edge(side, target_row):
        block = frame_blocks - 1 if side == 0 else 0
        return pltpu.make_async_remote_copy(
            src_ref=state.at[block],
            dst_ref=edge_in.at[side],
            send_sem=edge_send.at[side],
            recv_sem=edge_recv.at[side],
            device_id=(target_row, me),
            device_id_type=MESH,
        )

    frame_copies = [
        send(0, d, peer, frame_sums.at[pl.ds(peer * share, share)], frame_in.at[d])
        for d, peer in enumerate(peers)
    ]

    @pl.when(row < rows - 1)
    def _():
        edge(0, row + 1).start()

    @pl.when(row > 0)
    def _():
        edge(1, row - 1).start()

    point_copies = [
        send(1, d, peer, point_sums.at[pl.ds(peer * own_blocks, own_blocks)], point_in.at[d])
        for d, peer in enumerate(peers)
    ]

    extended[pl.ds(1, frame_blocks)] = state[...]
    extended[0] = jnp.zeros_like(extended[0])
    extended[frame_blocks + 1] = jnp.zeros_like(extended[0])

    @pl.when(row > 0)
    def _():
        edge(0, row - 1).wait_recv()
        extended[0] = edge_in[0]

    @pl.when(row < rows - 1)
    def _():
        edge(1, row + 1).wait_recv()
        extended[frame_blocks + 1] = edge_in[1]

    first = me * share
    mine = state[pl.ds(first, share)]
    ahead = extended[pl.ds(first + 2, share)]
    behind = extended[pl.ds(first, share)]
    after = jnp.concatenate([mine[:, :, 1:], ahead[:, :, :1]], axis=2)
    before = jnp.concatenate([behind[:, :, TILE - 1 :], mine[:, :, : TILE - 1]], axis=2)
    block_index = lax.broadcasted_iota(jnp.int32, (share, TILE), 0) + first
    lane = lax.broadcasted_iota(jnp.int32, (share, TILE), 1)
    final = (block_index * TILE + lane) == jnp.where(
        row == rows - 1, frame_blocks * TILE - 1, -1
    )

    total = frame_sums[pl.ds(first, share)]
    for d, copy in enumerate(frame_copies):
        copy.wait_recv()
        total = total + frame_in[d]
    poses = pose_update(total, mine, before, after, final)
    here = pl.ds(first, share)
    new_state[here] = mine
    for k in range(6):
        new_state[here, k, :] = poses[k]
    pose_copies = [
        send(2, d, peer, new_state.at[here], new_state.at[here])
        for d, peer in enumerate(peers)
    ]

    total = point_sums[pl.ds(me * own_blocks, own_blocks)]
    for d, copy in enumerate(point_copies):
        copy.wait_recv()
        total = total + point_in[d]
    points = point_update(total, own[...])
    new_own[...] = own[...]
    for k in range(3):
        new_own[:, k, :] = points[k]
    window_copies = []
    if last:
        new_window[...] = jnp.zeros_like(new_window)
    else:
        here_points = pl.ds(me * own_blocks, own_blocks)
        window_copies = [
            send(3, d, peer, new_own, new_window.at[here_points])
            for d, peer in enumerate(peers)
        ]
        new_window[here_points] = new_own[...]

    for copy in frame_copies + point_copies:
        copy.wait_send()
    for copy in pose_copies + window_copies:
        copy.wait()

    @pl.when(row < rows - 1)
    def _():
        edge(0, row + 1).wait_send()

    @pl.when(row > 0)
    def _():
        edge(1, row - 1).wait_send()


def exchange(frame_sums, point_sums, state, own, count, rows, last):
    frame_blocks = state.shape[0]
    own_blocks = own.shape[0]
    share = frame_blocks // count
    vmem = pl.BlockSpec(memory_space=pltpu.VMEM)
    point_blocks = 1 if last else own_blocks * count
    return pl.pallas_call(
        functools.partial(exchange_kernel, count, rows, last),
        out_shape=[
            jax.ShapeDtypeStruct(state.shape, jnp.float32),
            jax.ShapeDtypeStruct(own.shape, jnp.float32),
            jax.ShapeDtypeStruct((point_blocks,) + own.shape[1:], jnp.float32),
        ],
        in_specs=[vmem] * 4,
        out_specs=[vmem] * 3,
        scratch_shapes=[
            pltpu.VMEM((count - 1, share, 16, 128), jnp.float32),
            pltpu.VMEM((count - 1, own_blocks, 8, 128), jnp.float32),
            pltpu.VMEM((2, 16, TILE), jnp.float32),
            pltpu.VMEM((frame_blocks + 2, 16, TILE), jnp.float32),
            pltpu.SemaphoreType.DMA((4, count - 1)),
            pltpu.SemaphoreType.DMA((4, count - 1)),
            pltpu.SemaphoreType.DMA((2,)),
            pltpu.SemaphoreType.DMA((2,)),
        ],
        compiler_params=pltpu.CompilerParams(
            collective_id=2 if last else 1, has_side_effects=True
        ),
        name="exchange_last" if last else "exchange_first",
    )(frame_sums, point_sums, state, own)


def on_device(
    camera_poses,
    landmarks,
    odometry,
    odometry_info,
    observations,
    tile_frame,
    tile_block,
    tile_count,
    block_slot,
):
    frames = camera_poses.shape[1]
    blocks = frames // TILE
    rows, count = lax.axis_size("tm"), lax.axis_size("lm")
    own_blocks = landmarks.shape[1] // TILE
    packed = jnp.concatenate(
        [camera_poses, odometry, odometry_info[None, :], jnp.zeros((3, frames), jnp.float32)],
        axis=0,
    )
    state = jnp.transpose(packed.reshape(16, blocks, TILE), (1, 0, 2))
    own = jnp.concatenate([landmarks, jnp.zeros((5, own_blocks * TILE), jnp.float32)], axis=0)
    own = jnp.transpose(own.reshape(8, own_blocks, TILE), (1, 0, 2))
    observations = repack(observations)
    window = gather_points(own, count)
    for iteration in range(ITERS):
        last = iteration == ITERS - 1
        frame_sums, point_sums = tile_sums(
            state, window, observations, tile_frame, tile_block, tile_count, block_slot
        )
        state, own, window = exchange(frame_sums, point_sums, state, own, count, rows, last)
    poses = jnp.transpose(state[:, 0:6, :], (1, 0, 2)).reshape(6, frames)
    points = jnp.transpose(own[:, 0:3, :], (1, 0, 2)).reshape(3, own_blocks * TILE)
    return (poses, points)


def solution(mesh):
    return jax.shard_map(
        on_device,
        mesh=mesh,
        in_specs=(
            P(None, "tm"),
            P(None, ("tm", "lm")),
            P(None, "tm"),
            P("tm"),
            P(("tm", "lm"), None, None, None),
            P(("tm", "lm")),
            P(("tm", "lm")),
            P(("tm", "lm")),
            P("tm", None),
        ),
        out_specs=(P(None, "tm"), P(None, ("tm", "lm"))),
        check_vma=False,
    )
```

```python
import functools

import jax
import jax.numpy as jnp
from jax import lax
from jax.experimental import pallas as pl
from jax.experimental.pallas import tpu as pltpu
from jax.sharding import PartitionSpec as P

TILE = 64
HALF = 32
ITERS = 2
VMEM_LIMIT = 60 * 1024 * 1024
MESH = pl.DeviceIdType.MESH

robust_scale = 4.0
damping = 1.0
moment_pairs = ((0, 0), (1, 1), (2, 2), (0, 1), (0, 2), (1, 2))


def cross_product(left, right):
    return [
        left[1] * right[2] - left[2] * right[1],
        left[2] * right[0] - left[0] * right[2],
        left[0] * right[1] - left[1] * right[0],
    ]


def block_solve(matrix, vector):
    dimension = len(vector)
    factor = [[None] * dimension for i in range(dimension)]
    inverse_diag = [None] * dimension
    for i in range(dimension):
        for j in range(i + 1):
            running = matrix[i][j]
            for k in range(j):
                running = running - factor[i][k] * factor[j][k]
            if i == j:
                factor[i][i] = jnp.sqrt(running)
                inverse_diag[i] = 1.0 / factor[i][i]
            else:
                factor[i][j] = running * inverse_diag[j]
    forward = [None] * dimension
    for i in range(dimension):
        running = vector[i]
        for k in range(i):
            running = running - factor[i][k] * forward[k]
        forward[i] = running * inverse_diag[i]
    solution = [None] * dimension
    for i in reversed(range(dimension)):
        running = forward[i]
        for k in range(i + 1, dimension):
            running = running - factor[k][i] * solution[k]
        solution[i] = running * inverse_diag[i]
    return solution


def split_rows(value):
    high = value.astype(jnp.bfloat16)
    low = (value - high.astype(jnp.float32)).astype(jnp.bfloat16)
    return high, low


def pick_rows(rows, sub, default=0.0):
    value = jnp.full(sub.shape, default, jnp.float32)
    for s, row in rows.items():
        value = jnp.where(sub == s, row, value)
    return value


def frame_features(block_poses, sub, lane):
    image = lane // HALF
    first = image == 0
    features, linear = [], {}
    for half in range(2):
        part = block_poses[:, half * HALF : (half + 1) * HALF]
        part = jnp.concatenate([part] * 4, axis=1)
        value = [jnp.broadcast_to(part[k : k + 1], (8, 128)) for k in range(6)]
        w, t = value[0:3], value[3:6]
        turned = cross_product(w, t)
        rows = {}
        for m in range(3):
            a, b = (m + 1) % 3, (m + 2) % 3
            row = jnp.where(first, t[m] - turned[m], 0.0)
            row = jnp.where(image == 1 + m, -1.0, row)
            row = jnp.where(image == 1 + b, w[a], row)
            rows[m] = jnp.where(image == 1 + a, -w[b], row)
        square = w[0] * w[0] + w[1] * w[1] + w[2] * w[2]
        rows[3] = jnp.where(first, 1.0 + square, 0.0)
        products = [jnp.where(first, w[a] * w[b], 0.0) for a, b in moment_pairs]
        for m in range(4):
            rows[4 + m] = products[m]
        features.append(pick_rows(rows, sub))
        features.append(pick_rows({0: products[4], 1: products[5]}, sub))
        second, third = image == 1, image == 2
        zero = jnp.zeros_like(w[0])

        def by_part(x, y, z):
            return jnp.where(first, x, jnp.where(second, y, jnp.where(third, z, zero)))

        linear[half * 4] = by_part(t[0], t[1], t[2])
        linear[half * 4 + 1] = by_part(1.0, w[2], -w[1])
        linear[half * 4 + 2] = by_part(-w[2], 1.0, w[0])
        linear[half * 4 + 3] = by_part(w[1], -w[0], 1.0)
    return features, pick_rows(linear, sub)


def point_features(block_points, sub, lane):
    upper = lane >= TILE
    both = jnp.concatenate([block_points, block_points], axis=1)
    x = [jnp.broadcast_to(both[k : k + 1], (8, 128)) for k in range(3)]
    low = pick_rows({1: x[0], 2: x[1], 3: x[2]}, sub, 1.0)
    high = pick_rows({5: x[0], 6: x[1], 7: x[2]}, sub, 1.0)
    low = jnp.where((sub < 4) & jnp.logical_not(upper), low, 0.0)
    high = jnp.where((sub >= 4) & upper, high, 0.0)
    left = pick_rows({m: x[a] for m, (a, b) in enumerate(moment_pairs)}, sub)
    right = pick_rows({m: x[b] for m, (a, b) in enumerate(moment_pairs)}, sub)
    moments = left * right
    return [
        low,
        jnp.where(upper, 0.0, moments),
        high,
        jnp.where(upper, moments, 0.0),
    ]


def tiles_kernel(
    chunks,
    unroll,
    tile_frame,
    tile_block,
    tile_count,
    block_slot,
    poses_far,
    window_far,
    obs_far,
    frame_out,
    point_out,
    poses,
    window,
    obs,
    frame_feat,
    point_feat,
    frame_line,
    point_line,
    frame_acc,
    point_acc,
    sems,
):
    frame_blocks = poses.shape[0]
    point_blocks = window.shape[0]
    chunk_rows = obs.shape[1] // chunks
    chunk_tiles = chunk_rows // HALF

    def chunk_copy(c):
        part = pl.ds(c * chunk_rows, chunk_rows)
        return pltpu.make_async_copy(obs_far.at[:, part], obs.at[:, part], sems.at[2 + c])

    window_copy = pltpu.make_async_copy(window_far, window, sems.at[0])
    pose_copy = pltpu.make_async_copy(poses_far, poses, sems.at[1])
    window_copy.start()
    pose_copy.start()
    for c in range(chunks):
        chunk_copy(c).start()
    frame_acc[...] = jnp.zeros_like(frame_acc)
    point_acc[...] = jnp.zeros_like(point_acc)
    sub = lax.broadcasted_iota(jnp.int32, (8, 128), 0)
    lane = lax.broadcasted_iota(jnp.int32, (8, 128), 1)
    zeros = jnp.zeros((8, 128), jnp.float32)

    window_copy.wait()

    @pl.loop(0, point_blocks, step=4)
    def _(start):
        for u in range(4):
            block = start + u
            rows = point_features(window[block], sub, lane)
            high, low = split_rows(jnp.concatenate(rows, axis=0))
            point_feat[block, 0:32, :] = high
            point_feat[block, 32:64, :] = low
            ones = rows[0] + rows[2]
            high = ones.astype(jnp.bfloat16).astype(jnp.float32)
            stack = jnp.concatenate([high, ones - high, high, zeros], axis=0)
            point_line[block] = stack.astype(jnp.bfloat16)

    pose_copy.wait()

    @pl.loop(0, frame_blocks, step=2)
    def _(start):
        for u in range(2):
            block = start + u
            rows, linear = frame_features(poses[block, 0:8, :], sub, lane)
            high, low = split_rows(jnp.concatenate(rows, axis=0))
            frame_feat[block, 0:32, :] = high
            frame_feat[block, 32:64, :] = low
            high = linear.astype(jnp.bfloat16).astype(jnp.float32)
            stack = jnp.concatenate([high, high, linear - high, zeros], axis=0)
            frame_line[block] = jnp.transpose(stack)[0:96].astype(jnp.bfloat16)

    def one_tile(slot):
        live = slot < tile_count[0]
        f = jnp.where(live, tile_frame[slot], 0)
        p = jnp.where(live, block_slot[0, tile_block[slot]], 0)
        here = pl.ds(pl.multiple_of(slot * HALF, HALF), HALF)
        measured = [obs[k, here, :] for k in range(3)]
        seen = jnp.dot(frame_line[f], point_line[p], preferred_element_type=jnp.float32)
        residual = [seen[k * HALF : (k + 1) * HALF] - measured[k] for k in range(3)]
        squared = (
            residual[0] * residual[0] + residual[1] * residual[1] + residual[2] * residual[2]
        )
        weight = jnp.where(live, 1.0, 0.0) / (1.0 + squared * (1.0 / robust_scale))
        images = jnp.concatenate(
            [weight] + [weight * measured[k] for k in range(3)], axis=0
        )
        high, low = split_rows(images)
        sums = []
        for features, dims in ((frame_feat[f], (1, 0)), (point_feat[p], (1, 1))):
            dims = (((dims[0],), (dims[1],)), ((), ()))
            with_high = lax.dot_general(
                features, high, dims, preferred_element_type=jnp.float32
            )
            with_low = lax.dot_general(
                features[0:32], low, dims, preferred_element_type=jnp.float32
            )
            sums.append(with_high[0:32] + with_high[32:64] + with_low)
        return f, p, sums

    for c in range(chunks):
        chunk_copy(c).wait()
        here = jnp.clip(tile_count[0] - c * chunk_tiles, 0, chunk_tiles)

        @pl.loop(0, (here + unroll - 1) // unroll)
        def _(group):
            done = []
            for u in range(unroll):
                done.append(one_tile(c * chunk_tiles + group * unroll + u))
            for f, p, sums in done:
                point_acc[p] += sums[0]
                frame_acc[f] += sums[1]

    for block in range(frame_blocks):
        total = frame_acc[block]
        frame_out[block, 0:8, :] = total[0:8] + total[16:24]
        frame_out[block, 8:16, :] = jnp.where(
            lane < HALF, total[8:16], pltpu.roll(total[24:32], HALF, 1)
        )

    @pl.loop(0, point_blocks, step=4)
    def _(start):
        for u in range(4):
            total = point_acc[start + u]
            point_out[start + u] = jnp.where(
                lane >= TILE,
                pltpu.roll(total[8:16], TILE, 1) + total[24:32],
                total[0:8] + pltpu.roll(total[16:24], TILE, 1),
            )


def tile_sums(poses, window, packed, tile_frame, tile_block, tile_count, block_slot):
    slots = packed.shape[1] // HALF
    frame_blocks, point_blocks = poses.shape[0], window.shape[0]
    chunks = 2 if slots % 2 == 0 else 1
    unroll = max(u for u in (1, 2, 3, 4) if slots // chunks % u == 0)
    smem = pl.BlockSpec(memory_space=pltpu.SMEM)
    far = pl.BlockSpec(memory_space=pl.ANY)
    vmem = pl.BlockSpec(memory_space=pltpu.VMEM)
    return pl.pallas_call(
        functools.partial(tiles_kernel, chunks, unroll),
        in_specs=[smem] * 4 + [far] * 3,
        out_specs=[vmem] * 2,
        scratch_shapes=[
            pltpu.VMEM(poses.shape, jnp.float32),
            pltpu.VMEM(window.shape, jnp.float32),
            pltpu.VMEM(packed.shape, jnp.float32),
            pltpu.VMEM((frame_blocks, 64, 128), jnp.bfloat16),
            pltpu.VMEM((point_blocks, 64, 128), jnp.bfloat16),
            pltpu.VMEM((frame_blocks, 96, 32), jnp.bfloat16),
            pltpu.VMEM((point_blocks, 32, 128), jnp.bfloat16),
            pltpu.VMEM((frame_blocks, 32, 128), jnp.float32),
            pltpu.VMEM((point_blocks, 32, 128), jnp.float32),
            pltpu.SemaphoreType.DMA((2 + chunks,)),
        ],
        out_shape=[
            jax.ShapeDtypeStruct((frame_blocks, 16, 128), jnp.float32),
            jax.ShapeDtypeStruct((point_blocks, 8, 128), jnp.float32),
        ],
        compiler_params=pltpu.CompilerParams(vmem_limit_bytes=VMEM_LIMIT),
        name="tile_sums",
    )(tile_frame, tile_block, tile_count, block_slot, poses, window, packed)


def ring_peers(count):
    me = lax.axis_index("lm")
    return me, [lax.rem(me + d, count) for d in range(1, count)]


def greet(peers, row, rows):
    barrier = pltpu.get_barrier_semaphore()
    for peer in peers:
        pl.semaphore_signal(barrier, inc=1, device_id=(row, peer), device_id_type=MESH)
    if rows is None:
        pl.semaphore_wait(barrier, len(peers))
        return
    me = lax.axis_index("lm")

    @pl.when(row > 0)
    def _():
        pl.semaphore_signal(barrier, inc=1, device_id=(row - 1, me), device_id_type=MESH)

    @pl.when(row < rows - 1)
    def _():
        pl.semaphore_signal(barrier, inc=1, device_id=(row + 1, me), device_id_type=MESH)

    edges = jnp.minimum(row, 1) + jnp.minimum(rows - 1 - row, 1)
    pl.semaphore_wait(barrier, len(peers) + edges)


def prepare_kernel(
    count,
    camera_poses,
    odometry,
    odometry_info,
    landmarks,
    obs_far,
    state,
    own,
    window,
    packed_far,
    obs,
    packed,
    send_sem,
    recv_sem,
    load_sem,
    store_sem,
):
    row = lax.axis_index("tm")
    me, peers = ring_peers(count)
    blocks = own.shape[0]
    frame_blocks = state.shape[0]
    slots = obs.shape[3]
    loads = [
        pltpu.make_async_copy(obs_far.at[k], obs.at[k], load_sem.at[k]) for k in range(3)
    ]
    for load in loads:
        load.start()
    own[...] = jnp.zeros_like(own)
    for block in range(blocks):
        own[block, 0:3, :] = landmarks[:, block * TILE : (block + 1) * TILE]
    greet(peers, row, None)
    copies = []
    for d, peer in enumerate(peers):
        copies.append(
            pltpu.make_async_remote_copy(
                src_ref=own,
                dst_ref=window.at[pl.ds(me * blocks, blocks)],
                send_sem=send_sem.at[d],
                recv_sem=recv_sem.at[d],
                device_id=(row, peer),
                device_id_type=MESH,
            )
        )
        copies[-1].start()
    window[pl.ds(me * blocks, blocks)] = own[...]
    state[...] = jnp.zeros_like(state)
    for block in range(frame_blocks):
        here = slice(block * TILE, (block + 1) * TILE)
        state[block, 0:6, :] = camera_poses[:, here]
        state[block, 6:12, :] = odometry[:, here]
        state[block, 12:13, :] = odometry_info[:, here]

    row_id = lax.broadcasted_iota(jnp.int32, (slots, slots), 0)
    column_id = lax.broadcasted_iota(jnp.int32, (slots, slots), 1)
    identity = jnp.where(row_id == column_id, 1.0, 0.0).astype(jnp.bfloat16)
    stores = []
    for k in range(3):
        loads[k].wait()

        @pl.loop(0, HALF, step=8)
        def _(start):
            for u in range(8):
                i = start + u
                pairs = jnp.concatenate([obs[k, i], obs[k, i + HALF]], axis=0)
                turned = lax.dot_general(
                    identity,
                    pairs,
                    (((1,), (1,)), ((), ())),
                    preferred_element_type=jnp.float32,
                )
                packed[k, pl.ds(i, slots, stride=HALF), :] = turned

        stores.append(
            pltpu.make_async_copy(packed.at[k], packed_far.at[k], store_sem.at[k])
        )
        stores[-1].start()
    for copy in copies + stores:
        copy.wait()


def prepare(camera_poses, odometry, odometry_info, landmarks, observations, count):
    slots = observations.shape[0]
    frame_blocks = camera_poses.shape[1] // TILE
    blocks = landmarks.shape[1] // TILE
    by_tile = jnp.transpose(observations, (1, 2, 3, 0))
    vmem = pl.BlockSpec(memory_space=pltpu.VMEM)
    far = pl.BlockSpec(memory_space=pl.ANY)
    packed_shape = (3, slots * HALF, 128)
    return pl.pallas_call(
        functools.partial(prepare_kernel, count),
        out_shape=[
            jax.ShapeDtypeStruct((frame_blocks, 16, TILE), jnp.float32),
            jax.ShapeDtypeStruct((blocks, 8, TILE), jnp.float32),
            jax.ShapeDtypeStruct((blocks * count, 8, TILE), jnp.float32),
            jax.ShapeDtypeStruct(packed_shape, jnp.float32),
        ],
        in_specs=[vmem] * 4 + [far],
        out_specs=[vmem] * 3 + [far],
        scratch_shapes=[
            pltpu.VMEM(by_tile.shape, jnp.bfloat16),
            pltpu.VMEM(packed_shape, jnp.float32),
            pltpu.SemaphoreType.DMA((count - 1,)),
            pltpu.SemaphoreType.DMA((count - 1,)),
            pltpu.SemaphoreType.DMA((3,)),
            pltpu.SemaphoreType.DMA((3,)),
        ],
        compiler_params=pltpu.CompilerParams(
            collective_id=0, has_side_effects=True, vmem_limit_bytes=VMEM_LIMIT
        ),
        name="prepare",
    )(camera_poses, odometry, odometry_info[None, :], landmarks, by_tile)


def pose_update(total, state, before, after, final):
    def both(row_low, row_high, start):
        return jnp.concatenate(
            [total[:, row_low, start : start + HALF], total[:, row_high, start : start + HALF]],
            axis=1,
        )

    counted = both(0, 4, 0)
    centroid = [both(1 + k, 5 + k, 0) for k in range(3)]
    moments = [total[:, 8 + m, 0:TILE] for m in range(6)]
    seen = [both(0, 4, HALF * (1 + k)) for k in range(3)]

    def lever(a, k):
        return both(1 + a, 5 + a, HALF * (1 + k))

    current = [state[:, k, :] for k in range(6)]
    w, t = current[0:3], current[3:6]
    turned = cross_product(w, centroid)
    grad_off = [centroid[k] + turned[k] + t[k] * counted - seen[k] for k in range(3)]
    matrix_rows = [
        [moments[0], moments[3], moments[4]],
        [moments[3], moments[1], moments[5]],
        [moments[4], moments[5], moments[2]],
    ]
    trace = moments[0] + moments[1] + moments[2]
    pushed = cross_product(centroid, t)
    grad_rot = []
    for k in range(3):
        a, b = (k + 1) % 3, (k + 2) % 3
        product = (
            matrix_rows[k][0] * w[0] + matrix_rows[k][1] * w[1] + matrix_rows[k][2] * w[2]
        )
        grad_rot.append(trace * w[k] - product + pushed[k] - (lever(a, b) - lever(b, a)))

    weight_before = before[:, 12, :]
    weight_after = jnp.where(final, 0.0, state[:, 12, :])
    link_grad = []
    for k in range(6):
        ahead = after[:, k, :] - current[k] - state[:, 6 + k, :]
        behind = current[k] - before[:, k, :] - before[:, 6 + k, :]
        link_grad.append(weight_before * behind - weight_after * ahead)
    diagonal_add = weight_after + weight_before + damping

    zero_entry = jnp.zeros_like(counted)
    rotation_block = [
        [moments[1] + moments[2] + diagonal_add, -moments[3], -moments[4]],
        [-moments[3], moments[0] + moments[2] + diagonal_add, -moments[5]],
        [-moments[4], -moments[5], moments[0] + moments[1] + diagonal_add],
    ]
    cross_block = [
        [zero_entry, -centroid[2], centroid[1]],
        [centroid[2], zero_entry, -centroid[0]],
        [-centroid[1], centroid[0], zero_entry],
    ]
    matrix = [rotation_block[i] + cross_block[i] for i in range(3)]
    for i in range(3):
        offset_row = [counted + diagonal_add if i == k else zero_entry for k in range(3)]
        matrix.append([cross_block[k][i] for k in range(3)] + offset_row)
    sums = grad_rot + grad_off
    step = block_solve(matrix, [sums[k] + link_grad[k] for k in range(6)])
    return [current[k] - step[k] for k in range(6)]


def point_update(total, own):
    x = [own[:, k, :] for k in range(3)]
    spread = total[:, 3, 0:TILE]
    outer = [total[:, 4 + m, 0:TILE] for m in range(4)]
    outer += [total[:, m, TILE:] for m in range(2)]
    rows = [
        [outer[0], outer[3], outer[4]],
        [outer[3], outer[1], outer[5]],
        [outer[4], outer[5], outer[2]],
    ]
    gradient = [
        total[:, k, 0:TILE]
        + spread * x[k]
        - (rows[k][0] * x[0] + rows[k][1] * x[1] + rows[k][2] * x[2])
        for k in range(3)
    ]
    diagonal = spread + damping
    matrix = [
        [diagonal - outer[0], -outer[3], -outer[4]],
        [-outer[3], diagonal - outer[1], -outer[5]],
        [-outer[4], -outer[5], diagonal - outer[2]],
    ]
    step = block_solve(matrix, gradient)
    return [x[k] - step[k] for k in range(3)]


def exchange_kernel(
    count,
    rows,
    last,
    frame_far,
    point_far,
    state_far,
    own_far,
    pose_out,
    own_out,
    window_out,
    frame_in,
    point_in,
    edge_in,
    extended,
    own,
    fresh,
    gathered,
    fresh_points,
    send_sem,
    recv_sem,
    edge_send,
    edge_recv,
    load_sem,
    store_sem,
):
    row = lax.axis_index("tm")
    me, peers = ring_peers(count)
    frame_blocks = state_far.shape[0]
    share = frame_blocks // count
    own_blocks = own_far.shape[0]
    here = pl.ds(me * share, share)
    here_points = pl.ds(me * own_blocks, own_blocks)
    greet(peers, row, rows)

    def send(group, d, peer, source, target):
        copy = pltpu.make_async_remote_copy(
            src_ref=source,
            dst_ref=target,
            send_sem=send_sem.at[group, d],
            recv_sem=recv_sem.at[group, d],
            device_id=(row, peer),
            device_id_type=MESH,
        )
        copy.start()
        return copy

    def edge(side, target_row):
        block = frame_blocks - 1 if side == 0 else 0
        return pltpu.make_async_remote_copy(
            src_ref=state_far.at[block],
            dst_ref=edge_in.at[side],
            send_sem=edge_send.at[side],
            recv_sem=edge_recv.at[side],
            device_id=(target_row, me),
            device_id_type=MESH,
        )

    frame_copies = [
        send(0, d, peer, frame_far.at[pl.ds(peer * share, share)], frame_in.at[d])
        for d, peer in enumerate(peers)
    ]

    @pl.when(row < rows - 1)
    def _():
        edge(0, row + 1).start()

    @pl.when(row > 0)
    def _():
        edge(1, row - 1).start()

    point_copies = [
        send(1, d, peer, point_far.at[pl.ds(peer * own_blocks, own_blocks)], point_in.at[d])
        for d, peer in enumerate(peers)
    ]
    loads = [
        pltpu.make_async_copy(source, target, load_sem.at[n])
        for n, (source, target) in enumerate(
            (
                (state_far, extended.at[pl.ds(1, frame_blocks)]),
                (frame_far.at[here], frame_in.at[count - 1]),
                (point_far.at[here_points], point_in.at[count - 1]),
                (own_far, own),
            )
        )
    ]
    for load in loads:
        load.start()
    extended[0] = jnp.zeros_like(extended[0])
    extended[frame_blocks + 1] = jnp.zeros_like(extended[0])
    for load in loads:
        load.wait()

    @pl.when(row > 0)
    def _():
        edge(0, row - 1).wait_recv()
        extended[0] = edge_in[0]

    @pl.when(row < rows - 1)
    def _():
        edge(1, row + 1).wait_recv()
        extended[frame_blocks + 1] = edge_in[1]

    first = me * share
    mine = extended[pl.ds(first + 1, share)]
    ahead = extended[pl.ds(first + 2, share)]
    behind = extended[pl.ds(first, share)]
    after = jnp.concatenate([mine[:, :, 1:], ahead[:, :, :1]], axis=2)
    before = jnp.concatenate([behind[:, :, TILE - 1 :], mine[:, :, : TILE - 1]], axis=2)
    block_index = lax.broadcasted_iota(jnp.int32, (share, TILE), 0) + first
    lane = lax.broadcasted_iota(jnp.int32, (share, TILE), 1)
    final = (block_index * TILE + lane) == jnp.where(
        row == rows - 1, frame_blocks * TILE - 1, -1
    )

    total = frame_in[count - 1]
    for d, copy in enumerate(frame_copies):
        copy.wait_recv()
        total = total + frame_in[d]
    poses = pose_update(total, mine, before, after, final)
    stores = []
    if last:
        gathered[here] = mine[:, 0:8, :]
        for k in range(6):
            gathered[here, k, :] = poses[k]
        pose_copies = [
            send(2, d, peer, gathered.at[here], gathered.at[here])
            for d, peer in enumerate(peers)
        ]
    else:
        fresh[...] = mine
        for k in range(6):
            fresh[:, k, :] = poses[k]
        pose_copies = [
            send(2, d, peer, fresh, pose_out.at[here]) for d, peer in enumerate(peers)
        ]
        stores.append(pltpu.make_async_copy(fresh, pose_out.at[here], store_sem.at[0]))
        stores[-1].start()

    total = point_in[count - 1]
    for d, copy in enumerate(point_copies):
        copy.wait_recv()
        total = total + point_in[d]
    points = point_update(total, own[...])
    window_copies = []
    fresh_points[...] = own[...]
    for k in range(3):
        fresh_points[:, k, :] = points[k]
    if last:
        for pair in range(own_blocks // 2):
            own_out[:, pair * 128 : (pair + 1) * 128] = jnp.concatenate(
                [fresh_points[2 * pair, 0:3, :], fresh_points[2 * pair + 1, 0:3, :]], axis=1
            )
        window_out[...] = jnp.zeros_like(window_out)
    else:
        window_copies = [
            send(3, d, peer, fresh_points, window_out.at[here_points])
            for d, peer in enumerate(peers)
        ]
        for n, target in enumerate((window_out.at[here_points], own_out)):
            stores.append(pltpu.make_async_copy(fresh_points, target, store_sem.at[1 + n]))
            stores[-1].start()

    for copy in frame_copies + point_copies:
        copy.wait_send()
    for copy in pose_copies + window_copies + stores:
        copy.wait()
    if last:
        for pair in range(frame_blocks // 2):
            pose_out[:, pair * 128 : (pair + 1) * 128] = jnp.concatenate(
                [gathered[2 * pair, 0:6, :], gathered[2 * pair + 1, 0:6, :]], axis=1
            )

    @pl.when(row < rows - 1)
    def _():
        edge(0, row + 1).wait_send()

    @pl.when(row > 0)
    def _():
        edge(1, row - 1).wait_send()


def exchange(frame_sums, point_sums, state, own, count, rows, last):
    frame_blocks = state.shape[0]
    own_blocks = own.shape[0]
    share = frame_blocks // count
    vmem = pl.BlockSpec(memory_space=pltpu.VMEM)
    far = pl.BlockSpec(memory_space=pl.ANY)
    if last:
        shapes = [(6, frame_blocks * TILE), (3, own_blocks * TILE), (8, 128)]
    else:
        shapes = [state.shape, own.shape, (own_blocks * count,) + own.shape[1:]]
    return pl.pallas_call(
        functools.partial(exchange_kernel, count, rows, last),
        out_shape=[jax.ShapeDtypeStruct(shape, jnp.float32) for shape in shapes],
        in_specs=[far] * 4,
        out_specs=[vmem if last else far] * 3,
        scratch_shapes=[
            pltpu.VMEM((count, share, 16, 128), jnp.float32),
            pltpu.VMEM((count, own_blocks, 8, 128), jnp.float32),
            pltpu.VMEM((2, 16, TILE), jnp.float32),
            pltpu.VMEM((frame_blocks + 2, 16, TILE), jnp.float32),
            pltpu.VMEM(own.shape, jnp.float32),
            pltpu.VMEM((share, 16, TILE), jnp.float32),
            pltpu.VMEM((frame_blocks, 8, TILE), jnp.float32),
            pltpu.VMEM(own.shape, jnp.float32),
            pltpu.SemaphoreType.DMA((4, count - 1)),
            pltpu.SemaphoreType.DMA((4, count - 1)),
            pltpu.SemaphoreType.DMA((2,)),
            pltpu.SemaphoreType.DMA((2,)),
            pltpu.SemaphoreType.DMA((4,)),
            pltpu.SemaphoreType.DMA((3,)),
        ],
        compiler_params=pltpu.CompilerParams(
            collective_id=2 if last else 1,
            has_side_effects=True,
            vmem_limit_bytes=VMEM_LIMIT,
        ),
        name="exchange_last" if last else "exchange_first",
    )(frame_sums, point_sums, state, own)


def on_device(
    camera_poses,
    landmarks,
    odometry,
    odometry_info,
    observations,
    tile_frame,
    tile_block,
    tile_count,
    block_slot,
):
    rows, count = lax.axis_size("tm"), lax.axis_size("lm")
    state, own, window, packed = prepare(
        camera_poses, odometry, odometry_info, landmarks, observations, count
    )
    for iteration in range(ITERS):
        frame_sums, point_sums = tile_sums(
            state, window, packed, tile_frame, tile_block, tile_count, block_slot
        )
        last = iteration == ITERS - 1
        state, own, window = exchange(frame_sums, point_sums, state, own, count, rows, last)
    return (state, own)


def solution(mesh):
    return jax.shard_map(
        on_device,
        mesh=mesh,
        in_specs=(
            P(None, "tm"),
            P(None, ("tm", "lm")),
            P(None, "tm"),
            P("tm"),
            P(("tm", "lm"), None, None, None),
            P(("tm", "lm")),
            P(("tm", "lm")),
            P(("tm", "lm")),
            P("tm", None),
        ),
        out_specs=(P(None, "tm"), P(None, ("tm", "lm"))),
        check_vma=False,
    )
```

```python
import functools

import jax
import jax.numpy as jnp
from jax import lax
from jax.experimental import pallas as pl
from jax.experimental.pallas import tpu as pltpu
from jax.sharding import PartitionSpec as P

TILE = 64
HALF = 32
ITERS = 2
VMEM_LIMIT = 60 * 1024 * 1024
MESH = pl.DeviceIdType.MESH

robust_scale = 4.0
damping = 1.0
moment_pairs = ((0, 0), (1, 1), (2, 2), (0, 1), (0, 2), (1, 2))


def cross_product(left, right):
    return [
        left[1] * right[2] - left[2] * right[1],
        left[2] * right[0] - left[0] * right[2],
        left[0] * right[1] - left[1] * right[0],
    ]


def block_solve(matrix, vector):
    dimension = len(vector)
    factor = [[None] * dimension for i in range(dimension)]
    inverse_diag = [None] * dimension
    for i in range(dimension):
        for j in range(i + 1):
            running = matrix[i][j]
            for k in range(j):
                running = running - factor[i][k] * factor[j][k]
            if i == j:
                factor[i][i] = jnp.sqrt(running)
                inverse_diag[i] = 1.0 / factor[i][i]
            else:
                factor[i][j] = running * inverse_diag[j]
    forward = [None] * dimension
    for i in range(dimension):
        running = vector[i]
        for k in range(i):
            running = running - factor[i][k] * forward[k]
        forward[i] = running * inverse_diag[i]
    solution = [None] * dimension
    for i in reversed(range(dimension)):
        running = forward[i]
        for k in range(i + 1, dimension):
            running = running - factor[k][i] * solution[k]
        solution[i] = running * inverse_diag[i]
    return solution


def split_rows(value):
    high = value.astype(jnp.bfloat16)
    low = (value - high.astype(jnp.float32)).astype(jnp.bfloat16)
    return high, low


def pick_rows(rows, sub, default=0.0):
    value = jnp.full(sub.shape, default, jnp.float32)
    for s, row in rows.items():
        value = jnp.where(sub == s, row, value)
    return value


def frame_features(block_poses, sub, lane):
    image = lane // HALF
    first = image == 0
    features = []
    for half in range(2):
        part = block_poses[:, half * HALF : (half + 1) * HALF]
        part = jnp.concatenate([part] * 4, axis=1)
        value = [jnp.broadcast_to(part[k : k + 1], (8, 128)) for k in range(6)]
        w, t = value[0:3], value[3:6]
        turned = cross_product(w, t)
        rows = {}
        for m in range(3):
            a, b = (m + 1) % 3, (m + 2) % 3
            row = jnp.where(first, t[m] - turned[m], 0.0)
            row = jnp.where(image == 1 + m, -1.0, row)
            row = jnp.where(image == 1 + b, w[a], row)
            rows[m] = jnp.where(image == 1 + a, -w[b], row)
        square = w[0] * w[0] + w[1] * w[1] + w[2] * w[2]
        rows[3] = jnp.where(first, 1.0 + square, 0.0)
        products = [jnp.where(first, w[a] * w[b], 0.0) for a, b in moment_pairs]
        for m in range(4):
            rows[4 + m] = products[m]
        features.append(pick_rows(rows, sub))
        features.append(pick_rows({0: products[4], 1: products[5]}, sub))
    return features


def point_features(block_points, sub, lane):
    upper = lane >= TILE
    both = jnp.concatenate([block_points, block_points], axis=1)
    x = [jnp.broadcast_to(both[k : k + 1], (8, 128)) for k in range(3)]
    low = pick_rows({1: x[0], 2: x[1], 3: x[2]}, sub, 1.0)
    high = pick_rows({5: x[0], 6: x[1], 7: x[2]}, sub, 1.0)
    low = jnp.where((sub < 4) & jnp.logical_not(upper), low, 0.0)
    high = jnp.where((sub >= 4) & upper, high, 0.0)
    left = pick_rows({m: x[a] for m, (a, b) in enumerate(moment_pairs)}, sub)
    right = pick_rows({m: x[b] for m, (a, b) in enumerate(moment_pairs)}, sub)
    moments = left * right
    return [
        low,
        jnp.where(upper, 0.0, moments),
        high,
        jnp.where(upper, moments, 0.0),
    ]


def tiles_kernel(
    chunks,
    unroll,
    tile_frame,
    tile_block,
    tile_count,
    block_slot,
    poses_far,
    window_far,
    obs_far,
    frame_out,
    point_out,
    poses,
    window,
    obs,
    frame_feat,
    point_feat,
    pose_wide,
    point_wide,
    frame_acc,
    point_acc,
    sems,
):
    frame_blocks = poses.shape[0]
    point_blocks = window.shape[0]
    chunk_rows = obs.shape[1] // chunks
    chunk_tiles = chunk_rows // HALF

    def chunk_copy(c):
        part = pl.ds(c * chunk_rows, chunk_rows)
        return pltpu.make_async_copy(obs_far.at[:, part], obs.at[:, part], sems.at[2 + c])

    window_copy = pltpu.make_async_copy(window_far, window, sems.at[0])
    pose_copy = pltpu.make_async_copy(poses_far, poses, sems.at[1])
    window_copy.start()
    pose_copy.start()
    for c in range(chunks):
        chunk_copy(c).start()
    frame_acc[...] = jnp.zeros_like(frame_acc)
    point_acc[...] = jnp.zeros_like(point_acc)
    sub = lax.broadcasted_iota(jnp.int32, (8, 128), 0)
    lane = lax.broadcasted_iota(jnp.int32, (8, 128), 1)
    wide_upper = lax.broadcasted_iota(jnp.int32, (HALF, 128), 1) >= TILE

    window_copy.wait()

    @pl.loop(0, point_blocks, step=4)
    def _(start):
        for u in range(4):
            block = start + u
            rows = point_features(window[block], sub, lane)
            high, low = split_rows(jnp.concatenate(rows, axis=0))
            point_feat[block, 0:32, :] = high
            point_feat[block, 32:64, :] = low
            both = window[block]
            point_wide[block] = jnp.concatenate([both, both], axis=1)

    pose_copy.wait()

    @pl.loop(0, frame_blocks, step=2)
    def _(start):
        for u in range(2):
            block = start + u
            mine = poses[block, 0:8, :]
            rows = frame_features(mine, sub, lane)
            high, low = split_rows(jnp.concatenate(rows, axis=0))
            frame_feat[block, 0:32, 0:128] = high
            frame_feat[block, 0:32, 128:256] = high
            frame_feat[block, 32:64, 0:128] = low
            frame_feat[block, 32:64, 128:256] = jnp.zeros_like(low)
            columns = jnp.transpose(mine)
            for k in range(6):
                column = columns[:, k : k + 1]
                pose_wide[block, k] = jnp.where(
                    wide_upper,
                    jnp.broadcast_to(column[HALF:], (HALF, 128)),
                    jnp.broadcast_to(column[:HALF], (HALF, 128)),
                )

    def one_tile(slot):
        live = slot < tile_count[0]
        f = jnp.where(live, tile_frame[slot], 0)
        p = jnp.where(live, block_slot[0, tile_block[slot]], 0)
        here = pl.ds(pl.multiple_of(slot * HALF, HALF), HALF)
        measured = [obs[k, here, :] for k in range(3)]
        x = [point_wide[p, k : k + 1, :] for k in range(3)]
        w = [pose_wide[f, k] for k in range(3)]
        turned = cross_product(w, x)
        residual = [
            (x[k] + turned[k]) + (pose_wide[f, 3 + k] - measured[k]) for k in range(3)
        ]
        squared = (
            residual[0] * residual[0] + residual[1] * residual[1] + residual[2] * residual[2]
        )
        weight = jnp.where(live, 1.0, 0.0) / (1.0 + squared * (1.0 / robust_scale))
        images = jnp.concatenate(
            [weight] + [weight * measured[k] for k in range(3)], axis=0
        )
        stacked = jnp.concatenate(split_rows(images), axis=0)
        by_point = lax.dot_general(
            frame_feat[f], stacked, (((1,), (0,)), ((), ())), preferred_element_type=jnp.float32
        )
        by_frame = lax.dot_general(
            point_feat[p], stacked, (((1,), (1,)), ((), ())), preferred_element_type=jnp.float32
        )
        sums = (
            by_point[0:32] + by_point[32:64],
            by_frame[0:32, 0:128] + by_frame[0:32, 128:256] + by_frame[32:64, 0:128],
        )
        return f, p, sums

    for c in range(chunks):
        chunk_copy(c).wait()
        here = jnp.clip(tile_count[0] - c * chunk_tiles, 0, chunk_tiles)

        @pl.loop(0, (here + unroll - 1) // unroll)
        def _(group):
            done = []
            for u in range(unroll):
                done.append(one_tile(c * chunk_tiles + group * unroll + u))
            for f, p, sums in done:
                point_acc[p] += sums[0]
                frame_acc[f] += sums[1]

    for block in range(frame_blocks):
        total = frame_acc[block]
        frame_out[block, 0:8, :] = total[0:8] + total[16:24]
        frame_out[block, 8:16, :] = jnp.where(
            lane < HALF, total[8:16], pltpu.roll(total[24:32], HALF, 1)
        )

    @pl.loop(0, point_blocks, step=4)
    def _(start):
        for u in range(4):
            total = point_acc[start + u]
            point_out[start + u] = jnp.where(
                lane >= TILE,
                pltpu.roll(total[8:16], TILE, 1) + total[24:32],
                total[0:8] + pltpu.roll(total[16:24], TILE, 1),
            )


def tile_sums(poses, window, packed, tile_frame, tile_block, tile_count, block_slot):
    slots = packed.shape[1] // HALF
    frame_blocks, point_blocks = poses.shape[0], window.shape[0]
    chunks = 2 if slots % 2 == 0 else 1
    unroll = max(u for u in (1, 2, 3, 4, 6, 8) if slots // chunks % u == 0)
    smem = pl.BlockSpec(memory_space=pltpu.SMEM)
    far = pl.BlockSpec(memory_space=pl.ANY)
    vmem = pl.BlockSpec(memory_space=pltpu.VMEM)
    return pl.pallas_call(
        functools.partial(tiles_kernel, chunks, unroll),
        in_specs=[smem] * 4 + [far] * 3,
        out_specs=[vmem] * 2,
        scratch_shapes=[
            pltpu.VMEM(poses.shape, jnp.float32),
            pltpu.VMEM(window.shape, jnp.float32),
            pltpu.VMEM(packed.shape, jnp.float32),
            pltpu.VMEM((frame_blocks, 64, 256), jnp.bfloat16),
            pltpu.VMEM((point_blocks, 64, 128), jnp.bfloat16),
            pltpu.VMEM((frame_blocks, 6, HALF, 128), jnp.float32),
            pltpu.VMEM((point_blocks, 8, 128), jnp.float32),
            pltpu.VMEM((frame_blocks, 32, 128), jnp.float32),
            pltpu.VMEM((point_blocks, 32, 128), jnp.float32),
            pltpu.SemaphoreType.DMA((2 + chunks,)),
        ],
        out_shape=[
            jax.ShapeDtypeStruct((frame_blocks, 16, 128), jnp.float32),
            jax.ShapeDtypeStruct((point_blocks, 8, 128), jnp.float32),
        ],
        compiler_params=pltpu.CompilerParams(vmem_limit_bytes=VMEM_LIMIT),
        name="tile_sums",
    )(tile_frame, tile_block, tile_count, block_slot, poses, window, packed)


def ring_peers(count):
    me = lax.axis_index("lm")
    return me, [lax.rem(me + d, count) for d in range(1, count)]


def greet(peers, row, rows):
    barrier = pltpu.get_barrier_semaphore()
    for peer in peers:
        pl.semaphore_signal(barrier, inc=1, device_id=(row, peer), device_id_type=MESH)
    if rows is None:
        pl.semaphore_wait(barrier, len(peers))
        return
    me = lax.axis_index("lm")

    @pl.when(row > 0)
    def _():
        pl.semaphore_signal(barrier, inc=1, device_id=(row - 1, me), device_id_type=MESH)

    @pl.when(row < rows - 1)
    def _():
        pl.semaphore_signal(barrier, inc=1, device_id=(row + 1, me), device_id_type=MESH)

    edges = jnp.minimum(row, 1) + jnp.minimum(rows - 1 - row, 1)
    pl.semaphore_wait(barrier, len(peers) + edges)


def prepare_kernel(
    count,
    camera_poses,
    odometry,
    odometry_info,
    landmarks,
    obs_far,
    state,
    own,
    window,
    packed_far,
    obs,
    packed,
    send_sem,
    recv_sem,
    load_sem,
    store_sem,
):
    row = lax.axis_index("tm")
    me, peers = ring_peers(count)
    blocks = own.shape[0]
    frame_blocks = state.shape[0]
    slots = obs.shape[3]
    loads = [
        pltpu.make_async_copy(obs_far.at[k], obs.at[k], load_sem.at[k]) for k in range(3)
    ]
    for load in loads:
        load.start()
    own[...] = jnp.zeros_like(own)
    for block in range(blocks):
        own[block, 0:3, :] = landmarks[:, block * TILE : (block + 1) * TILE]
    greet(peers, row, None)
    copies = []
    for d, peer in enumerate(peers):
        copies.append(
            pltpu.make_async_remote_copy(
                src_ref=own,
                dst_ref=window.at[pl.ds(me * blocks, blocks)],
                send_sem=send_sem.at[d],
                recv_sem=recv_sem.at[d],
                device_id=(row, peer),
                device_id_type=MESH,
            )
        )
        copies[-1].start()
    window[pl.ds(me * blocks, blocks)] = own[...]
    state[...] = jnp.zeros_like(state)
    for block in range(frame_blocks):
        here = slice(block * TILE, (block + 1) * TILE)
        state[block, 0:6, :] = camera_poses[:, here]
        state[block, 6:12, :] = odometry[:, here]
        state[block, 12:13, :] = odometry_info[:, here]

    row_id = lax.broadcasted_iota(jnp.int32, (slots, slots), 0)
    column_id = lax.broadcasted_iota(jnp.int32, (slots, slots), 1)
    identity = jnp.where(row_id == column_id, 1.0, 0.0).astype(jnp.bfloat16)
    stores = []
    for k in range(3):
        loads[k].wait()

        @pl.loop(0, HALF, step=8)
        def _(start):
            for u in range(8):
                i = start + u
                pairs = jnp.concatenate([obs[k, i], obs[k, i + HALF]], axis=0)
                turned = lax.dot_general(
                    identity,
                    pairs,
                    (((1,), (1,)), ((), ())),
                    preferred_element_type=jnp.float32,
                )
                packed[k, pl.ds(i, slots, stride=HALF), :] = turned

        stores.append(
            pltpu.make_async_copy(packed.at[k], packed_far.at[k], store_sem.at[k])
        )
        stores[-1].start()
    for copy in copies + stores:
        copy.wait()


def prepare(camera_poses, odometry, odometry_info, landmarks, observations, count):
    slots = observations.shape[0]
    frame_blocks = camera_poses.shape[1] // TILE
    blocks = landmarks.shape[1] // TILE
    by_tile = jnp.transpose(observations, (1, 2, 3, 0))
    vmem = pl.BlockSpec(memory_space=pltpu.VMEM)
    far = pl.BlockSpec(memory_space=pl.ANY)
    packed_shape = (3, slots * HALF, 128)
    return pl.pallas_call(
        functools.partial(prepare_kernel, count),
        out_shape=[
            jax.ShapeDtypeStruct((frame_blocks, 16, TILE), jnp.float32),
            jax.ShapeDtypeStruct((blocks, 8, TILE), jnp.float32),
            jax.ShapeDtypeStruct((blocks * count, 8, TILE), jnp.float32),
            jax.ShapeDtypeStruct(packed_shape, jnp.float32),
        ],
        in_specs=[vmem] * 4 + [far],
        out_specs=[vmem] * 3 + [far],
        scratch_shapes=[
            pltpu.VMEM(by_tile.shape, jnp.bfloat16),
            pltpu.VMEM(packed_shape, jnp.float32),
            pltpu.SemaphoreType.DMA((count - 1,)),
            pltpu.SemaphoreType.DMA((count - 1,)),
            pltpu.SemaphoreType.DMA((3,)),
            pltpu.SemaphoreType.DMA((3,)),
        ],
        compiler_params=pltpu.CompilerParams(
            collective_id=0, has_side_effects=True, vmem_limit_bytes=VMEM_LIMIT
        ),
        name="prepare",
    )(camera_poses, odometry, odometry_info[None, :], landmarks, by_tile)


def pose_update(total, state, before, after, final):
    def both(row_low, row_high, start):
        return jnp.concatenate(
            [total[:, row_low, start : start + HALF], total[:, row_high, start : start + HALF]],
            axis=1,
        )

    counted = both(0, 4, 0)
    centroid = [both(1 + k, 5 + k, 0) for k in range(3)]
    moments = [total[:, 8 + m, 0:TILE] for m in range(6)]
    seen = [both(0, 4, HALF * (1 + k)) for k in range(3)]

    def lever(a, k):
        return both(1 + a, 5 + a, HALF * (1 + k))

    current = [state[:, k, :] for k in range(6)]
    w, t = current[0:3], current[3:6]
    turned = cross_product(w, centroid)
    grad_off = [centroid[k] + turned[k] + t[k] * counted - seen[k] for k in range(3)]
    matrix_rows = [
        [moments[0], moments[3], moments[4]],
        [moments[3], moments[1], moments[5]],
        [moments[4], moments[5], moments[2]],
    ]
    trace = moments[0] + moments[1] + moments[2]
    pushed = cross_product(centroid, t)
    grad_rot = []
    for k in range(3):
        a, b = (k + 1) % 3, (k + 2) % 3
        product = (
            matrix_rows[k][0] * w[0] + matrix_rows[k][1] * w[1] + matrix_rows[k][2] * w[2]
        )
        grad_rot.append(trace * w[k] - product + pushed[k] - (lever(a, b) - lever(b, a)))

    weight_before = before[:, 12, :]
    weight_after = jnp.where(final, 0.0, state[:, 12, :])
    link_grad = []
    for k in range(6):
        ahead = after[:, k, :] - current[k] - state[:, 6 + k, :]
        behind = current[k] - before[:, k, :] - before[:, 6 + k, :]
        link_grad.append(weight_before * behind - weight_after * ahead)
    diagonal_add = weight_after + weight_before + damping

    zero_entry = jnp.zeros_like(counted)
    rotation_block = [
        [moments[1] + moments[2] + diagonal_add, -moments[3], -moments[4]],
        [-moments[3], moments[0] + moments[2] + diagonal_add, -moments[5]],
        [-moments[4], -moments[5], moments[0] + moments[1] + diagonal_add],
    ]
    cross_block = [
        [zero_entry, -centroid[2], centroid[1]],
        [centroid[2], zero_entry, -centroid[0]],
        [-centroid[1], centroid[0], zero_entry],
    ]
    matrix = [rotation_block[i] + cross_block[i] for i in range(3)]
    for i in range(3):
        offset_row = [counted + diagonal_add if i == k else zero_entry for k in range(3)]
        matrix.append([cross_block[k][i] for k in range(3)] + offset_row)
    sums = grad_rot + grad_off
    step = block_solve(matrix, [sums[k] + link_grad[k] for k in range(6)])
    return [current[k] - step[k] for k in range(6)]


def point_update(total, own):
    x = [own[:, k, :] for k in range(3)]
    spread = total[:, 3, 0:TILE]
    outer = [total[:, 4 + m, 0:TILE] for m in range(4)]
    outer += [total[:, m, TILE:] for m in range(2)]
    rows = [
        [outer[0], outer[3], outer[4]],
        [outer[3], outer[1], outer[5]],
        [outer[4], outer[5], outer[2]],
    ]
    gradient = [
        total[:, k, 0:TILE]
        + spread * x[k]
        - (rows[k][0] * x[0] + rows[k][1] * x[1] + rows[k][2] * x[2])
        for k in range(3)
    ]
    diagonal = spread + damping
    matrix = [
        [diagonal - outer[0], -outer[3], -outer[4]],
        [-outer[3], diagonal - outer[1], -outer[5]],
        [-outer[4], -outer[5], diagonal - outer[2]],
    ]
    step = block_solve(matrix, gradient)
    return [x[k] - step[k] for k in range(3)]


def exchange_kernel(
    count,
    rows,
    last,
    frame_far,
    point_far,
    state_far,
    own_far,
    pose_out,
    own_out,
    window_out,
    frame_in,
    point_in,
    edge_in,
    extended,
    own,
    fresh,
    gathered,
    fresh_points,
    send_sem,
    recv_sem,
    edge_send,
    edge_recv,
    load_sem,
    store_sem,
):
    row = lax.axis_index("tm")
    me, peers = ring_peers(count)
    frame_blocks = state_far.shape[0]
    share = frame_blocks // count
    own_blocks = own_far.shape[0]
    here = pl.ds(me * share, share)
    here_points = pl.ds(me * own_blocks, own_blocks)
    greet(peers, row, rows)

    def send(group, d, peer, source, target):
        copy = pltpu.make_async_remote_copy(
            src_ref=source,
            dst_ref=target,
            send_sem=send_sem.at[group, d],
            recv_sem=recv_sem.at[group, d],
            device_id=(row, peer),
            device_id_type=MESH,
        )
        copy.start()
        return copy

    def edge(side, target_row):
        block = frame_blocks - 1 if side == 0 else 0
        return pltpu.make_async_remote_copy(
            src_ref=state_far.at[block],
            dst_ref=edge_in.at[side],
            send_sem=edge_send.at[side],
            recv_sem=edge_recv.at[side],
            device_id=(target_row, me),
            device_id_type=MESH,
        )

    frame_copies = [
        send(0, d, peer, frame_far.at[pl.ds(peer * share, share)], frame_in.at[d])
        for d, peer in enumerate(peers)
    ]

    @pl.when(row < rows - 1)
    def _():
        edge(0, row + 1).start()

    @pl.when(row > 0)
    def _():
        edge(1, row - 1).start()

    point_copies = [
        send(1, d, peer, point_far.at[pl.ds(peer * own_blocks, own_blocks)], point_in.at[d])
        for d, peer in enumerate(peers)
    ]
    loads = [
        pltpu.make_async_copy(source, target, load_sem.at[n])
        for n, (source, target) in enumerate(
            (
                (state_far, extended.at[pl.ds(1, frame_blocks)]),
                (frame_far.at[here], frame_in.at[count - 1]),
                (point_far.at[here_points], point_in.at[count - 1]),
                (own_far, own),
            )
        )
    ]
    for load in loads:
        load.start()
    extended[0] = jnp.zeros_like(extended[0])
    extended[frame_blocks + 1] = jnp.zeros_like(extended[0])
    for load in loads:
        load.wait()

    @pl.when(row > 0)
    def _():
        edge(0, row - 1).wait_recv()
        extended[0] = edge_in[0]

    @pl.when(row < rows - 1)
    def _():
        edge(1, row + 1).wait_recv()
        extended[frame_blocks + 1] = edge_in[1]

    first = me * share
    mine = extended[pl.ds(first + 1, share)]
    ahead = extended[pl.ds(first + 2, share)]
    behind = extended[pl.ds(first, share)]
    after = jnp.concatenate([mine[:, :, 1:], ahead[:, :, :1]], axis=2)
    before = jnp.concatenate([behind[:, :, TILE - 1 :], mine[:, :, : TILE - 1]], axis=2)
    block_index = lax.broadcasted_iota(jnp.int32, (share, TILE), 0) + first
    lane = lax.broadcasted_iota(jnp.int32, (share, TILE), 1)
    final = (block_index * TILE + lane) == jnp.where(
        row == rows - 1, frame_blocks * TILE - 1, -1
    )

    total = frame_in[count - 1]
    for d, copy in enumerate(frame_copies):
        copy.wait_recv()
        total = total + frame_in[d]
    poses = pose_update(total, mine, before, after, final)
    stores = []
    if last:
        gathered[here] = mine[:, 0:8, :]
        for k in range(6):
            gathered[here, k, :] = poses[k]
        pose_copies = [
            send(2, d, peer, gathered.at[here], gathered.at[here])
            for d, peer in enumerate(peers)
        ]
    else:
        fresh[...] = mine
        for k in range(6):
            fresh[:, k, :] = poses[k]
        pose_copies = [
            send(2, d, peer, fresh, pose_out.at[here]) for d, peer in enumerate(peers)
        ]
        stores.append(pltpu.make_async_copy(fresh, pose_out.at[here], store_sem.at[0]))
        stores[-1].start()

    total = point_in[count - 1]
    for d, copy in enumerate(point_copies):
        copy.wait_recv()
        total = total + point_in[d]
    points = point_update(total, own[...])
    window_copies = []
    fresh_points[...] = own[...]
    for k in range(3):
        fresh_points[:, k, :] = points[k]
    if last:
        for pair in range(own_blocks // 2):
            own_out[:, pair * 128 : (pair + 1) * 128] = jnp.concatenate(
                [fresh_points[2 * pair, 0:3, :], fresh_points[2 * pair + 1, 0:3, :]], axis=1
            )
        window_out[...] = jnp.zeros_like(window_out)
    else:
        window_copies = [
            send(3, d, peer, fresh_points, window_out.at[here_points])
            for d, peer in enumerate(peers)
        ]
        for n, target in enumerate((window_out.at[here_points], own_out)):
            stores.append(pltpu.make_async_copy(fresh_points, target, store_sem.at[1 + n]))
            stores[-1].start()

    for copy in frame_copies + point_copies:
        copy.wait_send()
    for copy in pose_copies + window_copies + stores:
        copy.wait()
    if last:
        for pair in range(frame_blocks // 2):
            pose_out[:, pair * 128 : (pair + 1) * 128] = jnp.concatenate(
                [gathered[2 * pair, 0:6, :], gathered[2 * pair + 1, 0:6, :]], axis=1
            )

    @pl.when(row < rows - 1)
    def _():
        edge(0, row + 1).wait_send()

    @pl.when(row > 0)
    def _():
        edge(1, row - 1).wait_send()


def exchange(frame_sums, point_sums, state, own, count, rows, last):
    frame_blocks = state.shape[0]
    own_blocks = own.shape[0]
    share = frame_blocks // count
    vmem = pl.BlockSpec(memory_space=pltpu.VMEM)
    far = pl.BlockSpec(memory_space=pl.ANY)
    if last:
        shapes = [(6, frame_blocks * TILE), (3, own_blocks * TILE), (8, 128)]
    else:
        shapes = [state.shape, own.shape, (own_blocks * count,) + own.shape[1:]]
    return pl.pallas_call(
        functools.partial(exchange_kernel, count, rows, last),
        out_shape=[jax.ShapeDtypeStruct(shape, jnp.float32) for shape in shapes],
        in_specs=[far] * 4,
        out_specs=[vmem if last else far] * 3,
        scratch_shapes=[
            pltpu.VMEM((count, share, 16, 128), jnp.float32),
            pltpu.VMEM((count, own_blocks, 8, 128), jnp.float32),
            pltpu.VMEM((2, 16, TILE), jnp.float32),
            pltpu.VMEM((frame_blocks + 2, 16, TILE), jnp.float32),
            pltpu.VMEM(own.shape, jnp.float32),
            pltpu.VMEM((share, 16, TILE), jnp.float32),
            pltpu.VMEM((frame_blocks, 8, TILE), jnp.float32),
            pltpu.VMEM(own.shape, jnp.float32),
            pltpu.SemaphoreType.DMA((4, count - 1)),
            pltpu.SemaphoreType.DMA((4, count - 1)),
            pltpu.SemaphoreType.DMA((2,)),
            pltpu.SemaphoreType.DMA((2,)),
            pltpu.SemaphoreType.DMA((4,)),
            pltpu.SemaphoreType.DMA((3,)),
        ],
        compiler_params=pltpu.CompilerParams(
            collective_id=2 if last else 1,
            has_side_effects=True,
            vmem_limit_bytes=VMEM_LIMIT,
        ),
        name="exchange_last" if last else "exchange_first",
    )(frame_sums, point_sums, state, own)


def emit_kernel(poses, points, poses_out, points_out, sems):
    copies = [
        pltpu.make_async_copy(poses, poses_out, sems.at[0]),
        pltpu.make_async_copy(points, points_out, sems.at[1]),
    ]
    for copy in copies:
        copy.start()
    for copy in copies:
        copy.wait()


def emit(poses, points):
    far = pl.BlockSpec(memory_space=pl.ANY)
    return pl.pallas_call(
        emit_kernel,
        in_specs=[far] * 2,
        out_specs=[far] * 2,
        out_shape=[jax.ShapeDtypeStruct(a.shape, a.dtype) for a in (poses, points)],
        scratch_shapes=[pltpu.SemaphoreType.DMA((2,))],
        compiler_params=pltpu.CompilerParams(vmem_limit_bytes=VMEM_LIMIT),
        name="emit",
    )(poses, points)


def on_device(
    camera_poses,
    landmarks,
    odometry,
    odometry_info,
    observations,
    tile_frame,
    tile_block,
    tile_count,
    block_slot,
):
    rows, count = lax.axis_size("tm"), lax.axis_size("lm")
    state, own, window, packed = prepare(
        camera_poses, odometry, odometry_info, landmarks, observations, count
    )
    for iteration in range(ITERS):
        frame_sums, point_sums = tile_sums(
            state, window, packed, tile_frame, tile_block, tile_count, block_slot
        )
        last = iteration == ITERS - 1
        state, own, window = exchange(frame_sums, point_sums, state, own, count, rows, last)
    return tuple(emit(state, own))


def solution(mesh):
    return jax.shard_map(
        on_device,
        mesh=mesh,
        in_specs=(
            P(None, "tm"),
            P(None, ("tm", "lm")),
            P(None, "tm"),
            P("tm"),
            P(("tm", "lm"), None, None, None),
            P(("tm", "lm")),
            P(("tm", "lm")),
            P(("tm", "lm")),
            P("tm", None),
        ),
        out_specs=(P(None, "tm"), P(None, ("tm", "lm"))),
        check_vma=False,
    )
```

```python
import functools

import jax
import jax.numpy as jnp
from jax import lax
from jax.experimental import pallas as pl
from jax.experimental.pallas import tpu as pltpu
from jax.sharding import PartitionSpec as P

TILE = 64
HALF = 32
ITERS = 2
VMEM_LIMIT = 60 * 1024 * 1024
MESH = pl.DeviceIdType.MESH

robust_scale = 4.0
damping = 1.0
moment_pairs = ((0, 0), (1, 1), (2, 2), (0, 1), (0, 2), (1, 2))


def cross_product(left, right):
    return [
        left[1] * right[2] - left[2] * right[1],
        left[2] * right[0] - left[0] * right[2],
        left[0] * right[1] - left[1] * right[0],
    ]


def block_solve(matrix, vector):
    dimension = len(vector)
    factor = [[None] * dimension for i in range(dimension)]
    inverse_diag = [None] * dimension
    for i in range(dimension):
        for j in range(i + 1):
            running = matrix[i][j]
            for k in range(j):
                running = running - factor[i][k] * factor[j][k]
            if i == j:
                factor[i][i] = jnp.sqrt(running)
                inverse_diag[i] = 1.0 / factor[i][i]
            else:
                factor[i][j] = running * inverse_diag[j]
    forward = [None] * dimension
    for i in range(dimension):
        running = vector[i]
        for k in range(i):
            running = running - factor[i][k] * forward[k]
        forward[i] = running * inverse_diag[i]
    solution = [None] * dimension
    for i in reversed(range(dimension)):
        running = forward[i]
        for k in range(i + 1, dimension):
            running = running - factor[k][i] * solution[k]
        solution[i] = running * inverse_diag[i]
    return solution


def split_rows(value):
    high = value.astype(jnp.bfloat16)
    low = (value - high.astype(jnp.float32)).astype(jnp.bfloat16)
    return high, low


def pick_rows(rows, sub, default=0.0):
    value = jnp.full(sub.shape, default, jnp.float32)
    for s, row in rows.items():
        value = jnp.where(sub == s, row, value)
    return value


def frame_features(block_poses, sub, lane):
    image = lane // HALF
    first = image == 0
    features = []
    for half in range(2):
        part = block_poses[:, half * HALF : (half + 1) * HALF]
        part = jnp.concatenate([part] * 4, axis=1)
        value = [jnp.broadcast_to(part[k : k + 1], (8, 128)) for k in range(6)]
        w, t = value[0:3], value[3:6]
        turned = cross_product(w, t)
        rows = {}
        for m in range(3):
            a, b = (m + 1) % 3, (m + 2) % 3
            row = jnp.where(first, t[m] - turned[m], 0.0)
            row = jnp.where(image == 1 + m, -1.0, row)
            row = jnp.where(image == 1 + b, w[a], row)
            rows[m] = jnp.where(image == 1 + a, -w[b], row)
        square = w[0] * w[0] + w[1] * w[1] + w[2] * w[2]
        rows[3] = jnp.where(first, 1.0 + square, 0.0)
        products = [jnp.where(first, w[a] * w[b], 0.0) for a, b in moment_pairs]
        for m in range(4):
            rows[4 + m] = products[m]
        features.append(pick_rows(rows, sub))
        features.append(pick_rows({0: products[4], 1: products[5]}, sub))
    return features


def point_features(block_points, sub, lane):
    upper = lane >= TILE
    x = [jnp.broadcast_to(block_points[k], (8, 128)) for k in range(3)]
    low = pick_rows({1: x[0], 2: x[1], 3: x[2]}, sub, 1.0)
    high = pick_rows({5: x[0], 6: x[1], 7: x[2]}, sub, 1.0)
    low = jnp.where((sub < 4) & jnp.logical_not(upper), low, 0.0)
    high = jnp.where((sub >= 4) & upper, high, 0.0)
    left = pick_rows({m: x[a] for m, (a, b) in enumerate(moment_pairs)}, sub)
    right = pick_rows({m: x[b] for m, (a, b) in enumerate(moment_pairs)}, sub)
    moments = left * right
    return [
        low,
        jnp.where(upper, 0.0, moments),
        high,
        jnp.where(upper, moments, 0.0),
    ]


def tiles_kernel(
    chunks,
    unroll,
    frame_list_far,
    block_list_far,
    count_far,
    slot_far,
    poses_far,
    window_far,
    obs_far,
    frame_out,
    point_out,
    poses,
    window,
    obs,
    frame_feat,
    point_feat,
    pose_wide,
    point_wide,
    frame_acc,
    point_acc,
    tile_frame,
    tile_block,
    tile_count,
    block_slot,
    sems,
    list_sems,
):
    frame_blocks = poses.shape[0]
    point_blocks = window.shape[0]
    chunk_tiles = obs.shape[1] // chunks

    def chunk_copy(c):
        part = pl.ds(c * chunk_tiles, chunk_tiles)
        return pltpu.make_async_copy(obs_far.at[:, part], obs.at[:, part], sems.at[2 + c])

    window_copy = pltpu.make_async_copy(window_far, window, sems.at[0])
    pose_copy = pltpu.make_async_copy(poses_far, poses, sems.at[1])
    window_copy.start()
    pose_copy.start()
    lists = [
        pltpu.make_async_copy(source, target, list_sems.at[n])
        for n, (source, target) in enumerate(
            (
                (frame_list_far, tile_frame),
                (block_list_far, tile_block),
                (count_far, tile_count),
                (slot_far, block_slot),
            )
        )
    ]
    for copy in lists:
        copy.start()
    for c in range(chunks):
        chunk_copy(c).start()
    frame_acc[...] = jnp.zeros_like(frame_acc)
    point_acc[...] = jnp.zeros_like(point_acc)
    sub = lax.broadcasted_iota(jnp.int32, (8, 128), 0)
    lane = lax.broadcasted_iota(jnp.int32, (8, 128), 1)
    wide_upper = lax.broadcasted_iota(jnp.int32, (HALF, 128), 1) >= TILE

    window_copy.wait()

    @pl.loop(0, point_blocks, step=4)
    def _(start):
        for u in range(4):
            block = start + u
            line = window[pl.ds(block, 1), :]
            both = []
            for k in range(3):
                part = line[:, k * TILE : (k + 1) * TILE]
                both.append(jnp.concatenate([part, part], axis=1))
                point_wide[block, k : k + 1, :] = both[k]
            rows = point_features(both, sub, lane)
            high, low = split_rows(jnp.concatenate(rows, axis=0))
            point_feat[block, 0:32, :] = high
            point_feat[block, 32:64, :] = low

    pose_copy.wait()

    @pl.loop(0, frame_blocks, step=2)
    def _(start):
        for u in range(2):
            block = start + u
            mine = poses[block, 0:8, :]
            rows = frame_features(mine, sub, lane)
            high, low = split_rows(jnp.concatenate(rows, axis=0))
            frame_feat[block, 0:32, 0:128] = high
            frame_feat[block, 0:32, 128:256] = high
            frame_feat[block, 32:64, 0:128] = low
            frame_feat[block, 32:64, 128:256] = jnp.zeros_like(low)
            columns = jnp.transpose(mine)
            for k in range(6):
                column = columns[:, k : k + 1]
                pose_wide[block, k] = jnp.where(
                    wide_upper,
                    jnp.broadcast_to(column[HALF:], (HALF, 128)),
                    jnp.broadcast_to(column[:HALF], (HALF, 128)),
                )

    def one_tile(slot):
        live = slot < tile_count[0]
        f = jnp.where(live, tile_frame[slot], 0)
        p = jnp.where(live, block_slot[0, tile_block[slot]], 0)
        measured = [obs[k, slot] for k in range(3)]
        x = [point_wide[p, k : k + 1, :] for k in range(3)]
        w = [pose_wide[f, k] for k in range(3)]
        turned = cross_product(w, x)
        residual = [
            (x[k] + turned[k]) + (pose_wide[f, 3 + k] - measured[k]) for k in range(3)
        ]
        squared = (
            residual[0] * residual[0] + residual[1] * residual[1] + residual[2] * residual[2]
        )
        weight = jnp.where(live, 1.0, 0.0) / (1.0 + squared * (1.0 / robust_scale))
        images = jnp.concatenate(
            [weight] + [weight * measured[k] for k in range(3)], axis=0
        )
        stacked = jnp.concatenate(split_rows(images), axis=0)
        by_point = lax.dot_general(
            frame_feat[f], stacked, (((1,), (0,)), ((), ())), preferred_element_type=jnp.float32
        )
        by_frame = lax.dot_general(
            point_feat[p], stacked, (((1,), (1,)), ((), ())), preferred_element_type=jnp.float32
        )
        sums = (
            by_point[0:32] + by_point[32:64],
            by_frame[0:32, 0:128] + by_frame[0:32, 128:256] + by_frame[32:64, 0:128],
        )
        return f, p, sums

    for copy in lists:
        copy.wait()
    for c in range(chunks):
        chunk_copy(c).wait()
        here = jnp.clip(tile_count[0] - c * chunk_tiles, 0, chunk_tiles)

        @pl.loop(0, (here + unroll - 1) // unroll)
        def _(group):
            done = []
            for u in range(unroll):
                done.append(one_tile(c * chunk_tiles + group * unroll + u))
            for f, p, sums in done:
                point_acc[p] += sums[0]
                frame_acc[f] += sums[1]

    for block in range(frame_blocks):
        total = frame_acc[block]
        frame_out[block, 0:8, :] = total[0:8] + total[16:24]
        frame_out[block, 8:16, :] = jnp.where(
            lane < HALF, total[8:16], pltpu.roll(total[24:32], HALF, 1)
        )

    @pl.loop(0, point_blocks, step=4)
    def _(start):
        for u in range(4):
            total = point_acc[start + u]
            point_out[start + u] = jnp.where(
                lane >= TILE,
                pltpu.roll(total[8:16], TILE, 1) + total[24:32],
                total[0:8] + pltpu.roll(total[16:24], TILE, 1),
            )


def tile_sums(poses, window, packed, tile_frame, tile_block, tile_count, block_slot):
    slots = packed.shape[1]
    frame_blocks, point_blocks = poses.shape[0], window.shape[0]
    chunks = 2 if slots % 2 == 0 else 1
    unroll = max(u for u in (1, 2, 3, 4, 6, 8) if slots // chunks % u == 0)
    far = pl.BlockSpec(memory_space=pl.ANY)
    vmem = pl.BlockSpec(memory_space=pltpu.VMEM)
    return pl.pallas_call(
        functools.partial(tiles_kernel, chunks, unroll),
        in_specs=[far] * 7,
        out_specs=[vmem] * 2,
        scratch_shapes=[
            pltpu.VMEM(poses.shape, jnp.float32),
            pltpu.VMEM(window.shape, jnp.float32),
            pltpu.VMEM(packed.shape, jnp.float32),
            pltpu.VMEM((frame_blocks, 64, 256), jnp.bfloat16),
            pltpu.VMEM((point_blocks, 64, 128), jnp.bfloat16),
            pltpu.VMEM((frame_blocks, 6, HALF, 128), jnp.float32),
            pltpu.VMEM((point_blocks, 8, 128), jnp.float32),
            pltpu.VMEM((frame_blocks, 32, 128), jnp.float32),
            pltpu.VMEM((point_blocks, 32, 128), jnp.float32),
            pltpu.SMEM(tile_frame.shape, jnp.int32),
            pltpu.SMEM(tile_block.shape, jnp.int32),
            pltpu.SMEM(tile_count.shape, jnp.int32),
            pltpu.SMEM(block_slot.shape, jnp.int32),
            pltpu.SemaphoreType.DMA((2 + chunks,)),
            pltpu.SemaphoreType.DMA((4,)),
        ],
        out_shape=[
            jax.ShapeDtypeStruct((frame_blocks, 16, 128), jnp.float32),
            jax.ShapeDtypeStruct((point_blocks, 8, 128), jnp.float32),
        ],
        compiler_params=pltpu.CompilerParams(vmem_limit_bytes=VMEM_LIMIT),
        name="tile_sums",
    )(tile_frame, tile_block, tile_count, block_slot, poses, window, packed)


def ring_peers(count):
    me = lax.axis_index("lm")
    return me, [lax.rem(me + d, count) for d in range(1, count)]


def greet(peers, row, rows):
    barrier = pltpu.get_barrier_semaphore()
    for peer in peers:
        pl.semaphore_signal(barrier, inc=1, device_id=(row, peer), device_id_type=MESH)
    if rows is None:
        pl.semaphore_wait(barrier, len(peers))
        return
    me = lax.axis_index("lm")

    @pl.when(row > 0)
    def _():
        pl.semaphore_signal(barrier, inc=1, device_id=(row - 1, me), device_id_type=MESH)

    @pl.when(row < rows - 1)
    def _():
        pl.semaphore_signal(barrier, inc=1, device_id=(row + 1, me), device_id_type=MESH)

    edges = jnp.minimum(row, 1) + jnp.minimum(rows - 1 - row, 1)
    pl.semaphore_wait(barrier, len(peers) + edges)


def prepare_kernel(
    count,
    camera_poses,
    odometry,
    odometry_info,
    landmarks,
    obs_far,
    state,
    links,
    own,
    window,
    packed_far,
    obs,
    packed,
    send_sem,
    recv_sem,
    load_sem,
    store_sem,
):
    row = lax.axis_index("tm")
    me, peers = ring_peers(count)
    blocks = own.shape[0]
    frame_blocks = state.shape[0]
    slots = obs.shape[3]
    loads = [
        pltpu.make_async_copy(obs_far.at[k], obs.at[k], load_sem.at[k]) for k in range(3)
    ]
    for load in loads:
        load.start()
    own_rows = pl.ds(pl.multiple_of(me * blocks, blocks), blocks)
    own[...] = jnp.zeros_like(own)
    for block in range(blocks):
        for k in range(3):
            own[block : block + 1, k * TILE : (k + 1) * TILE] = landmarks[
                k : k + 1, block * TILE : (block + 1) * TILE
            ]
    greet(peers, row, None)
    copies = []
    for d, peer in enumerate(peers):
        copies.append(
            pltpu.make_async_remote_copy(
                src_ref=own,
                dst_ref=window.at[own_rows],
                send_sem=send_sem.at[d],
                recv_sem=recv_sem.at[d],
                device_id=(row, peer),
                device_id_type=MESH,
            )
        )
        copies[-1].start()
    window[own_rows] = own[...]
    state[...] = jnp.zeros_like(state)
    links[...] = jnp.zeros_like(links)
    for block in range(frame_blocks):
        here = slice(block * TILE, (block + 1) * TILE)
        state[block, 0:6, :] = camera_poses[:, here]
        links[block, 0:6, :] = odometry[:, here]
        links[block, 6:7, :] = odometry_info[:, here]

    row_id = lax.broadcasted_iota(jnp.int32, (slots, slots), 0)
    column_id = lax.broadcasted_iota(jnp.int32, (slots, slots), 1)
    identity = jnp.where(row_id == column_id, 1.0, 0.0).astype(jnp.bfloat16)
    stores = []
    for k in range(3):
        loads[k].wait()

        @pl.loop(0, HALF, step=8)
        def _(start):
            turned = []
            for u in range(8):
                pairs = jnp.concatenate(
                    [obs[k, start + u], obs[k, start + u + HALF]], axis=0
                )
                turned.append(
                    lax.dot_general(
                        identity,
                        pairs,
                        (((1,), (1,)), ((), ())),
                        preferred_element_type=jnp.float32,
                    )
                )
            here = pl.ds(pl.multiple_of(start, 8), 8)
            packed[k, :, here, :] = jnp.swapaxes(jnp.stack(turned), 0, 1)

        stores.append(
            pltpu.make_async_copy(packed.at[k], packed_far.at[k], store_sem.at[k])
        )
        stores[-1].start()
    for copy in copies + stores:
        copy.wait()


def prepare(camera_poses, odometry, odometry_info, landmarks, observations, count):
    slots = observations.shape[0]
    frame_blocks = camera_poses.shape[1] // TILE
    blocks = landmarks.shape[1] // TILE
    by_tile = jnp.transpose(observations, (1, 2, 3, 0))
    vmem = pl.BlockSpec(memory_space=pltpu.VMEM)
    far = pl.BlockSpec(memory_space=pl.ANY)
    packed_shape = (3, slots, HALF, 128)
    return pl.pallas_call(
        functools.partial(prepare_kernel, count),
        out_shape=[
            jax.ShapeDtypeStruct((frame_blocks, 8, TILE), jnp.float32),
            jax.ShapeDtypeStruct((frame_blocks, 8, TILE), jnp.float32),
            jax.ShapeDtypeStruct((blocks, 4 * TILE), jnp.float32),
            jax.ShapeDtypeStruct((blocks * count, 4 * TILE), jnp.float32),
            jax.ShapeDtypeStruct(packed_shape, jnp.float32),
        ],
        in_specs=[vmem] * 4 + [far],
        out_specs=[vmem] * 4 + [far],
        scratch_shapes=[
            pltpu.VMEM(by_tile.shape, jnp.bfloat16),
            pltpu.VMEM(packed_shape, jnp.float32),
            pltpu.SemaphoreType.DMA((count - 1,)),
            pltpu.SemaphoreType.DMA((count - 1,)),
            pltpu.SemaphoreType.DMA((3,)),
            pltpu.SemaphoreType.DMA((3,)),
        ],
        compiler_params=pltpu.CompilerParams(
            collective_id=0, has_side_effects=True, vmem_limit_bytes=VMEM_LIMIT
        ),
        name="prepare",
    )(camera_poses, odometry, odometry_info[None, :], landmarks, by_tile)


def pose_update(total, state, links, before, links_before, after, final):
    def both(row_low, row_high, start):
        return jnp.concatenate(
            [total[:, row_low, start : start + HALF], total[:, row_high, start : start + HALF]],
            axis=1,
        )

    counted = both(0, 4, 0)
    centroid = [both(1 + k, 5 + k, 0) for k in range(3)]
    moments = [total[:, 8 + m, 0:TILE] for m in range(6)]
    seen = [both(0, 4, HALF * (1 + k)) for k in range(3)]

    def lever(a, k):
        return both(1 + a, 5 + a, HALF * (1 + k))

    current = [state[:, k, :] for k in range(6)]
    w, t = current[0:3], current[3:6]
    turned = cross_product(w, centroid)
    grad_off = [centroid[k] + turned[k] + t[k] * counted - seen[k] for k in range(3)]
    matrix_rows = [
        [moments[0], moments[3], moments[4]],
        [moments[3], moments[1], moments[5]],
        [moments[4], moments[5], moments[2]],
    ]
    trace = moments[0] + moments[1] + moments[2]
    pushed = cross_product(centroid, t)
    grad_rot = []
    for k in range(3):
        a, b = (k + 1) % 3, (k + 2) % 3
        product = (
            matrix_rows[k][0] * w[0] + matrix_rows[k][1] * w[1] + matrix_rows[k][2] * w[2]
        )
        grad_rot.append(trace * w[k] - product + pushed[k] - (lever(a, b) - lever(b, a)))

    weight_before = links_before[:, 6, :]
    weight_after = jnp.where(final, 0.0, links[:, 6, :])
    link_grad = []
    for k in range(6):
        ahead = after[:, k, :] - current[k] - links[:, k, :]
        behind = current[k] - before[:, k, :] - links_before[:, k, :]
        link_grad.append(weight_before * behind - weight_after * ahead)
    diagonal_add = weight_after + weight_before + damping

    zero_entry = jnp.zeros_like(counted)
    rotation_block = [
        [moments[1] + moments[2] + diagonal_add, -moments[3], -moments[4]],
        [-moments[3], moments[0] + moments[2] + diagonal_add, -moments[5]],
        [-moments[4], -moments[5], moments[0] + moments[1] + diagonal_add],
    ]
    cross_block = [
        [zero_entry, -centroid[2], centroid[1]],
        [centroid[2], zero_entry, -centroid[0]],
        [-centroid[1], centroid[0], zero_entry],
    ]
    matrix = [rotation_block[i] + cross_block[i] for i in range(3)]
    for i in range(3):
        offset_row = [counted + diagonal_add if i == k else zero_entry for k in range(3)]
        matrix.append([cross_block[k][i] for k in range(3)] + offset_row)
    sums = grad_rot + grad_off
    step = block_solve(matrix, [sums[k] + link_grad[k] for k in range(6)])
    return current, step


def point_update(total, own):
    x = [own[:, k * TILE : (k + 1) * TILE] for k in range(3)]
    spread = total[:, 3, 0:TILE]
    outer = [total[:, 4 + m, 0:TILE] for m in range(4)]
    outer += [total[:, m, TILE:] for m in range(2)]
    rows = [
        [outer[0], outer[3], outer[4]],
        [outer[3], outer[1], outer[5]],
        [outer[4], outer[5], outer[2]],
    ]
    gradient = [
        total[:, k, 0:TILE]
        + spread * x[k]
        - (rows[k][0] * x[0] + rows[k][1] * x[1] + rows[k][2] * x[2])
        for k in range(3)
    ]
    diagonal = spread + damping
    matrix = [
        [diagonal - outer[0], -outer[3], -outer[4]],
        [-outer[3], diagonal - outer[1], -outer[5]],
        [-outer[4], -outer[5], diagonal - outer[2]],
    ]
    step = block_solve(matrix, gradient)
    return x, step


def exchange_kernel(count, rows, last, frame_far, point_far, state_far, links_far, own_far, *refs):
    outs, refs = (refs[:4], refs[4:]) if last else (refs[:3], refs[3:])
    (
        frame_in,
        point_in,
        edge_in,
        extended,
        extended_links,
        own,
        fresh,
        gathered,
        fresh_points,
        send_sem,
        recv_sem,
        edge_send,
        edge_recv,
        load_sem,
        store_sem,
    ) = refs
    row = lax.axis_index("tm")
    me, peers = ring_peers(count)
    frame_blocks = state_far.shape[0]
    share = frame_blocks // count
    own_blocks = own_far.shape[0]
    here = pl.ds(me * share, share)
    here_points = pl.ds(pl.multiple_of(me * own_blocks, own_blocks), own_blocks)
    greet(peers, row, rows)

    def send(group, d, peer, source, target):
        copy = pltpu.make_async_remote_copy(
            src_ref=source,
            dst_ref=target,
            send_sem=send_sem.at[group, d],
            recv_sem=recv_sem.at[group, d],
            device_id=(row, peer),
            device_id_type=MESH,
        )
        copy.start()
        return copy

    def edge(side, target_row):
        source = (
            state_far.at[frame_blocks - 1],
            links_far.at[frame_blocks - 1],
            state_far.at[0],
        )[side]
        return pltpu.make_async_remote_copy(
            src_ref=source,
            dst_ref=edge_in.at[side],
            send_sem=edge_send.at[side],
            recv_sem=edge_recv.at[side],
            device_id=(target_row, me),
            device_id_type=MESH,
        )

    frame_copies = [
        send(0, d, peer, frame_far.at[pl.ds(peer * share, share)], frame_in.at[d])
        for d, peer in enumerate(peers)
    ]

    @pl.when(row < rows - 1)
    def _():
        edge(0, row + 1).start()
        edge(1, row + 1).start()

    @pl.when(row > 0)
    def _():
        edge(2, row - 1).start()

    point_copies = [
        send(1, d, peer, point_far.at[pl.ds(peer * own_blocks, own_blocks)], point_in.at[d])
        for d, peer in enumerate(peers)
    ]
    loads = [
        pltpu.make_async_copy(source, target, load_sem.at[n])
        for n, (source, target) in enumerate(
            (
                (state_far, extended.at[pl.ds(1, frame_blocks)]),
                (links_far, extended_links.at[pl.ds(1, frame_blocks)]),
                (frame_far.at[here], frame_in.at[count - 1]),
                (point_far.at[pl.ds(me * own_blocks, own_blocks)], point_in.at[count - 1]),
                (own_far, own),
            )
        )
    ]
    for load in loads:
        load.start()
    extended[0] = jnp.zeros_like(extended[0])
    extended[frame_blocks + 1] = jnp.zeros_like(extended[0])
    extended_links[0] = jnp.zeros_like(extended_links[0])
    for load in loads:
        load.wait()
    if last:
        for pair in range(frame_blocks // 2):
            outs[0][:, pair * 128 : (pair + 1) * 128] = jnp.concatenate(
                [extended[2 * pair + 1, 0:6, :], extended[2 * pair + 2, 0:6, :]], axis=1
            )

    @pl.when(row > 0)
    def _():
        edge(0, row - 1).wait_recv()
        edge(1, row - 1).wait_recv()
        extended[0] = edge_in[0]
        extended_links[0] = edge_in[1]

    @pl.when(row < rows - 1)
    def _():
        edge(2, row + 1).wait_recv()
        extended[frame_blocks + 1] = edge_in[2]

    first = me * share

    def shifted(earlier, current):
        return jnp.concatenate([earlier[:, :, TILE - 1 :], current[:, :, : TILE - 1]], axis=2)

    mine = extended[pl.ds(first + 1, share)]
    mine_links = extended_links[pl.ds(first + 1, share)]
    ahead = extended[pl.ds(first + 2, share)]
    after = jnp.concatenate([mine[:, :, 1:], ahead[:, :, :1]], axis=2)
    before = shifted(extended[pl.ds(first, share)], mine)
    links_before = shifted(extended_links[pl.ds(first, share)], mine_links)
    block_index = lax.broadcasted_iota(jnp.int32, (share, TILE), 0) + first
    lane = lax.broadcasted_iota(jnp.int32, (share, TILE), 1)
    final = (block_index * TILE + lane) == jnp.where(
        row == rows - 1, frame_blocks * TILE - 1, -1
    )

    for copy in frame_copies + point_copies:
        copy.wait_recv()
    frame_total, point_total = frame_in[count - 1], point_in[count - 1]
    for d in range(count - 1):
        frame_total = frame_total + frame_in[d]
        point_total = point_total + point_in[d]
    poses, pose_step = pose_update(
        frame_total, mine, mine_links, before, links_before, after, final
    )
    points, point_step = point_update(point_total, own[...])
    window_copies, stores = [], []
    if last:
        gathered[here] = jnp.zeros_like(mine)
        for k in range(6):
            gathered[here, k, :] = pose_step[k]
        pose_copies = [
            send(2, d, peer, gathered.at[here], gathered.at[here])
            for d, peer in enumerate(peers)
        ]
        for k in range(3):
            for out, value in ((outs[2], points[k]), (outs[3], point_step[k])):
                for pair in range(own_blocks // 2):
                    out[k : k + 1, pair * 128 : (pair + 1) * 128] = jnp.concatenate(
                        [value[2 * pair : 2 * pair + 1], value[2 * pair + 1 : 2 * pair + 2]],
                        axis=1,
                    )
    else:
        pose_out, own_out, window_out = outs
        fresh[...] = mine
        for k in range(6):
            fresh[:, k, :] = poses[k] - pose_step[k]
        pose_copies = [
            send(2, d, peer, fresh, pose_out.at[here]) for d, peer in enumerate(peers)
        ]
        fresh_points[...] = own[...]
        for k in range(3):
            fresh_points[:, k * TILE : (k + 1) * TILE] = points[k] - point_step[k]
        window_copies = [
            send(3, d, peer, fresh_points, window_out.at[here_points])
            for d, peer in enumerate(peers)
        ]
        for n, (source, target) in enumerate(
            (
                (fresh, pose_out.at[here]),
                (fresh_points, window_out.at[here_points]),
                (fresh_points, own_out),
            )
        ):
            stores.append(pltpu.make_async_copy(source, target, store_sem.at[n]))
            stores[-1].start()

    for copy in frame_copies + point_copies:
        copy.wait_send()
    for copy in pose_copies + window_copies + stores:
        copy.wait()
    if last:
        for pair in range(frame_blocks // 2):
            outs[1][:, pair * 128 : (pair + 1) * 128] = jnp.concatenate(
                [gathered[2 * pair, 0:6, :], gathered[2 * pair + 1, 0:6, :]], axis=1
            )

    @pl.when(row < rows - 1)
    def _():
        edge(0, row + 1).wait_send()
        edge(1, row + 1).wait_send()

    @pl.when(row > 0)
    def _():
        edge(2, row - 1).wait_send()


def exchange(frame_sums, point_sums, state, links, own, count, rows, last):
    frame_blocks = state.shape[0]
    own_blocks = own.shape[0]
    share = frame_blocks // count
    vmem = pl.BlockSpec(memory_space=pltpu.VMEM)
    far = pl.BlockSpec(memory_space=pl.ANY)
    if last:
        shapes = [(6, frame_blocks * TILE)] * 2 + [(3, own_blocks * TILE)] * 2
    else:
        shapes = [state.shape, own.shape, (own_blocks * count,) + own.shape[1:]]
    return pl.pallas_call(
        functools.partial(exchange_kernel, count, rows, last),
        out_shape=[jax.ShapeDtypeStruct(shape, jnp.float32) for shape in shapes],
        in_specs=[far] * 5,
        out_specs=[vmem if last else far] * len(shapes),
        scratch_shapes=[
            pltpu.VMEM((count, share, 16, 128), jnp.float32),
            pltpu.VMEM((count, own_blocks, 8, 128), jnp.float32),
            pltpu.VMEM((3, 8, TILE), jnp.float32),
            pltpu.VMEM((frame_blocks + 2, 8, TILE), jnp.float32),
            pltpu.VMEM((frame_blocks + 2, 8, TILE), jnp.float32),
            pltpu.VMEM(own.shape, jnp.float32),
            pltpu.VMEM((share, 8, TILE), jnp.float32),
            pltpu.VMEM((frame_blocks, 8, TILE), jnp.float32),
            pltpu.VMEM(own.shape, jnp.float32),
            pltpu.SemaphoreType.DMA((4, count - 1)),
            pltpu.SemaphoreType.DMA((4, count - 1)),
            pltpu.SemaphoreType.DMA((3,)),
            pltpu.SemaphoreType.DMA((3,)),
            pltpu.SemaphoreType.DMA((5,)),
            pltpu.SemaphoreType.DMA((3,)),
        ],
        compiler_params=pltpu.CompilerParams(
            collective_id=2 if last else 1,
            has_side_effects=True,
            vmem_limit_bytes=VMEM_LIMIT,
        ),
        name="exchange_last" if last else "exchange_first",
    )(frame_sums, point_sums, state, links, own)


def on_device(
    camera_poses,
    landmarks,
    odometry,
    odometry_info,
    observations,
    tile_frame,
    tile_block,
    tile_count,
    block_slot,
):
    rows, count = lax.axis_size("tm"), lax.axis_size("lm")
    state, links, own, window, packed = prepare(
        camera_poses, odometry, odometry_info, landmarks, observations, count
    )
    for iteration in range(ITERS - 1):
        sums = tile_sums(state, window, packed, tile_frame, tile_block, tile_count, block_slot)
        state, own, window = exchange(*sums, state, links, own, count, rows, False)
    sums = tile_sums(state, window, packed, tile_frame, tile_block, tile_count, block_slot)
    poses, pose_step, points, point_step = exchange(
        *sums, state, links, own, count, rows, True
    )
    return (poses - pose_step, points - point_step)


def solution(mesh):
    return jax.shard_map(
        on_device,
        mesh=mesh,
        in_specs=(
            P(None, "tm"),
            P(None, ("tm", "lm")),
            P(None, "tm"),
            P("tm"),
            P(("tm", "lm"), None, None, None),
            P(("tm", "lm")),
            P(("tm", "lm")),
            P(("tm", "lm")),
            P("tm", None),
        ),
        out_specs=(P(None, "tm"), P(None, ("tm", "lm"))),
        check_vma=False,
    )
```

```python
import functools

import jax
import jax.numpy as jnp
from jax import lax
from jax.experimental import pallas as pl
from jax.experimental.pallas import tpu as pltpu
from jax.sharding import PartitionSpec as P

TILE = 64
HALF = 32
ITERS = 2
VMEM_LIMIT = 60 * 1024 * 1024
MESH = pl.DeviceIdType.MESH

robust_scale = 4.0
damping = 1.0
moment_pairs = ((0, 0), (1, 1), (2, 2), (0, 1), (0, 2), (1, 2))


def cross_product(left, right):
    return [
        left[1] * right[2] - left[2] * right[1],
        left[2] * right[0] - left[0] * right[2],
        left[0] * right[1] - left[1] * right[0],
    ]


def block_solve(matrix, vector):
    dimension = len(vector)
    factor = [[None] * dimension for i in range(dimension)]
    inverse_diag = [None] * dimension
    for i in range(dimension):
        for j in range(i + 1):
            running = matrix[i][j]
            for k in range(j):
                running = running - factor[i][k] * factor[j][k]
            if i == j:
                factor[i][i] = jnp.sqrt(running)
                inverse_diag[i] = 1.0 / factor[i][i]
            else:
                factor[i][j] = running * inverse_diag[j]
    forward = [None] * dimension
    for i in range(dimension):
        running = vector[i]
        for k in range(i):
            running = running - factor[i][k] * forward[k]
        forward[i] = running * inverse_diag[i]
    solution = [None] * dimension
    for i in reversed(range(dimension)):
        running = forward[i]
        for k in range(i + 1, dimension):
            running = running - factor[k][i] * solution[k]
        solution[i] = running * inverse_diag[i]
    return solution


def split_rows(value):
    high = value.astype(jnp.bfloat16)
    low = (value - high.astype(jnp.float32)).astype(jnp.bfloat16)
    return high, low


def pick_rows(rows, sub, default=0.0):
    value = jnp.full(sub.shape, default, jnp.float32)
    for s, row in rows.items():
        value = jnp.where(sub == s, row, value)
    return value


def frame_features(block_poses, sub, lane):
    image = lane // HALF
    first = image == 0
    features = []
    for half in range(2):
        part = block_poses[:, half * HALF : (half + 1) * HALF]
        part = jnp.concatenate([part] * 4, axis=1)
        value = [jnp.broadcast_to(part[k : k + 1], (8, 128)) for k in range(6)]
        w, t = value[0:3], value[3:6]
        turned = cross_product(w, t)
        rows = {}
        for m in range(3):
            a, b = (m + 1) % 3, (m + 2) % 3
            row = jnp.where(first, t[m] - turned[m], 0.0)
            row = jnp.where(image == 1 + m, -1.0, row)
            row = jnp.where(image == 1 + b, w[a], row)
            rows[m] = jnp.where(image == 1 + a, -w[b], row)
        square = w[0] * w[0] + w[1] * w[1] + w[2] * w[2]
        rows[3] = jnp.where(first, 1.0 + square, 0.0)
        products = [jnp.where(first, w[a] * w[b], 0.0) for a, b in moment_pairs]
        for m in range(4):
            rows[4 + m] = products[m]
        features.append(pick_rows(rows, sub))
        features.append(pick_rows({0: products[4], 1: products[5]}, sub))
    return features


def point_features(block_points, sub, lane):
    upper = lane >= TILE
    x = [jnp.broadcast_to(block_points[k], (8, 128)) for k in range(3)]
    low = pick_rows({1: x[0], 2: x[1], 3: x[2]}, sub, 1.0)
    high = pick_rows({5: x[0], 6: x[1], 7: x[2]}, sub, 1.0)
    low = jnp.where((sub < 4) & jnp.logical_not(upper), low, 0.0)
    high = jnp.where((sub >= 4) & upper, high, 0.0)
    left = pick_rows({m: x[a] for m, (a, b) in enumerate(moment_pairs)}, sub)
    right = pick_rows({m: x[b] for m, (a, b) in enumerate(moment_pairs)}, sub)
    moments = left * right
    return [
        low,
        jnp.where(upper, 0.0, moments),
        high,
        jnp.where(upper, moments, 0.0),
    ]


def tiles_kernel(
    chunks,
    unroll,
    frame_list_far,
    block_list_far,
    count_far,
    slot_far,
    poses_far,
    window_far,
    obs_far,
    frame_out,
    point_out,
    poses,
    window,
    obs,
    frame_feat,
    point_feat,
    pose_wide,
    point_wide,
    frame_acc,
    point_acc,
    tile_frame,
    tile_block,
    tile_count,
    block_slot,
    sems,
    list_sems,
):
    frame_blocks = poses.shape[0]
    point_blocks = window.shape[0]
    chunk_tiles = obs.shape[1] // chunks

    def chunk_copy(c):
        part = pl.ds(c * chunk_tiles, chunk_tiles)
        return pltpu.make_async_copy(obs_far.at[:, part], obs.at[:, part], sems.at[2 + c])

    window_copy = pltpu.make_async_copy(window_far, window, sems.at[0])
    pose_copy = pltpu.make_async_copy(poses_far, poses, sems.at[1])
    window_copy.start()
    pose_copy.start()
    lists = [
        pltpu.make_async_copy(source, target, list_sems.at[n])
        for n, (source, target) in enumerate(
            (
                (frame_list_far, tile_frame),
                (block_list_far, tile_block),
                (count_far, tile_count),
                (slot_far, block_slot),
            )
        )
    ]
    for copy in lists:
        copy.start()
    for c in range(chunks):
        chunk_copy(c).start()
    frame_acc[...] = jnp.zeros_like(frame_acc)
    point_acc[...] = jnp.zeros_like(point_acc)
    sub = lax.broadcasted_iota(jnp.int32, (8, 128), 0)
    lane = lax.broadcasted_iota(jnp.int32, (8, 128), 1)
    wide_upper = lax.broadcasted_iota(jnp.int32, (HALF, 128), 1) >= TILE

    window_copy.wait()

    @pl.loop(0, point_blocks, step=8)
    def _(start):
        for u in range(8):
            block = start + u
            line = window[pl.ds(block, 1), :]
            both = []
            for k in range(3):
                part = line[:, k * TILE : (k + 1) * TILE]
                both.append(jnp.concatenate([part, part], axis=1))
                point_wide[block, k : k + 1, :] = both[k]
            rows = point_features(both, sub, lane)
            high, low = split_rows(jnp.concatenate(rows, axis=0))
            point_feat[block, 0:32, :] = high
            point_feat[block, 32:64, :] = low

    pose_copy.wait()

    @pl.loop(0, frame_blocks, step=4)
    def _(start):
        for u in range(4):
            block = start + u
            mine = poses[block, 0:8, :]
            rows = frame_features(mine, sub, lane)
            high, low = split_rows(jnp.concatenate(rows, axis=0))
            frame_feat[block, 0:32, 0:128] = high
            frame_feat[block, 0:32, 128:256] = high
            frame_feat[block, 32:64, 0:128] = low
            frame_feat[block, 32:64, 128:256] = jnp.zeros_like(low)
            columns = jnp.transpose(mine)
            for k in range(6):
                column = columns[:, k : k + 1]
                pose_wide[block, k] = jnp.where(
                    wide_upper,
                    jnp.broadcast_to(column[HALF:], (HALF, 128)),
                    jnp.broadcast_to(column[:HALF], (HALF, 128)),
                )

    def one_tile(slot):
        live = slot < tile_count[0]
        f = jnp.where(live, tile_frame[slot], 0)
        p = jnp.where(live, block_slot[0, tile_block[slot]], 0)
        measured = [obs[k, slot] for k in range(3)]
        x = [point_wide[p, k : k + 1, :] for k in range(3)]
        w = [pose_wide[f, k] for k in range(3)]
        turned = cross_product(w, x)
        residual = [
            (x[k] + turned[k]) + (pose_wide[f, 3 + k] - measured[k]) for k in range(3)
        ]
        squared = (
            residual[0] * residual[0] + residual[1] * residual[1] + residual[2] * residual[2]
        )
        weight = jnp.where(live, 1.0, 0.0) / (1.0 + squared * (1.0 / robust_scale))
        images = jnp.concatenate(
            [weight] + [weight * measured[k] for k in range(3)], axis=0
        )
        stacked = jnp.concatenate(split_rows(images), axis=0)
        by_point = lax.dot_general(
            frame_feat[f], stacked, (((1,), (0,)), ((), ())), preferred_element_type=jnp.float32
        )
        by_frame = lax.dot_general(
            point_feat[p], stacked, (((1,), (1,)), ((), ())), preferred_element_type=jnp.float32
        )
        sums = (
            by_point[0:32] + by_point[32:64],
            by_frame[0:32, 0:128] + by_frame[0:32, 128:256] + by_frame[32:64, 0:128],
        )
        return f, p, sums

    for copy in lists:
        copy.wait()
    for c in range(chunks):
        chunk_copy(c).wait()
        here = jnp.clip(tile_count[0] - c * chunk_tiles, 0, chunk_tiles)

        @pl.loop(0, (here + unroll - 1) // unroll)
        def _(group):
            done = []
            for u in range(unroll):
                done.append(one_tile(c * chunk_tiles + group * unroll + u))
            for f, p, sums in done:
                point_acc[p] += sums[0]
                frame_acc[f] += sums[1]

    for block in range(frame_blocks):
        total = frame_acc[block]
        frame_out[block, 0:8, :] = total[0:8] + total[16:24]
        frame_out[block, 8:16, :] = jnp.where(
            lane < HALF, total[8:16], pltpu.roll(total[24:32], HALF, 1)
        )

    @pl.loop(0, point_blocks, step=4)
    def _(start):
        for u in range(4):
            total = point_acc[start + u]
            point_out[start + u] = jnp.where(
                lane >= TILE,
                pltpu.roll(total[8:16], TILE, 1) + total[24:32],
                total[0:8] + pltpu.roll(total[16:24], TILE, 1),
            )


def tile_sums(poses, window, packed, tile_frame, tile_block, tile_count, block_slot):
    slots = packed.shape[1]
    frame_blocks, point_blocks = poses.shape[0], window.shape[0]
    chunks = 2 if slots % 2 == 0 else 1
    unroll = max(u for u in (1, 2, 3, 4, 6, 8) if slots // chunks % u == 0)
    far = pl.BlockSpec(memory_space=pl.ANY)
    vmem = pl.BlockSpec(memory_space=pltpu.VMEM)
    return pl.pallas_call(
        functools.partial(tiles_kernel, chunks, unroll),
        in_specs=[far] * 7,
        out_specs=[vmem] * 2,
        scratch_shapes=[
            pltpu.VMEM(poses.shape, jnp.float32),
            pltpu.VMEM(window.shape, jnp.float32),
            pltpu.VMEM(packed.shape, jnp.float32),
            pltpu.VMEM((frame_blocks, 64, 256), jnp.bfloat16),
            pltpu.VMEM((point_blocks, 64, 128), jnp.bfloat16),
            pltpu.VMEM((frame_blocks, 6, HALF, 128), jnp.float32),
            pltpu.VMEM((point_blocks, 8, 128), jnp.float32),
            pltpu.VMEM((frame_blocks, 32, 128), jnp.float32),
            pltpu.VMEM((point_blocks, 32, 128), jnp.float32),
            pltpu.SMEM(tile_frame.shape, jnp.int32),
            pltpu.SMEM(tile_block.shape, jnp.int32),
            pltpu.SMEM(tile_count.shape, jnp.int32),
            pltpu.SMEM(block_slot.shape, jnp.int32),
            pltpu.SemaphoreType.DMA((2 + chunks,)),
            pltpu.SemaphoreType.DMA((4,)),
        ],
        out_shape=[
            jax.ShapeDtypeStruct((frame_blocks, 16, 128), jnp.float32),
            jax.ShapeDtypeStruct((point_blocks, 8, 128), jnp.float32),
        ],
        compiler_params=pltpu.CompilerParams(vmem_limit_bytes=VMEM_LIMIT),
        name="tile_sums",
    )(tile_frame, tile_block, tile_count, block_slot, poses, window, packed)


def ring_peers(count):
    me = lax.axis_index("lm")
    return me, [lax.rem(me + d, count) for d in range(1, count)]


def greet(peers, row, rows):
    barrier = pltpu.get_barrier_semaphore()
    for peer in peers:
        pl.semaphore_signal(barrier, inc=1, device_id=(row, peer), device_id_type=MESH)
    if rows is None:
        pl.semaphore_wait(barrier, len(peers))
        return
    me = lax.axis_index("lm")

    @pl.when(row > 0)
    def _():
        pl.semaphore_signal(barrier, inc=1, device_id=(row - 1, me), device_id_type=MESH)

    @pl.when(row < rows - 1)
    def _():
        pl.semaphore_signal(barrier, inc=1, device_id=(row + 1, me), device_id_type=MESH)

    edges = jnp.minimum(row, 1) + jnp.minimum(rows - 1 - row, 1)
    pl.semaphore_wait(barrier, len(peers) + edges)


def prepare_kernel(
    count,
    poses_far,
    odometry_far,
    info_far,
    landmarks_far,
    obs_far,
    state_out,
    links_out,
    own_out,
    window_out,
    packed_far,
    camera_poses,
    odometry,
    odometry_info,
    landmarks,
    state,
    links,
    own,
    obs,
    packed,
    send_sem,
    recv_sem,
    load_sem,
    store_sem,
):
    row = lax.axis_index("tm")
    me, peers = ring_peers(count)
    blocks = own.shape[0]
    frame_blocks = state.shape[0]
    slots = obs.shape[3]
    own_rows = pl.ds(pl.multiple_of(me * blocks, blocks), blocks)
    loads = [
        pltpu.make_async_copy(source, target, load_sem.at[n])
        for n, (source, target) in enumerate(
            (
                (obs_far.at[0], obs.at[0]),
                (landmarks_far, landmarks),
                (poses_far, camera_poses),
                (odometry_far, odometry),
                (info_far, odometry_info),
                (obs_far.at[1], obs.at[1]),
                (obs_far.at[2], obs.at[2]),
            )
        )
    ]
    for load in loads:
        load.start()
    stores = []

    def store(source, target):
        stores.append(pltpu.make_async_copy(source, target, store_sem.at[len(stores)]))
        stores[-1].start()

    own[...] = jnp.zeros_like(own)
    state[...] = jnp.zeros_like(state)
    links[...] = jnp.zeros_like(links)
    loads[1].wait()
    for block in range(blocks):
        for k in range(3):
            own[block : block + 1, k * TILE : (k + 1) * TILE] = landmarks[
                k : k + 1, block * TILE : (block + 1) * TILE
            ]
    greet(peers, row, None)
    copies = []
    for d, peer in enumerate(peers):
        copies.append(
            pltpu.make_async_remote_copy(
                src_ref=own,
                dst_ref=window_out.at[own_rows],
                send_sem=send_sem.at[d],
                recv_sem=recv_sem.at[d],
                device_id=(row, peer),
                device_id_type=MESH,
            )
        )
        copies[-1].start()
    store(own, window_out.at[own_rows])
    store(own, own_out)
    for load in loads[2:5]:
        load.wait()
    for block in range(frame_blocks):
        here = slice(block * TILE, (block + 1) * TILE)
        state[block, 0:6, :] = camera_poses[:, here]
        links[block, 0:6, :] = odometry[:, here]
        links[block, 6:7, :] = odometry_info[:, here]
    store(state, state_out)
    store(links, links_out)

    row_id = lax.broadcasted_iota(jnp.int32, (slots, slots), 0)
    column_id = lax.broadcasted_iota(jnp.int32, (slots, slots), 1)
    identity = jnp.where(row_id == column_id, 1.0, 0.0).astype(jnp.bfloat16)
    for k in range(3):
        loads[(0, 5, 6)[k]].wait()

        @pl.loop(0, HALF, step=8)
        def _(start):
            turned = []
            for u in range(8):
                pairs = jnp.concatenate(
                    [obs[k, start + u], obs[k, start + u + HALF]], axis=0
                )
                turned.append(
                    lax.dot_general(
                        identity,
                        pairs,
                        (((1,), (1,)), ((), ())),
                        preferred_element_type=jnp.float32,
                    )
                )
            here = pl.ds(pl.multiple_of(start, 8), 8)
            packed[k, :, here, :] = jnp.swapaxes(jnp.stack(turned), 0, 1)

        store(packed.at[k], packed_far.at[k])
    for copy in copies + stores:
        copy.wait()


def prepare(camera_poses, odometry, odometry_info, landmarks, observations, count):
    slots = observations.shape[0]
    frame_blocks = camera_poses.shape[1] // TILE
    blocks = landmarks.shape[1] // TILE
    by_tile = jnp.transpose(observations, (1, 2, 3, 0))
    far = pl.BlockSpec(memory_space=pl.ANY)
    info = odometry_info[None, :]
    inputs = (camera_poses, odometry, info, landmarks, by_tile)
    state_shape = (frame_blocks, 8, TILE)
    own_shape = (blocks, 4 * TILE)
    packed_shape = (3, slots, HALF, 128)
    shapes = [state_shape, state_shape, own_shape, (blocks * count, 4 * TILE), packed_shape]
    return pl.pallas_call(
        functools.partial(prepare_kernel, count),
        out_shape=[jax.ShapeDtypeStruct(shape, jnp.float32) for shape in shapes],
        in_specs=[far] * 5,
        out_specs=[far] * 5,
        scratch_shapes=[pltpu.VMEM(a.shape, jnp.float32) for a in inputs[:4]]
        + [pltpu.VMEM(shape, jnp.float32) for shape in shapes[:3]]
        + [
            pltpu.VMEM(by_tile.shape, jnp.bfloat16),
            pltpu.VMEM(packed_shape, jnp.float32),
            pltpu.SemaphoreType.DMA((count - 1,)),
            pltpu.SemaphoreType.DMA((count - 1,)),
            pltpu.SemaphoreType.DMA((7,)),
            pltpu.SemaphoreType.DMA((7,)),
        ],
        compiler_params=pltpu.CompilerParams(
            collective_id=0, has_side_effects=True, vmem_limit_bytes=VMEM_LIMIT
        ),
        name="prepare",
    )(*inputs)


def pose_update(total, state, links, before, links_before, after, final):
    def both(row_low, row_high, start):
        return jnp.concatenate(
            [total[:, row_low, start : start + HALF], total[:, row_high, start : start + HALF]],
            axis=1,
        )

    counted = both(0, 4, 0)
    centroid = [both(1 + k, 5 + k, 0) for k in range(3)]
    moments = [total[:, 8 + m, 0:TILE] for m in range(6)]
    seen = [both(0, 4, HALF * (1 + k)) for k in range(3)]

    def lever(a, k):
        return both(1 + a, 5 + a, HALF * (1 + k))

    current = [state[:, k, :] for k in range(6)]
    w, t = current[0:3], current[3:6]
    turned = cross_product(w, centroid)
    grad_off = [centroid[k] + turned[k] + t[k] * counted - seen[k] for k in range(3)]
    matrix_rows = [
        [moments[0], moments[3], moments[4]],
        [moments[3], moments[1], moments[5]],
        [moments[4], moments[5], moments[2]],
    ]
    trace = moments[0] + moments[1] + moments[2]
    pushed = cross_product(centroid, t)
    grad_rot = []
    for k in range(3):
        a, b = (k + 1) % 3, (k + 2) % 3
        product = (
            matrix_rows[k][0] * w[0] + matrix_rows[k][1] * w[1] + matrix_rows[k][2] * w[2]
        )
        grad_rot.append(trace * w[k] - product + pushed[k] - (lever(a, b) - lever(b, a)))

    weight_before = links_before[:, 6, :]
    weight_after = jnp.where(final, 0.0, links[:, 6, :])
    link_grad = []
    for k in range(6):
        ahead = after[:, k, :] - current[k] - links[:, k, :]
        behind = current[k] - before[:, k, :] - links_before[:, k, :]
        link_grad.append(weight_before * behind - weight_after * ahead)
    diagonal_add = weight_after + weight_before + damping

    zero_entry = jnp.zeros_like(counted)
    rotation_block = [
        [moments[1] + moments[2] + diagonal_add, -moments[3], -moments[4]],
        [-moments[3], moments[0] + moments[2] + diagonal_add, -moments[5]],
        [-moments[4], -moments[5], moments[0] + moments[1] + diagonal_add],
    ]
    cross_block = [
        [zero_entry, -centroid[2], centroid[1]],
        [centroid[2], zero_entry, -centroid[0]],
        [-centroid[1], centroid[0], zero_entry],
    ]
    matrix = [rotation_block[i] + cross_block[i] for i in range(3)]
    for i in range(3):
        offset_row = [counted + diagonal_add if i == k else zero_entry for k in range(3)]
        matrix.append([cross_block[k][i] for k in range(3)] + offset_row)
    sums = grad_rot + grad_off
    step = block_solve(matrix, [sums[k] + link_grad[k] for k in range(6)])
    return current, step


def point_update(total, own):
    x = [own[:, k * TILE : (k + 1) * TILE] for k in range(3)]
    spread = total[:, 3, 0:TILE]
    outer = [total[:, 4 + m, 0:TILE] for m in range(4)]
    outer += [total[:, m, TILE:] for m in range(2)]
    rows = [
        [outer[0], outer[3], outer[4]],
        [outer[3], outer[1], outer[5]],
        [outer[4], outer[5], outer[2]],
    ]
    gradient = [
        total[:, k, 0:TILE]
        + spread * x[k]
        - (rows[k][0] * x[0] + rows[k][1] * x[1] + rows[k][2] * x[2])
        for k in range(3)
    ]
    diagonal = spread + damping
    matrix = [
        [diagonal - outer[0], -outer[3], -outer[4]],
        [-outer[3], diagonal - outer[1], -outer[5]],
        [-outer[4], -outer[5], diagonal - outer[2]],
    ]
    step = block_solve(matrix, gradient)
    return x, step


def exchange_kernel(count, rows, last, frame_far, point_far, state_far, links_far, own_far, *refs):
    pose_out, own_out = refs[:2]
    window_out = None if last else refs[2]
    (
        frame_in,
        point_in,
        edge_in,
        extended,
        extended_links,
        own,
        fresh,
        fresh_points,
        send_sem,
        recv_sem,
        edge_send,
        edge_recv,
        load_sem,
        store_sem,
    ) = refs[2 if last else 3 :]
    row = lax.axis_index("tm")
    me, peers = ring_peers(count)
    frame_blocks = state_far.shape[0]
    share = frame_blocks // count
    own_blocks = own_far.shape[0]
    here = pl.ds(me * share, share)
    here_points = pl.ds(pl.multiple_of(me * own_blocks, own_blocks), own_blocks)
    greet(peers, row, rows)

    def send(group, d, peer, source, target):
        copy = pltpu.make_async_remote_copy(
            src_ref=source,
            dst_ref=target,
            send_sem=send_sem.at[group, d],
            recv_sem=recv_sem.at[group, d],
            device_id=(row, peer),
            device_id_type=MESH,
        )
        copy.start()
        return copy

    def edge(side, target_row):
        source = (
            state_far.at[frame_blocks - 1],
            links_far.at[frame_blocks - 1],
            state_far.at[0],
        )[side]
        return pltpu.make_async_remote_copy(
            src_ref=source,
            dst_ref=edge_in.at[side],
            send_sem=edge_send.at[side],
            recv_sem=edge_recv.at[side],
            device_id=(target_row, me),
            device_id_type=MESH,
        )

    frame_copies = [
        send(0, d, peer, frame_far.at[pl.ds(peer * share, share)], frame_in.at[d])
        for d, peer in enumerate(peers)
    ]

    @pl.when(row < rows - 1)
    def _():
        edge(0, row + 1).start()
        edge(1, row + 1).start()

    @pl.when(row > 0)
    def _():
        edge(2, row - 1).start()

    point_copies = [
        send(1, d, peer, point_far.at[pl.ds(peer * own_blocks, own_blocks)], point_in.at[d])
        for d, peer in enumerate(peers)
    ]
    loads = [
        pltpu.make_async_copy(source, target, load_sem.at[n])
        for n, (source, target) in enumerate(
            (
                (state_far, extended.at[pl.ds(1, frame_blocks)]),
                (links_far, extended_links.at[pl.ds(1, frame_blocks)]),
                (frame_far.at[here], frame_in.at[count - 1]),
                (point_far.at[pl.ds(me * own_blocks, own_blocks)], point_in.at[count - 1]),
                (own_far, own),
            )
        )
    ]
    for load in loads:
        load.start()
    extended[0] = jnp.zeros_like(extended[0])
    extended[frame_blocks + 1] = jnp.zeros_like(extended[0])
    extended_links[0] = jnp.zeros_like(extended_links[0])
    for load in loads:
        load.wait()
    @pl.when(row > 0)
    def _():
        edge(0, row - 1).wait_recv()
        edge(1, row - 1).wait_recv()
        extended[0] = edge_in[0]
        extended_links[0] = edge_in[1]

    @pl.when(row < rows - 1)
    def _():
        edge(2, row + 1).wait_recv()
        extended[frame_blocks + 1] = edge_in[2]

    first = me * share

    def shifted(earlier, current):
        return jnp.concatenate([earlier[:, :, TILE - 1 :], current[:, :, : TILE - 1]], axis=2)

    mine = extended[pl.ds(first + 1, share)]
    mine_links = extended_links[pl.ds(first + 1, share)]
    ahead = extended[pl.ds(first + 2, share)]
    after = jnp.concatenate([mine[:, :, 1:], ahead[:, :, :1]], axis=2)
    before = shifted(extended[pl.ds(first, share)], mine)
    links_before = shifted(extended_links[pl.ds(first, share)], mine_links)
    block_index = lax.broadcasted_iota(jnp.int32, (share, TILE), 0) + first
    lane = lax.broadcasted_iota(jnp.int32, (share, TILE), 1)
    final = (block_index * TILE + lane) == jnp.where(
        row == rows - 1, frame_blocks * TILE - 1, -1
    )

    for copy in frame_copies + point_copies:
        copy.wait_recv()
    frame_total, point_total = frame_in[count - 1], point_in[count - 1]
    for d in range(count - 1):
        frame_total = frame_total + frame_in[d]
        point_total = point_total + point_in[d]
    poses, pose_step = pose_update(
        frame_total, mine, mine_links, before, links_before, after, final
    )
    points, point_step = point_update(point_total, own[...])
    fresh[...] = mine
    for k in range(6):
        fresh[:, k, :] = poses[k] - pose_step[k]
    gathers = [send(2, d, peer, fresh, pose_out.at[here]) for d, peer in enumerate(peers)]
    fresh_points[...] = own[...]
    for k in range(3):
        fresh_points[:, k * TILE : (k + 1) * TILE] = points[k] - point_step[k]
    targets = [(fresh, pose_out.at[here]), (fresh_points, own_out)]
    if not last:
        gathers += [
            send(3, d, peer, fresh_points, window_out.at[here_points])
            for d, peer in enumerate(peers)
        ]
        targets.append((fresh_points, window_out.at[here_points]))
    stores = [
        pltpu.make_async_copy(source, target, store_sem.at[n])
        for n, (source, target) in enumerate(targets)
    ]
    for copy in stores:
        copy.start()
    for copy in frame_copies + point_copies:
        copy.wait_send()
    for copy in gathers + stores:
        copy.wait()

    @pl.when(row < rows - 1)
    def _():
        edge(0, row + 1).wait_send()
        edge(1, row + 1).wait_send()

    @pl.when(row > 0)
    def _():
        edge(2, row - 1).wait_send()


def exchange(frame_sums, point_sums, state, links, own, count, rows, last):
    frame_blocks = state.shape[0]
    own_blocks = own.shape[0]
    share = frame_blocks // count
    far = pl.BlockSpec(memory_space=pl.ANY)
    shapes = [state.shape, own.shape]
    if not last:
        shapes.append((own_blocks * count,) + own.shape[1:])
    return pl.pallas_call(
        functools.partial(exchange_kernel, count, rows, last),
        out_shape=[jax.ShapeDtypeStruct(shape, jnp.float32) for shape in shapes],
        in_specs=[far] * 5,
        out_specs=[far] * len(shapes),
        scratch_shapes=[
            pltpu.VMEM((count, share, 16, 128), jnp.float32),
            pltpu.VMEM((count, own_blocks, 8, 128), jnp.float32),
            pltpu.VMEM((3, 8, TILE), jnp.float32),
            pltpu.VMEM((frame_blocks + 2, 8, TILE), jnp.float32),
            pltpu.VMEM((frame_blocks + 2, 8, TILE), jnp.float32),
            pltpu.VMEM(own.shape, jnp.float32),
            pltpu.VMEM((share, 8, TILE), jnp.float32),
            pltpu.VMEM(own.shape, jnp.float32),
            pltpu.SemaphoreType.DMA((4, count - 1)),
            pltpu.SemaphoreType.DMA((4, count - 1)),
            pltpu.SemaphoreType.DMA((3,)),
            pltpu.SemaphoreType.DMA((3,)),
            pltpu.SemaphoreType.DMA((5,)),
            pltpu.SemaphoreType.DMA((3,)),
        ],
        compiler_params=pltpu.CompilerParams(
            collective_id=2 if last else 1,
            has_side_effects=True,
            vmem_limit_bytes=VMEM_LIMIT,
        ),
        name="exchange_last" if last else "exchange_first",
    )(frame_sums, point_sums, state, links, own)


def emit_kernel(state, own, poses, points):
    for pair in range(state.shape[0] // 2):
        here = slice(pair * 128, (pair + 1) * 128)
        poses[:, here] = jnp.concatenate(
            [state[2 * pair, 0:6, :], state[2 * pair + 1, 0:6, :]], axis=1
        )
    for pair in range(own.shape[0] // 2):
        here = slice(pair * 128, (pair + 1) * 128)
        for k in range(3):
            part = own[2 * pair : 2 * pair + 2, k * TILE : (k + 1) * TILE]
            points[k : k + 1, here] = jnp.concatenate([part[0:1], part[1:2]], axis=1)


def emit(state, own):
    vmem = pl.BlockSpec(memory_space=pltpu.VMEM)
    return pl.pallas_call(
        emit_kernel,
        in_specs=[vmem] * 2,
        out_specs=[vmem] * 2,
        out_shape=[
            jax.ShapeDtypeStruct((6, state.shape[0] * TILE), jnp.float32),
            jax.ShapeDtypeStruct((3, own.shape[0] * TILE), jnp.float32),
        ],
        compiler_params=pltpu.CompilerParams(vmem_limit_bytes=VMEM_LIMIT),
        name="emit",
    )(state, own)


def on_device(
    camera_poses,
    landmarks,
    odometry,
    odometry_info,
    observations,
    tile_frame,
    tile_block,
    tile_count,
    block_slot,
):
    rows, count = lax.axis_size("tm"), lax.axis_size("lm")
    state, links, own, window, packed = prepare(
        camera_poses, odometry, odometry_info, landmarks, observations, count
    )
    for iteration in range(ITERS - 1):
        sums = tile_sums(state, window, packed, tile_frame, tile_block, tile_count, block_slot)
        state, own, window = exchange(*sums, state, links, own, count, rows, False)
    sums = tile_sums(state, window, packed, tile_frame, tile_block, tile_count, block_slot)
    state, own = exchange(*sums, state, links, own, count, rows, True)
    return tuple(emit(state, own))


def solution(mesh):
    return jax.shard_map(
        on_device,
        mesh=mesh,
        in_specs=(
            P(None, "tm"),
            P(None, ("tm", "lm")),
            P(None, "tm"),
            P("tm"),
            P(("tm", "lm"), None, None, None),
            P(("tm", "lm")),
            P(("tm", "lm")),
            P(("tm", "lm")),
            P("tm", None),
        ),
        out_specs=(P(None, "tm"), P(None, ("tm", "lm"))),
        check_vma=False,
    )
```

```python
import functools

import jax
import jax.numpy as jnp
from jax import lax
from jax.experimental import pallas as pl
from jax.experimental.pallas import tpu as pltpu
from jax.sharding import PartitionSpec as P

TILE = 64
HALF = 32
ITERS = 2
VMEM_LIMIT = 60 * 1024 * 1024
MESH = pl.DeviceIdType.MESH

robust_scale = 4.0
damping = 1.0
moment_pairs = ((0, 0), (1, 1), (2, 2), (0, 1), (0, 2), (1, 2))


def cross_product(left, right):
    return [
        left[1] * right[2] - left[2] * right[1],
        left[2] * right[0] - left[0] * right[2],
        left[0] * right[1] - left[1] * right[0],
    ]


def block_solve(matrix, vector):
    dimension = len(vector)
    factor = [[None] * dimension for i in range(dimension)]
    inverse_diag = [None] * dimension
    for i in range(dimension):
        for j in range(i + 1):
            running = matrix[i][j]
            for k in range(j):
                running = running - factor[i][k] * factor[j][k]
            if i == j:
                factor[i][i] = jnp.sqrt(running)
                inverse_diag[i] = 1.0 / factor[i][i]
            else:
                factor[i][j] = running * inverse_diag[j]
    forward = [None] * dimension
    for i in range(dimension):
        running = vector[i]
        for k in range(i):
            running = running - factor[i][k] * forward[k]
        forward[i] = running * inverse_diag[i]
    solution = [None] * dimension
    for i in reversed(range(dimension)):
        running = forward[i]
        for k in range(i + 1, dimension):
            running = running - factor[k][i] * solution[k]
        solution[i] = running * inverse_diag[i]
    return solution


def split_rows(value):
    high = value.astype(jnp.bfloat16)
    low = (value - high.astype(jnp.float32)).astype(jnp.bfloat16)
    return high, low


def pick_rows(rows, sub, default=0.0):
    value = jnp.full(sub.shape, default, jnp.float32)
    for s, row in rows.items():
        value = jnp.where(sub == s, row, value)
    return value


def frame_features(block_poses, sub, lane):
    image = lane // HALF
    first = image == 0
    features = []
    for half in range(2):
        part = block_poses[:, half * HALF : (half + 1) * HALF]
        part = jnp.concatenate([part] * 4, axis=1)
        value = [jnp.broadcast_to(part[k : k + 1], (8, 128)) for k in range(6)]
        w, t = value[0:3], value[3:6]
        turned = cross_product(w, t)
        rows = {}
        for m in range(3):
            a, b = (m + 1) % 3, (m + 2) % 3
            row = jnp.where(first, t[m] - turned[m], 0.0)
            row = jnp.where(image == 1 + m, -1.0, row)
            row = jnp.where(image == 1 + b, w[a], row)
            rows[m] = jnp.where(image == 1 + a, -w[b], row)
        square = w[0] * w[0] + w[1] * w[1] + w[2] * w[2]
        rows[3] = jnp.where(first, 1.0 + square, 0.0)
        products = [jnp.where(first, w[a] * w[b], 0.0) for a, b in moment_pairs]
        for m in range(4):
            rows[4 + m] = products[m]
        features.append(pick_rows(rows, sub))
        features.append(pick_rows({0: products[4], 1: products[5]}, sub))
    return features


def point_features(block_points, sub, lane):
    upper = lane >= TILE
    x = [jnp.broadcast_to(block_points[k], (8, 128)) for k in range(3)]
    low = pick_rows({1: x[0], 2: x[1], 3: x[2]}, sub, 1.0)
    high = pick_rows({5: x[0], 6: x[1], 7: x[2]}, sub, 1.0)
    low = jnp.where((sub < 4) & jnp.logical_not(upper), low, 0.0)
    high = jnp.where((sub >= 4) & upper, high, 0.0)
    left = pick_rows({m: x[a] for m, (a, b) in enumerate(moment_pairs)}, sub)
    right = pick_rows({m: x[b] for m, (a, b) in enumerate(moment_pairs)}, sub)
    moments = left * right
    return [
        low,
        jnp.where(upper, 0.0, moments),
        high,
        jnp.where(upper, moments, 0.0),
    ]


def tiles_kernel(
    chunks,
    unroll,
    frame_list_far,
    block_list_far,
    count_far,
    slot_far,
    poses_far,
    window_far,
    obs_far,
    frame_out,
    point_out,
    poses,
    window,
    obs,
    frame_feat,
    point_feat,
    pose_wide,
    point_wide,
    frame_acc,
    point_acc,
    tile_frame,
    tile_block,
    tile_count,
    block_slot,
    sems,
    list_sems,
):
    frame_blocks = poses.shape[0]
    point_blocks = window.shape[0]
    chunk_tiles = obs.shape[1] // chunks

    def chunk_copy(c):
        part = pl.ds(c * chunk_tiles, chunk_tiles)
        return pltpu.make_async_copy(obs_far.at[:, part], obs.at[:, part], sems.at[2 + c])

    window_copy = pltpu.make_async_copy(window_far, window, sems.at[0])
    pose_copy = pltpu.make_async_copy(poses_far, poses, sems.at[1])
    window_copy.start()
    pose_copy.start()
    lists = [
        pltpu.make_async_copy(source, target, list_sems.at[n])
        for n, (source, target) in enumerate(
            (
                (frame_list_far, tile_frame),
                (block_list_far, tile_block),
                (count_far, tile_count),
                (slot_far, block_slot),
            )
        )
    ]
    for copy in lists:
        copy.start()
    for c in range(chunks):
        chunk_copy(c).start()
    frame_acc[...] = jnp.zeros_like(frame_acc)
    point_acc[...] = jnp.zeros_like(point_acc)
    sub = lax.broadcasted_iota(jnp.int32, (8, 128), 0)
    lane = lax.broadcasted_iota(jnp.int32, (8, 128), 1)
    wide_upper = lax.broadcasted_iota(jnp.int32, (HALF, 128), 1) >= TILE

    window_copy.wait()

    @pl.loop(0, point_blocks, step=8)
    def _(start):
        for u in range(8):
            block = start + u
            line = window[pl.ds(block, 1), :]
            both = []
            for k in range(3):
                part = line[:, k * TILE : (k + 1) * TILE]
                both.append(jnp.concatenate([part, part], axis=1))
                point_wide[block, k : k + 1, :] = both[k]
            rows = point_features(both, sub, lane)
            high, low = split_rows(jnp.concatenate(rows, axis=0))
            point_feat[block, 0:32, :] = high
            point_feat[block, 32:64, :] = low

    pose_copy.wait()

    @pl.loop(0, frame_blocks, step=4)
    def _(start):
        for u in range(4):
            block = start + u
            mine = poses[block, 0:8, :]
            rows = frame_features(mine, sub, lane)
            high, low = split_rows(jnp.concatenate(rows, axis=0))
            frame_feat[block, 0:32, 0:128] = high
            frame_feat[block, 0:32, 128:256] = high
            frame_feat[block, 32:64, 0:128] = low
            frame_feat[block, 32:64, 128:256] = jnp.zeros_like(low)
            columns = jnp.transpose(mine)
            for k in range(6):
                column = columns[:, k : k + 1]
                pose_wide[block, k] = jnp.where(
                    wide_upper,
                    jnp.broadcast_to(column[HALF:], (HALF, 128)),
                    jnp.broadcast_to(column[:HALF], (HALF, 128)),
                )

    def one_tile(slot):
        live = slot < tile_count[0]
        f = jnp.where(live, tile_frame[slot], 0)
        p = jnp.where(live, block_slot[0, tile_block[slot]], 0)
        measured = [obs[k, slot] for k in range(3)]
        x = [point_wide[p, k : k + 1, :] for k in range(3)]
        w = [pose_wide[f, k] for k in range(3)]
        turned = cross_product(w, x)
        residual = [
            (x[k] + turned[k]) + (pose_wide[f, 3 + k] - measured[k]) for k in range(3)
        ]
        squared = (
            residual[0] * residual[0] + residual[1] * residual[1] + residual[2] * residual[2]
        )
        divisor = 1.0 + squared * (1.0 / robust_scale)
        weight = pl.reciprocal(divisor, approx=True)
        weight = jnp.where(live, 1.0, 0.0) * (weight * (2.0 - divisor * weight))
        images = jnp.concatenate(
            [weight] + [weight * measured[k] for k in range(3)], axis=0
        )
        stacked = jnp.concatenate(split_rows(images), axis=0)
        by_point = lax.dot_general(
            frame_feat[f], stacked, (((1,), (0,)), ((), ())), preferred_element_type=jnp.float32
        )
        by_frame = lax.dot_general(
            point_feat[p], stacked, (((1,), (1,)), ((), ())), preferred_element_type=jnp.float32
        )
        sums = (
            by_point[0:32] + by_point[32:64],
            by_frame[0:32, 0:128] + by_frame[0:32, 128:256] + by_frame[32:64, 0:128],
        )
        return f, p, sums

    for copy in lists:
        copy.wait()
    for c in range(chunks):
        chunk_copy(c).wait()
        here = jnp.clip(tile_count[0] - c * chunk_tiles, 0, chunk_tiles)

        @pl.loop(0, (here + unroll - 1) // unroll)
        def _(group):
            done = []
            for u in range(unroll):
                done.append(one_tile(c * chunk_tiles + group * unroll + u))
            for f, p, sums in done:
                point_acc[p] += sums[0]
                frame_acc[f] += sums[1]

    for block in range(frame_blocks):
        total = frame_acc[block]
        frame_out[block, 0:8, :] = total[0:8] + total[16:24]
        frame_out[block, 8:16, :] = jnp.where(
            lane < HALF, total[8:16], pltpu.roll(total[24:32], HALF, 1)
        )

    @pl.loop(0, point_blocks, step=4)
    def _(start):
        for u in range(4):
            total = point_acc[start + u]
            point_out[start + u] = jnp.where(
                lane >= TILE,
                pltpu.roll(total[8:16], TILE, 1) + total[24:32],
                total[0:8] + pltpu.roll(total[16:24], TILE, 1),
            )


def tile_sums(poses, window, packed, tile_frame, tile_block, tile_count, block_slot):
    slots = packed.shape[1]
    frame_blocks, point_blocks = poses.shape[0], window.shape[0]
    chunks = 2 if slots % 2 == 0 else 1
    unroll = max(u for u in (1, 2, 3, 4, 6, 8) if slots // chunks % u == 0)
    far = pl.BlockSpec(memory_space=pl.ANY)
    vmem = pl.BlockSpec(memory_space=pltpu.VMEM)
    return pl.pallas_call(
        functools.partial(tiles_kernel, chunks, unroll),
        in_specs=[far] * 7,
        out_specs=[vmem] * 2,
        scratch_shapes=[
            pltpu.VMEM(poses.shape, jnp.float32),
            pltpu.VMEM(window.shape, jnp.float32),
            pltpu.VMEM(packed.shape, jnp.float32),
            pltpu.VMEM((frame_blocks, 64, 256), jnp.bfloat16),
            pltpu.VMEM((point_blocks, 64, 128), jnp.bfloat16),
            pltpu.VMEM((frame_blocks, 6, HALF, 128), jnp.float32),
            pltpu.VMEM((point_blocks, 8, 128), jnp.float32),
            pltpu.VMEM((frame_blocks, 32, 128), jnp.float32),
            pltpu.VMEM((point_blocks, 32, 128), jnp.float32),
            pltpu.SMEM(tile_frame.shape, jnp.int32),
            pltpu.SMEM(tile_block.shape, jnp.int32),
            pltpu.SMEM(tile_count.shape, jnp.int32),
            pltpu.SMEM(block_slot.shape, jnp.int32),
            pltpu.SemaphoreType.DMA((2 + chunks,)),
            pltpu.SemaphoreType.DMA((4,)),
        ],
        out_shape=[
            jax.ShapeDtypeStruct((frame_blocks, 16, 128), jnp.float32),
            jax.ShapeDtypeStruct((point_blocks, 8, 128), jnp.float32),
        ],
        compiler_params=pltpu.CompilerParams(vmem_limit_bytes=VMEM_LIMIT),
        name="tile_sums",
    )(tile_frame, tile_block, tile_count, block_slot, poses, window, packed)


def ring_peers(count):
    me = lax.axis_index("lm")
    return me, [lax.rem(me + d, count) for d in range(1, count)]


def greet(peers, row, rows):
    barrier = pltpu.get_barrier_semaphore()
    for peer in peers:
        pl.semaphore_signal(barrier, inc=1, device_id=(row, peer), device_id_type=MESH)
    if rows is None:
        pl.semaphore_wait(barrier, len(peers))
        return
    me = lax.axis_index("lm")

    @pl.when(row > 0)
    def _():
        pl.semaphore_signal(barrier, inc=1, device_id=(row - 1, me), device_id_type=MESH)

    @pl.when(row < rows - 1)
    def _():
        pl.semaphore_signal(barrier, inc=1, device_id=(row + 1, me), device_id_type=MESH)

    edges = jnp.minimum(row, 1) + jnp.minimum(rows - 1 - row, 1)
    pl.semaphore_wait(barrier, len(peers) + edges)


def prepare_kernel(
    count,
    poses_far,
    odometry_far,
    info_far,
    landmarks_far,
    obs_far,
    state_out,
    links_out,
    own_out,
    window_out,
    packed_far,
    camera_poses,
    odometry,
    odometry_info,
    landmarks,
    state,
    links,
    own,
    obs,
    packed,
    send_sem,
    recv_sem,
    load_sem,
    store_sem,
):
    row = lax.axis_index("tm")
    me, peers = ring_peers(count)
    blocks = own.shape[0]
    frame_blocks = state.shape[0]
    slots = obs.shape[3]
    own_rows = pl.ds(pl.multiple_of(me * blocks, blocks), blocks)
    loads = [
        pltpu.make_async_copy(source, target, load_sem.at[n])
        for n, (source, target) in enumerate(
            (
                (obs_far.at[0], obs.at[0]),
                (landmarks_far, landmarks),
                (poses_far, camera_poses),
                (odometry_far, odometry),
                (info_far, odometry_info),
                (obs_far.at[1], obs.at[1]),
                (obs_far.at[2], obs.at[2]),
            )
        )
    ]
    for load in loads:
        load.start()
    stores = []

    def store(source, target):
        stores.append(pltpu.make_async_copy(source, target, store_sem.at[len(stores)]))
        stores[-1].start()

    own[...] = jnp.zeros_like(own)
    state[...] = jnp.zeros_like(state)
    links[...] = jnp.zeros_like(links)
    loads[1].wait()
    for block in range(blocks):
        for k in range(3):
            own[block : block + 1, k * TILE : (k + 1) * TILE] = landmarks[
                k : k + 1, block * TILE : (block + 1) * TILE
            ]
    greet(peers, row, None)
    copies = []
    for d, peer in enumerate(peers):
        copies.append(
            pltpu.make_async_remote_copy(
                src_ref=own,
                dst_ref=window_out.at[own_rows],
                send_sem=send_sem.at[d],
                recv_sem=recv_sem.at[d],
                device_id=(row, peer),
                device_id_type=MESH,
            )
        )
        copies[-1].start()
    store(own, window_out.at[own_rows])
    store(own, own_out)
    for load in loads[2:5]:
        load.wait()
    for block in range(frame_blocks):
        here = slice(block * TILE, (block + 1) * TILE)
        state[block, 0:6, :] = camera_poses[:, here]
        links[block, 0:6, :] = odometry[:, here]
        links[block, 6:7, :] = odometry_info[:, here]
    store(state, state_out)
    store(links, links_out)

    row_id = lax.broadcasted_iota(jnp.int32, (slots, slots), 0)
    column_id = lax.broadcasted_iota(jnp.int32, (slots, slots), 1)
    identity = jnp.where(row_id == column_id, 1.0, 0.0).astype(jnp.bfloat16)
    for k in range(3):
        loads[(0, 5, 6)[k]].wait()

        @pl.loop(0, HALF, step=8)
        def _(start):
            turned = []
            for u in range(8):
                pairs = jnp.concatenate(
                    [obs[k, start + u], obs[k, start + u + HALF]], axis=0
                )
                turned.append(
                    lax.dot_general(
                        identity,
                        pairs,
                        (((1,), (1,)), ((), ())),
                        preferred_element_type=jnp.float32,
                    )
                )
            here = pl.ds(pl.multiple_of(start, 8), 8)
            packed[k, :, here, :] = jnp.swapaxes(jnp.stack(turned), 0, 1)

        store(packed.at[k], packed_far.at[k])
    for copy in copies + stores:
        copy.wait()


def prepare(camera_poses, odometry, odometry_info, landmarks, observations, count):
    slots = observations.shape[0]
    frame_blocks = camera_poses.shape[1] // TILE
    blocks = landmarks.shape[1] // TILE
    by_tile = jnp.transpose(observations, (1, 2, 3, 0))
    far = pl.BlockSpec(memory_space=pl.ANY)
    info = odometry_info[None, :]
    inputs = (camera_poses, odometry, info, landmarks, by_tile)
    state_shape = (frame_blocks, 8, TILE)
    own_shape = (blocks, 4 * TILE)
    packed_shape = (3, slots, HALF, 128)
    shapes = [state_shape, state_shape, own_shape, (blocks * count, 4 * TILE), packed_shape]
    return pl.pallas_call(
        functools.partial(prepare_kernel, count),
        out_shape=[jax.ShapeDtypeStruct(shape, jnp.float32) for shape in shapes],
        in_specs=[far] * 5,
        out_specs=[far] * 5,
        scratch_shapes=[pltpu.VMEM(a.shape, jnp.float32) for a in inputs[:4]]
        + [pltpu.VMEM(shape, jnp.float32) for shape in shapes[:3]]
        + [
            pltpu.VMEM(by_tile.shape, jnp.bfloat16),
            pltpu.VMEM(packed_shape, jnp.float32),
            pltpu.SemaphoreType.DMA((count - 1,)),
            pltpu.SemaphoreType.DMA((count - 1,)),
            pltpu.SemaphoreType.DMA((7,)),
            pltpu.SemaphoreType.DMA((7,)),
        ],
        compiler_params=pltpu.CompilerParams(
            collective_id=0, has_side_effects=True, vmem_limit_bytes=VMEM_LIMIT
        ),
        name="prepare",
    )(*inputs)


def link_terms(state, links, before, links_before, after, final):
    current = [state[:, k, :] for k in range(6)]
    weight_before = links_before[:, 6, :]
    weight_after = jnp.where(final, 0.0, links[:, 6, :])
    link_grad = []
    for k in range(6):
        ahead = after[:, k, :] - current[k] - links[:, k, :]
        behind = current[k] - before[:, k, :] - links_before[:, k, :]
        link_grad.append(weight_before * behind - weight_after * ahead)
    return current, link_grad, weight_after + weight_before + damping


def pose_update(total, current, link_grad, diagonal_add):
    def both(row_low, row_high, start):
        return jnp.concatenate(
            [total[:, row_low, start : start + HALF], total[:, row_high, start : start + HALF]],
            axis=1,
        )

    counted = both(0, 4, 0)
    centroid = [both(1 + k, 5 + k, 0) for k in range(3)]
    moments = [total[:, 8 + m, 0:TILE] for m in range(6)]
    seen = [both(0, 4, HALF * (1 + k)) for k in range(3)]

    def lever(a, k):
        return both(1 + a, 5 + a, HALF * (1 + k))

    w, t = current[0:3], current[3:6]
    turned = cross_product(w, centroid)
    grad_off = [centroid[k] + turned[k] + t[k] * counted - seen[k] for k in range(3)]
    matrix_rows = [
        [moments[0], moments[3], moments[4]],
        [moments[3], moments[1], moments[5]],
        [moments[4], moments[5], moments[2]],
    ]
    trace = moments[0] + moments[1] + moments[2]
    pushed = cross_product(centroid, t)
    grad_rot = []
    for k in range(3):
        a, b = (k + 1) % 3, (k + 2) % 3
        product = (
            matrix_rows[k][0] * w[0] + matrix_rows[k][1] * w[1] + matrix_rows[k][2] * w[2]
        )
        grad_rot.append(trace * w[k] - product + pushed[k] - (lever(a, b) - lever(b, a)))

    zero_entry = jnp.zeros_like(counted)
    rotation_block = [
        [moments[1] + moments[2] + diagonal_add, -moments[3], -moments[4]],
        [-moments[3], moments[0] + moments[2] + diagonal_add, -moments[5]],
        [-moments[4], -moments[5], moments[0] + moments[1] + diagonal_add],
    ]
    cross_block = [
        [zero_entry, -centroid[2], centroid[1]],
        [centroid[2], zero_entry, -centroid[0]],
        [-centroid[1], centroid[0], zero_entry],
    ]
    matrix = [rotation_block[i] + cross_block[i] for i in range(3)]
    for i in range(3):
        offset_row = [counted + diagonal_add if i == k else zero_entry for k in range(3)]
        matrix.append([cross_block[k][i] for k in range(3)] + offset_row)
    sums = grad_rot + grad_off
    step = block_solve(matrix, [sums[k] + link_grad[k] for k in range(6)])
    return step


def point_update(total, own):
    x = [own[:, k * TILE : (k + 1) * TILE] for k in range(3)]
    spread = total[:, 3, 0:TILE]
    outer = [total[:, 4 + m, 0:TILE] for m in range(4)]
    outer += [total[:, m, TILE:] for m in range(2)]
    rows = [
        [outer[0], outer[3], outer[4]],
        [outer[3], outer[1], outer[5]],
        [outer[4], outer[5], outer[2]],
    ]
    gradient = [
        total[:, k, 0:TILE]
        + spread * x[k]
        - (rows[k][0] * x[0] + rows[k][1] * x[1] + rows[k][2] * x[2])
        for k in range(3)
    ]
    diagonal = spread + damping
    matrix = [
        [diagonal - outer[0], -outer[3], -outer[4]],
        [-outer[3], diagonal - outer[1], -outer[5]],
        [-outer[4], -outer[5], diagonal - outer[2]],
    ]
    step = block_solve(matrix, gradient)
    return x, step


def exchange_kernel(count, rows, last, frame_far, point_far, state_far, links_far, own_far, *refs):
    pose_out, own_out = refs[:2]
    window_out = None if last else refs[2]
    (
        frame_in,
        point_in,
        edge_in,
        extended,
        extended_links,
        own,
        fresh,
        fresh_points,
        send_sem,
        recv_sem,
        edge_send,
        edge_recv,
        load_sem,
        store_sem,
    ) = refs[2 if last else 3 :]
    row = lax.axis_index("tm")
    me, peers = ring_peers(count)
    frame_blocks = state_far.shape[0]
    share = frame_blocks // count
    own_blocks = own_far.shape[0]
    here = pl.ds(me * share, share)
    here_points = pl.ds(pl.multiple_of(me * own_blocks, own_blocks), own_blocks)
    greet(peers, row, rows)

    def send(group, d, peer, source, target):
        copy = pltpu.make_async_remote_copy(
            src_ref=source,
            dst_ref=target,
            send_sem=send_sem.at[group, d],
            recv_sem=recv_sem.at[group, d],
            device_id=(row, peer),
            device_id_type=MESH,
        )
        copy.start()
        return copy

    def edge(side, target_row):
        source = (
            state_far.at[frame_blocks - 1],
            links_far.at[frame_blocks - 1],
            state_far.at[0],
        )[side]
        return pltpu.make_async_remote_copy(
            src_ref=source,
            dst_ref=edge_in.at[side],
            send_sem=edge_send.at[side],
            recv_sem=edge_recv.at[side],
            device_id=(target_row, me),
            device_id_type=MESH,
        )

    frame_copies = [
        send(0, d, peer, frame_far.at[pl.ds(peer * share, share)], frame_in.at[d])
        for d, peer in enumerate(peers)
    ]

    @pl.when(row < rows - 1)
    def _():
        edge(0, row + 1).start()
        edge(1, row + 1).start()

    @pl.when(row > 0)
    def _():
        edge(2, row - 1).start()

    point_copies = [
        send(1, d, peer, point_far.at[pl.ds(peer * own_blocks, own_blocks)], point_in.at[d])
        for d, peer in enumerate(peers)
    ]
    loads = [
        pltpu.make_async_copy(source, target, load_sem.at[n])
        for n, (source, target) in enumerate(
            (
                (state_far, extended.at[pl.ds(1, frame_blocks)]),
                (links_far, extended_links.at[pl.ds(1, frame_blocks)]),
                (frame_far.at[here], frame_in.at[count - 1]),
                (point_far.at[pl.ds(me * own_blocks, own_blocks)], point_in.at[count - 1]),
                (own_far, own),
            )
        )
    ]
    for load in loads:
        load.start()
    extended[0] = jnp.zeros_like(extended[0])
    extended[frame_blocks + 1] = jnp.zeros_like(extended[0])
    extended_links[0] = jnp.zeros_like(extended_links[0])
    for load in loads:
        load.wait()
    @pl.when(row > 0)
    def _():
        edge(0, row - 1).wait_recv()
        edge(1, row - 1).wait_recv()
        extended[0] = edge_in[0]
        extended_links[0] = edge_in[1]

    @pl.when(row < rows - 1)
    def _():
        edge(2, row + 1).wait_recv()
        extended[frame_blocks + 1] = edge_in[2]

    first = me * share

    def shifted(earlier, current):
        return jnp.concatenate([earlier[:, :, TILE - 1 :], current[:, :, : TILE - 1]], axis=2)

    mine = extended[pl.ds(first + 1, share)]
    mine_links = extended_links[pl.ds(first + 1, share)]
    ahead = extended[pl.ds(first + 2, share)]
    after = jnp.concatenate([mine[:, :, 1:], ahead[:, :, :1]], axis=2)
    before = shifted(extended[pl.ds(first, share)], mine)
    links_before = shifted(extended_links[pl.ds(first, share)], mine_links)
    block_index = lax.broadcasted_iota(jnp.int32, (share, TILE), 0) + first
    lane = lax.broadcasted_iota(jnp.int32, (share, TILE), 1)
    final = (block_index * TILE + lane) == jnp.where(
        row == rows - 1, frame_blocks * TILE - 1, -1
    )

    poses, link_grad, diagonal_add = link_terms(
        mine, mine_links, before, links_before, after, final
    )

    for copy in frame_copies + point_copies:
        copy.wait_recv()
    frame_total, point_total = frame_in[count - 1], point_in[count - 1]
    for d in range(count - 1):
        frame_total = frame_total + frame_in[d]
        point_total = point_total + point_in[d]
    pose_step = pose_update(frame_total, poses, link_grad, diagonal_add)
    points, point_step = point_update(point_total, own[...])
    fresh[...] = mine
    for k in range(6):
        fresh[:, k, :] = poses[k] - pose_step[k]
    gathers = [send(2, d, peer, fresh, pose_out.at[here]) for d, peer in enumerate(peers)]
    fresh_points[...] = own[...]
    for k in range(3):
        fresh_points[:, k * TILE : (k + 1) * TILE] = points[k] - point_step[k]
    targets = [(fresh, pose_out.at[here]), (fresh_points, own_out)]
    if not last:
        gathers += [
            send(3, d, peer, fresh_points, window_out.at[here_points])
            for d, peer in enumerate(peers)
        ]
        targets.append((fresh_points, window_out.at[here_points]))
    stores = [
        pltpu.make_async_copy(source, target, store_sem.at[n])
        for n, (source, target) in enumerate(targets)
    ]
    for copy in stores:
        copy.start()
    for copy in frame_copies + point_copies:
        copy.wait_send()
    for copy in gathers + stores:
        copy.wait()

    @pl.when(row < rows - 1)
    def _():
        edge(0, row + 1).wait_send()
        edge(1, row + 1).wait_send()

    @pl.when(row > 0)
    def _():
        edge(2, row - 1).wait_send()


def exchange(frame_sums, point_sums, state, links, own, count, rows, last):
    frame_blocks = state.shape[0]
    own_blocks = own.shape[0]
    share = frame_blocks // count
    far = pl.BlockSpec(memory_space=pl.ANY)
    shapes = [state.shape, own.shape]
    if not last:
        shapes.append((own_blocks * count,) + own.shape[1:])
    return pl.pallas_call(
        functools.partial(exchange_kernel, count, rows, last),
        out_shape=[jax.ShapeDtypeStruct(shape, jnp.float32) for shape in shapes],
        in_specs=[far] * 5,
        out_specs=[far] * len(shapes),
        scratch_shapes=[
            pltpu.VMEM((count, share, 16, 128), jnp.float32),
            pltpu.VMEM((count, own_blocks, 8, 128), jnp.float32),
            pltpu.VMEM((3, 8, TILE), jnp.float32),
            pltpu.VMEM((frame_blocks + 2, 8, TILE), jnp.float32),
            pltpu.VMEM((frame_blocks + 2, 8, TILE), jnp.float32),
            pltpu.VMEM(own.shape, jnp.float32),
            pltpu.VMEM((share, 8, TILE), jnp.float32),
            pltpu.VMEM(own.shape, jnp.float32),
            pltpu.SemaphoreType.DMA((4, count - 1)),
            pltpu.SemaphoreType.DMA((4, count - 1)),
            pltpu.SemaphoreType.DMA((3,)),
            pltpu.SemaphoreType.DMA((3,)),
            pltpu.SemaphoreType.DMA((5,)),
            pltpu.SemaphoreType.DMA((3,)),
        ],
        compiler_params=pltpu.CompilerParams(
            collective_id=2 if last else 1,
            has_side_effects=True,
            vmem_limit_bytes=VMEM_LIMIT,
        ),
        name="exchange_last" if last else "exchange_first",
    )(frame_sums, point_sums, state, links, own)


def emit_kernel(state, own, poses, points):
    for pair in range(state.shape[0] // 2):
        here = slice(pair * 128, (pair + 1) * 128)
        poses[:, here] = jnp.concatenate(
            [state[2 * pair, 0:6, :], state[2 * pair + 1, 0:6, :]], axis=1
        )
    for pair in range(own.shape[0] // 2):
        here = slice(pair * 128, (pair + 1) * 128)
        for k in range(3):
            part = own[2 * pair : 2 * pair + 2, k * TILE : (k + 1) * TILE]
            points[k : k + 1, here] = jnp.concatenate([part[0:1], part[1:2]], axis=1)


def emit(state, own):
    vmem = pl.BlockSpec(memory_space=pltpu.VMEM)
    return pl.pallas_call(
        emit_kernel,
        in_specs=[vmem] * 2,
        out_specs=[vmem] * 2,
        out_shape=[
            jax.ShapeDtypeStruct((6, state.shape[0] * TILE), jnp.float32),
            jax.ShapeDtypeStruct((3, own.shape[0] * TILE), jnp.float32),
        ],
        compiler_params=pltpu.CompilerParams(vmem_limit_bytes=VMEM_LIMIT),
        name="emit",
    )(state, own)


def on_device(
    camera_poses,
    landmarks,
    odometry,
    odometry_info,
    observations,
    tile_frame,
    tile_block,
    tile_count,
    block_slot,
):
    rows, count = lax.axis_size("tm"), lax.axis_size("lm")
    state, links, own, window, packed = prepare(
        camera_poses, odometry, odometry_info, landmarks, observations, count
    )
    for iteration in range(ITERS - 1):
        sums = tile_sums(state, window, packed, tile_frame, tile_block, tile_count, block_slot)
        state, own, window = exchange(*sums, state, links, own, count, rows, False)
    sums = tile_sums(state, window, packed, tile_frame, tile_block, tile_count, block_slot)
    state, own = exchange(*sums, state, links, own, count, rows, True)
    return tuple(emit(state, own))


def solution(mesh):
    return jax.shard_map(
        on_device,
        mesh=mesh,
        in_specs=(
            P(None, "tm"),
            P(None, ("tm", "lm")),
            P(None, "tm"),
            P("tm"),
            P(("tm", "lm"), None, None, None),
            P(("tm", "lm")),
            P(("tm", "lm")),
            P(("tm", "lm")),
            P("tm", None),
        ),
        out_specs=(P(None, "tm"), P(None, ("tm", "lm"))),
        check_vma=False,
    )
```

```python
import functools

import jax
import jax.numpy as jnp
from jax import lax
from jax.experimental import pallas as pl
from jax.experimental.pallas import tpu as pltpu
from jax.sharding import PartitionSpec as P

TILE = 64
HALF = 32
ITERS = 2
VMEM_LIMIT = 60 * 1024 * 1024
MESH = pl.DeviceIdType.MESH

robust_scale = 4.0
damping = 1.0
moment_pairs = ((0, 0), (1, 1), (2, 2), (0, 1), (0, 2), (1, 2))


def cross_product(left, right):
    return [
        left[1] * right[2] - left[2] * right[1],
        left[2] * right[0] - left[0] * right[2],
        left[0] * right[1] - left[1] * right[0],
    ]


def block_solve(matrix, vector):
    dimension = len(vector)
    factor = [[None] * dimension for i in range(dimension)]
    inverse_diag = [None] * dimension
    for i in range(dimension):
        for j in range(i + 1):
            running = matrix[i][j]
            for k in range(j):
                running = running - factor[i][k] * factor[j][k]
            if i == j:
                factor[i][i] = jnp.sqrt(running)
                inverse_diag[i] = 1.0 / factor[i][i]
            else:
                factor[i][j] = running * inverse_diag[j]
    forward = [None] * dimension
    for i in range(dimension):
        running = vector[i]
        for k in range(i):
            running = running - factor[i][k] * forward[k]
        forward[i] = running * inverse_diag[i]
    solution = [None] * dimension
    for i in reversed(range(dimension)):
        running = forward[i]
        for k in range(i + 1, dimension):
            running = running - factor[k][i] * solution[k]
        solution[i] = running * inverse_diag[i]
    return solution


def split_rows(value):
    high = value.astype(jnp.bfloat16)
    low = (value - high.astype(jnp.float32)).astype(jnp.bfloat16)
    return high, low


def pick_rows(rows, sub, default=0.0):
    value = jnp.full(sub.shape, default, jnp.float32)
    for s, row in rows.items():
        value = jnp.where(sub == s, row, value)
    return value


def frame_features(block_poses, sub, lane):
    image = lane // HALF
    first = image == 0
    features = []
    for half in range(2):
        part = block_poses[:, half * HALF : (half + 1) * HALF]
        part = jnp.concatenate([part] * 4, axis=1)
        value = [jnp.broadcast_to(part[k : k + 1], (8, 128)) for k in range(6)]
        w, t = value[0:3], value[3:6]
        turned = cross_product(w, t)
        rows = {}
        for m in range(3):
            a, b = (m + 1) % 3, (m + 2) % 3
            row = jnp.where(first, t[m] - turned[m], 0.0)
            row = jnp.where(image == 1 + m, -1.0, row)
            row = jnp.where(image == 1 + b, w[a], row)
            rows[m] = jnp.where(image == 1 + a, -w[b], row)
        square = w[0] * w[0] + w[1] * w[1] + w[2] * w[2]
        rows[3] = jnp.where(first, 1.0 + square, 0.0)
        products = [jnp.where(first, w[a] * w[b], 0.0) for a, b in moment_pairs]
        for m in range(4):
            rows[4 + m] = products[m]
        features.append(pick_rows(rows, sub))
        features.append(pick_rows({0: products[4], 1: products[5]}, sub))
    return features


def point_features(block_points, sub, lane):
    upper = lane >= TILE
    x = [jnp.broadcast_to(block_points[k], (8, 128)) for k in range(3)]
    low = pick_rows({1: x[0], 2: x[1], 3: x[2]}, sub, 1.0)
    high = pick_rows({5: x[0], 6: x[1], 7: x[2]}, sub, 1.0)
    low = jnp.where((sub < 4) & jnp.logical_not(upper), low, 0.0)
    high = jnp.where((sub >= 4) & upper, high, 0.0)
    left = pick_rows({m: x[a] for m, (a, b) in enumerate(moment_pairs)}, sub)
    right = pick_rows({m: x[b] for m, (a, b) in enumerate(moment_pairs)}, sub)
    moments = left * right
    return [
        low,
        jnp.where(upper, 0.0, moments),
        high,
        jnp.where(upper, moments, 0.0),
    ]


def tiles_kernel(
    chunks,
    unroll,
    frame_list_far,
    block_list_far,
    count_far,
    slot_far,
    poses_far,
    window_far,
    obs_far,
    frame_out,
    point_out,
    poses,
    window,
    obs,
    frame_feat,
    point_feat,
    pose_wide,
    point_wide,
    frame_acc,
    point_acc,
    tile_frame,
    tile_block,
    tile_count,
    block_slot,
    sems,
    list_sems,
):
    frame_blocks = poses.shape[0]
    point_blocks = window.shape[0]
    chunk_tiles = obs.shape[1] // chunks

    def chunk_copy(c):
        part = pl.ds(c * chunk_tiles, chunk_tiles)
        return pltpu.make_async_copy(obs_far.at[:, part], obs.at[:, part], sems.at[2 + c])

    window_copy = pltpu.make_async_copy(window_far, window, sems.at[0])
    pose_copy = pltpu.make_async_copy(poses_far, poses, sems.at[1])
    window_copy.start()
    pose_copy.start()
    lists = [
        pltpu.make_async_copy(source, target, list_sems.at[n])
        for n, (source, target) in enumerate(
            (
                (frame_list_far, tile_frame),
                (block_list_far, tile_block),
                (count_far, tile_count),
                (slot_far, block_slot),
            )
        )
    ]
    for copy in lists:
        copy.start()
    for c in range(chunks):
        chunk_copy(c).start()
    frame_acc[...] = jnp.zeros_like(frame_acc)
    point_acc[...] = jnp.zeros_like(point_acc)
    sub = lax.broadcasted_iota(jnp.int32, (8, 128), 0)
    lane = lax.broadcasted_iota(jnp.int32, (8, 128), 1)
    wide_upper = lax.broadcasted_iota(jnp.int32, (HALF, 128), 1) >= TILE

    window_copy.wait()

    @pl.loop(0, point_blocks, step=8)
    def _(start):
        for u in range(8):
            block = start + u
            line = window[pl.ds(block, 1), :]
            both = []
            for k in range(3):
                part = line[:, k * TILE : (k + 1) * TILE]
                both.append(jnp.concatenate([part, part], axis=1))
                point_wide[block, k : k + 1, :] = both[k]
            rows = point_features(both, sub, lane)
            high, low = split_rows(jnp.concatenate(rows, axis=0))
            point_feat[block, 0:32, :] = high
            point_feat[block, 32:64, :] = low

    pose_copy.wait()

    @pl.loop(0, frame_blocks, step=4)
    def _(start):
        for u in range(4):
            block = start + u
            mine = poses[block, 0:8, :]
            rows = frame_features(mine, sub, lane)
            high, low = split_rows(jnp.concatenate(rows, axis=0))
            frame_feat[block, 0:32, 0:128] = high
            frame_feat[block, 0:32, 128:256] = high
            frame_feat[block, 32:64, 0:128] = low
            frame_feat[block, 32:64, 128:256] = jnp.zeros_like(low)
            columns = jnp.transpose(mine)
            for k in range(6):
                column = columns[:, k : k + 1]
                pose_wide[block, k] = jnp.where(
                    wide_upper,
                    jnp.broadcast_to(column[HALF:], (HALF, 128)),
                    jnp.broadcast_to(column[:HALF], (HALF, 128)),
                )

    def one_tile(slot):
        live = slot < tile_count[0]
        f = jnp.where(live, tile_frame[slot], 0)
        p = jnp.where(live, block_slot[0, tile_block[slot]], 0)
        measured = [obs[k, slot] for k in range(3)]
        x = [point_wide[p, k : k + 1, :] for k in range(3)]
        w = [pose_wide[f, k] for k in range(3)]
        turned = cross_product(w, x)
        residual = [
            (x[k] + turned[k]) + (pose_wide[f, 3 + k] - measured[k]) for k in range(3)
        ]
        squared = (
            residual[0] * residual[0] + residual[1] * residual[1] + residual[2] * residual[2]
        )
        divisor = 1.0 + squared * (1.0 / robust_scale)
        weight = pl.reciprocal(divisor, approx=True)
        weight = jnp.where(live, 1.0, 0.0) * (weight * (2.0 - divisor * weight))
        images = jnp.concatenate(
            [weight] + [weight * measured[k] for k in range(3)], axis=0
        )
        stacked = jnp.concatenate(split_rows(images), axis=0)
        by_point = lax.dot_general(
            frame_feat[f], stacked, (((1,), (0,)), ((), ())), preferred_element_type=jnp.float32
        )
        by_frame = lax.dot_general(
            point_feat[p], stacked, (((1,), (1,)), ((), ())), preferred_element_type=jnp.float32
        )
        sums = (
            by_point[0:32] + by_point[32:64],
            by_frame[0:32, 0:128] + by_frame[0:32, 128:256] + by_frame[32:64, 0:128],
        )
        return f, p, sums

    for copy in lists:
        copy.wait()
    for c in range(chunks):
        chunk_copy(c).wait()
        here = jnp.clip(tile_count[0] - c * chunk_tiles, 0, chunk_tiles)

        @pl.loop(0, (here + unroll - 1) // unroll)
        def _(group):
            done = []
            for u in range(unroll):
                done.append(one_tile(c * chunk_tiles + group * unroll + u))
            for f, p, sums in done:
                point_acc[p] += sums[0]
                frame_acc[f] += sums[1]

    for block in range(frame_blocks):
        total = frame_acc[block]
        frame_out[block, 0:8, :] = total[0:8] + total[16:24]
        frame_out[block, 8:16, :] = jnp.where(
            lane < HALF, total[8:16], pltpu.roll(total[24:32], HALF, 1)
        )

    @pl.loop(0, point_blocks, step=4)
    def _(start):
        for u in range(4):
            total = point_acc[start + u]
            point_out[start + u] = jnp.where(
                lane >= TILE,
                pltpu.roll(total[8:16], TILE, 1) + total[24:32],
                total[0:8] + pltpu.roll(total[16:24], TILE, 1),
            )


def tile_sums(poses, window, packed, tile_frame, tile_block, tile_count, block_slot):
    slots = packed.shape[1]
    frame_blocks, point_blocks = poses.shape[0], window.shape[0]
    chunks = 2 if slots % 2 == 0 else 1
    unroll = max(u for u in (1, 2, 3, 4, 6, 8) if slots // chunks % u == 0)
    far = pl.BlockSpec(memory_space=pl.ANY)
    vmem = pl.BlockSpec(memory_space=pltpu.VMEM)
    return pl.pallas_call(
        functools.partial(tiles_kernel, chunks, unroll),
        in_specs=[far] * 7,
        out_specs=[vmem] * 2,
        scratch_shapes=[
            pltpu.VMEM(poses.shape, jnp.float32),
            pltpu.VMEM(window.shape, jnp.float32),
            pltpu.VMEM(packed.shape, jnp.float32),
            pltpu.VMEM((frame_blocks, 64, 256), jnp.bfloat16),
            pltpu.VMEM((point_blocks, 64, 128), jnp.bfloat16),
            pltpu.VMEM((frame_blocks, 6, HALF, 128), jnp.float32),
            pltpu.VMEM((point_blocks, 8, 128), jnp.float32),
            pltpu.VMEM((frame_blocks, 32, 128), jnp.float32),
            pltpu.VMEM((point_blocks, 32, 128), jnp.float32),
            pltpu.SMEM(tile_frame.shape, jnp.int32),
            pltpu.SMEM(tile_block.shape, jnp.int32),
            pltpu.SMEM(tile_count.shape, jnp.int32),
            pltpu.SMEM(block_slot.shape, jnp.int32),
            pltpu.SemaphoreType.DMA((2 + chunks,)),
            pltpu.SemaphoreType.DMA((4,)),
        ],
        out_shape=[
            jax.ShapeDtypeStruct((frame_blocks, 16, 128), jnp.float32),
            jax.ShapeDtypeStruct((point_blocks, 8, 128), jnp.float32),
        ],
        compiler_params=pltpu.CompilerParams(vmem_limit_bytes=VMEM_LIMIT),
        name="tile_sums",
    )(tile_frame, tile_block, tile_count, block_slot, poses, window, packed)


def ring_peers(count):
    me = lax.axis_index("lm")
    return me, [lax.rem(me + d, count) for d in range(1, count)]


def greet(peers, row, rows):
    barrier = pltpu.get_barrier_semaphore()
    for peer in peers:
        pl.semaphore_signal(barrier, inc=1, device_id=(row, peer), device_id_type=MESH)
    if rows is None:
        pl.semaphore_wait(barrier, len(peers))
        return
    me = lax.axis_index("lm")

    @pl.when(row > 0)
    def _():
        pl.semaphore_signal(barrier, inc=1, device_id=(row - 1, me), device_id_type=MESH)

    @pl.when(row < rows - 1)
    def _():
        pl.semaphore_signal(barrier, inc=1, device_id=(row + 1, me), device_id_type=MESH)

    edges = jnp.minimum(row, 1) + jnp.minimum(rows - 1 - row, 1)
    pl.semaphore_wait(barrier, len(peers) + edges)


def prepare_kernel(
    count,
    poses_far,
    odometry_far,
    info_far,
    landmarks_far,
    obs_far,
    state_out,
    links_out,
    own_out,
    window_out,
    packed_far,
    camera_poses,
    odometry,
    odometry_info,
    landmarks,
    state,
    links,
    own,
    obs,
    packed,
    send_sem,
    recv_sem,
    load_sem,
    store_sem,
):
    row = lax.axis_index("tm")
    me, peers = ring_peers(count)
    blocks = own.shape[0]
    frame_blocks = state.shape[0]
    slots = obs.shape[3]
    own_rows = pl.ds(pl.multiple_of(me * blocks, blocks), blocks)
    loads = [
        pltpu.make_async_copy(source, target, load_sem.at[n])
        for n, (source, target) in enumerate(
            (
                (obs_far.at[0], obs.at[0]),
                (landmarks_far, landmarks),
                (poses_far, camera_poses),
                (odometry_far, odometry),
                (info_far, odometry_info),
                (obs_far.at[1], obs.at[1]),
                (obs_far.at[2], obs.at[2]),
            )
        )
    ]
    for load in loads:
        load.start()
    stores = []

    def store(source, target):
        stores.append(pltpu.make_async_copy(source, target, store_sem.at[len(stores)]))
        stores[-1].start()

    own[...] = jnp.zeros_like(own)
    state[...] = jnp.zeros_like(state)
    links[...] = jnp.zeros_like(links)
    loads[1].wait()
    for block in range(blocks):
        for k in range(3):
            own[block : block + 1, k * TILE : (k + 1) * TILE] = landmarks[
                k : k + 1, block * TILE : (block + 1) * TILE
            ]
    greet(peers, row, None)
    copies = []
    for d, peer in enumerate(peers):
        copies.append(
            pltpu.make_async_remote_copy(
                src_ref=own,
                dst_ref=window_out.at[own_rows],
                send_sem=send_sem.at[d],
                recv_sem=recv_sem.at[d],
                device_id=(row, peer),
                device_id_type=MESH,
            )
        )
        copies[-1].start()
    store(own, window_out.at[own_rows])
    store(own, own_out)
    for load in loads[2:5]:
        load.wait()
    for block in range(frame_blocks):
        here = slice(block * TILE, (block + 1) * TILE)
        state[block, 0:6, :] = camera_poses[:, here]
        links[block, 0:6, :] = odometry[:, here]
        links[block, 6:7, :] = odometry_info[:, here]
    store(state, state_out)
    store(links, links_out)

    row_id = lax.broadcasted_iota(jnp.int32, (slots, slots), 0)
    column_id = lax.broadcasted_iota(jnp.int32, (slots, slots), 1)
    identity = jnp.where(row_id == column_id, 1.0, 0.0).astype(jnp.bfloat16)
    for k in range(3):
        loads[(0, 5, 6)[k]].wait()

        @pl.loop(0, HALF, step=8, unroll=2)
        def _(start):
            turned = []
            for u in range(8):
                pairs = jnp.concatenate(
                    [obs[k, start + u], obs[k, start + u + HALF]], axis=0
                )
                turned.append(
                    lax.dot_general(
                        identity,
                        pairs,
                        (((1,), (1,)), ((), ())),
                        preferred_element_type=jnp.float32,
                    )
                )
            here = pl.ds(pl.multiple_of(start, 8), 8)
            packed[k, :, here, :] = jnp.swapaxes(jnp.stack(turned), 0, 1)

        store(packed.at[k], packed_far.at[k])
    for copy in copies + stores:
        copy.wait()


def prepare(camera_poses, odometry, odometry_info, landmarks, observations, count):
    slots = observations.shape[0]
    frame_blocks = camera_poses.shape[1] // TILE
    blocks = landmarks.shape[1] // TILE
    by_tile = jnp.transpose(observations, (1, 2, 3, 0))
    far = pl.BlockSpec(memory_space=pl.ANY)
    info = odometry_info[None, :]
    inputs = (camera_poses, odometry, info, landmarks, by_tile)
    state_shape = (frame_blocks, 8, TILE)
    own_shape = (blocks, 4 * TILE)
    packed_shape = (3, slots, HALF, 128)
    shapes = [state_shape, state_shape, own_shape, (blocks * count, 4 * TILE), packed_shape]
    return pl.pallas_call(
        functools.partial(prepare_kernel, count),
        out_shape=[jax.ShapeDtypeStruct(shape, jnp.float32) for shape in shapes],
        in_specs=[far] * 5,
        out_specs=[far] * 5,
        scratch_shapes=[pltpu.VMEM(a.shape, jnp.float32) for a in inputs[:4]]
        + [pltpu.VMEM(shape, jnp.float32) for shape in shapes[:3]]
        + [
            pltpu.VMEM(by_tile.shape, jnp.bfloat16),
            pltpu.VMEM(packed_shape, jnp.float32),
            pltpu.SemaphoreType.DMA((count - 1,)),
            pltpu.SemaphoreType.DMA((count - 1,)),
            pltpu.SemaphoreType.DMA((7,)),
            pltpu.SemaphoreType.DMA((7,)),
        ],
        compiler_params=pltpu.CompilerParams(
            collective_id=0, has_side_effects=True, vmem_limit_bytes=VMEM_LIMIT
        ),
        name="prepare",
    )(*inputs)


def link_terms(state, links, before, links_before, after, final):
    current = [state[:, k, :] for k in range(6)]
    weight_before = links_before[:, 6, :]
    weight_after = jnp.where(final, 0.0, links[:, 6, :])
    link_grad = []
    for k in range(6):
        ahead = after[:, k, :] - current[k] - links[:, k, :]
        behind = current[k] - before[:, k, :] - links_before[:, k, :]
        link_grad.append(weight_before * behind - weight_after * ahead)
    return current, link_grad, weight_after + weight_before + damping


def pose_update(total, current, link_grad, diagonal_add):
    def both(row_low, row_high, start):
        return jnp.concatenate(
            [total[:, row_low, start : start + HALF], total[:, row_high, start : start + HALF]],
            axis=1,
        )

    counted = both(0, 4, 0)
    centroid = [both(1 + k, 5 + k, 0) for k in range(3)]
    moments = [total[:, 8 + m, 0:TILE] for m in range(6)]
    seen = [both(0, 4, HALF * (1 + k)) for k in range(3)]

    def lever(a, k):
        return both(1 + a, 5 + a, HALF * (1 + k))

    w, t = current[0:3], current[3:6]
    turned = cross_product(w, centroid)
    grad_off = [centroid[k] + turned[k] + t[k] * counted - seen[k] for k in range(3)]
    matrix_rows = [
        [moments[0], moments[3], moments[4]],
        [moments[3], moments[1], moments[5]],
        [moments[4], moments[5], moments[2]],
    ]
    trace = moments[0] + moments[1] + moments[2]
    pushed = cross_product(centroid, t)
    grad_rot = []
    for k in range(3):
        a, b = (k + 1) % 3, (k + 2) % 3
        product = (
            matrix_rows[k][0] * w[0] + matrix_rows[k][1] * w[1] + matrix_rows[k][2] * w[2]
        )
        grad_rot.append(trace * w[k] - product + pushed[k] - (lever(a, b) - lever(b, a)))

    zero_entry = jnp.zeros_like(counted)
    rotation_block = [
        [moments[1] + moments[2] + diagonal_add, -moments[3], -moments[4]],
        [-moments[3], moments[0] + moments[2] + diagonal_add, -moments[5]],
        [-moments[4], -moments[5], moments[0] + moments[1] + diagonal_add],
    ]
    cross_block = [
        [zero_entry, -centroid[2], centroid[1]],
        [centroid[2], zero_entry, -centroid[0]],
        [-centroid[1], centroid[0], zero_entry],
    ]
    matrix = [rotation_block[i] + cross_block[i] for i in range(3)]
    for i in range(3):
        offset_row = [counted + diagonal_add if i == k else zero_entry for k in range(3)]
        matrix.append([cross_block[k][i] for k in range(3)] + offset_row)
    sums = grad_rot + grad_off
    step = block_solve(matrix, [sums[k] + link_grad[k] for k in range(6)])
    return step


def point_update(total, own):
    x = [own[:, k * TILE : (k + 1) * TILE] for k in range(3)]
    spread = total[:, 3, 0:TILE]
    outer = [total[:, 4 + m, 0:TILE] for m in range(4)]
    outer += [total[:, m, TILE:] for m in range(2)]
    rows = [
        [outer[0], outer[3], outer[4]],
        [outer[3], outer[1], outer[5]],
        [outer[4], outer[5], outer[2]],
    ]
    gradient = [
        total[:, k, 0:TILE]
        + spread * x[k]
        - (rows[k][0] * x[0] + rows[k][1] * x[1] + rows[k][2] * x[2])
        for k in range(3)
    ]
    diagonal = spread + damping
    matrix = [
        [diagonal - outer[0], -outer[3], -outer[4]],
        [-outer[3], diagonal - outer[1], -outer[5]],
        [-outer[4], -outer[5], diagonal - outer[2]],
    ]
    step = block_solve(matrix, gradient)
    return x, step


def exchange_kernel(count, rows, last, frame_far, point_far, state_far, links_far, own_far, *refs):
    pose_out, own_out = refs[:2]
    window_out = None if last else refs[2]
    (
        frame_in,
        point_in,
        edge_in,
        extended,
        extended_links,
        own,
        fresh,
        fresh_points,
        send_sem,
        recv_sem,
        edge_send,
        edge_recv,
        load_sem,
        store_sem,
    ) = refs[2 if last else 3 :]
    row = lax.axis_index("tm")
    me, peers = ring_peers(count)
    frame_blocks = state_far.shape[0]
    share = frame_blocks // count
    own_blocks = own_far.shape[0]
    here = pl.ds(me * share, share)
    here_points = pl.ds(pl.multiple_of(me * own_blocks, own_blocks), own_blocks)
    greet(peers, row, rows)

    def send(group, d, peer, source, target):
        copy = pltpu.make_async_remote_copy(
            src_ref=source,
            dst_ref=target,
            send_sem=send_sem.at[group, d],
            recv_sem=recv_sem.at[group, d],
            device_id=(row, peer),
            device_id_type=MESH,
        )
        copy.start()
        return copy

    def edge(side, target_row):
        source = (
            state_far.at[frame_blocks - 1],
            links_far.at[frame_blocks - 1],
            state_far.at[0],
        )[side]
        return pltpu.make_async_remote_copy(
            src_ref=source,
            dst_ref=edge_in.at[side],
            send_sem=edge_send.at[side],
            recv_sem=edge_recv.at[side],
            device_id=(target_row, me),
            device_id_type=MESH,
        )

    frame_copies = [
        send(0, d, peer, frame_far.at[pl.ds(peer * share, share)], frame_in.at[d])
        for d, peer in enumerate(peers)
    ]

    @pl.when(row < rows - 1)
    def _():
        edge(0, row + 1).start()
        edge(1, row + 1).start()

    @pl.when(row > 0)
    def _():
        edge(2, row - 1).start()

    point_copies = [
        send(1, d, peer, point_far.at[pl.ds(peer * own_blocks, own_blocks)], point_in.at[d])
        for d, peer in enumerate(peers)
    ]
    loads = [
        pltpu.make_async_copy(source, target, load_sem.at[n])
        for n, (source, target) in enumerate(
            (
                (state_far, extended.at[pl.ds(1, frame_blocks)]),
                (links_far, extended_links.at[pl.ds(1, frame_blocks)]),
                (frame_far.at[here], frame_in.at[count - 1]),
                (point_far.at[pl.ds(me * own_blocks, own_blocks)], point_in.at[count - 1]),
                (own_far, own),
            )
        )
    ]
    for load in loads:
        load.start()
    extended[0] = jnp.zeros_like(extended[0])
    extended[frame_blocks + 1] = jnp.zeros_like(extended[0])
    extended_links[0] = jnp.zeros_like(extended_links[0])
    for load in loads:
        load.wait()
    @pl.when(row > 0)
    def _():
        edge(0, row - 1).wait_recv()
        edge(1, row - 1).wait_recv()
        extended[0] = edge_in[0]
        extended_links[0] = edge_in[1]

    @pl.when(row < rows - 1)
    def _():
        edge(2, row + 1).wait_recv()
        extended[frame_blocks + 1] = edge_in[2]

    first = me * share

    def shifted(earlier, current):
        return jnp.concatenate([earlier[:, :, TILE - 1 :], current[:, :, : TILE - 1]], axis=2)

    mine = extended[pl.ds(first + 1, share)]
    mine_links = extended_links[pl.ds(first + 1, share)]
    ahead = extended[pl.ds(first + 2, share)]
    after = jnp.concatenate([mine[:, :, 1:], ahead[:, :, :1]], axis=2)
    before = shifted(extended[pl.ds(first, share)], mine)
    links_before = shifted(extended_links[pl.ds(first, share)], mine_links)
    block_index = lax.broadcasted_iota(jnp.int32, (share, TILE), 0) + first
    lane = lax.broadcasted_iota(jnp.int32, (share, TILE), 1)
    final = (block_index * TILE + lane) == jnp.where(
        row == rows - 1, frame_blocks * TILE - 1, -1
    )

    poses, link_grad, diagonal_add = link_terms(
        mine, mine_links, before, links_before, after, final
    )

    for copy in frame_copies + point_copies:
        copy.wait_recv()
    frame_total, point_total = frame_in[count - 1], point_in[count - 1]
    for d in range(count - 1):
        frame_total = frame_total + frame_in[d]
        point_total = point_total + point_in[d]
    pose_step = pose_update(frame_total, poses, link_grad, diagonal_add)
    points, point_step = point_update(point_total, own[...])
    fresh[...] = mine
    for k in range(6):
        fresh[:, k, :] = poses[k] - pose_step[k]
    gathers = [send(2, d, peer, fresh, pose_out.at[here]) for d, peer in enumerate(peers)]
    fresh_points[...] = own[...]
    for k in range(3):
        fresh_points[:, k * TILE : (k + 1) * TILE] = points[k] - point_step[k]
    targets = [(fresh, pose_out.at[here]), (fresh_points, own_out)]
    if not last:
        gathers += [
            send(3, d, peer, fresh_points, window_out.at[here_points])
            for d, peer in enumerate(peers)
        ]
        targets.append((fresh_points, window_out.at[here_points]))
    stores = [
        pltpu.make_async_copy(source, target, store_sem.at[n])
        for n, (source, target) in enumerate(targets)
    ]
    for copy in stores:
        copy.start()
    for copy in frame_copies + point_copies:
        copy.wait_send()
    for copy in gathers + stores:
        copy.wait()

    @pl.when(row < rows - 1)
    def _():
        edge(0, row + 1).wait_send()
        edge(1, row + 1).wait_send()

    @pl.when(row > 0)
    def _():
        edge(2, row - 1).wait_send()


def exchange(frame_sums, point_sums, state, links, own, count, rows, last):
    frame_blocks = state.shape[0]
    own_blocks = own.shape[0]
    share = frame_blocks // count
    far = pl.BlockSpec(memory_space=pl.ANY)
    shapes = [state.shape, own.shape]
    if not last:
        shapes.append((own_blocks * count,) + own.shape[1:])
    return pl.pallas_call(
        functools.partial(exchange_kernel, count, rows, last),
        out_shape=[jax.ShapeDtypeStruct(shape, jnp.float32) for shape in shapes],
        in_specs=[far] * 5,
        out_specs=[far] * len(shapes),
        scratch_shapes=[
            pltpu.VMEM((count, share, 16, 128), jnp.float32),
            pltpu.VMEM((count, own_blocks, 8, 128), jnp.float32),
            pltpu.VMEM((3, 8, TILE), jnp.float32),
            pltpu.VMEM((frame_blocks + 2, 8, TILE), jnp.float32),
            pltpu.VMEM((frame_blocks + 2, 8, TILE), jnp.float32),
            pltpu.VMEM(own.shape, jnp.float32),
            pltpu.VMEM((share, 8, TILE), jnp.float32),
            pltpu.VMEM(own.shape, jnp.float32),
            pltpu.SemaphoreType.DMA((4, count - 1)),
            pltpu.SemaphoreType.DMA((4, count - 1)),
            pltpu.SemaphoreType.DMA((3,)),
            pltpu.SemaphoreType.DMA((3,)),
            pltpu.SemaphoreType.DMA((5,)),
            pltpu.SemaphoreType.DMA((3,)),
        ],
        compiler_params=pltpu.CompilerParams(
            collective_id=2 if last else 1,
            has_side_effects=True,
            vmem_limit_bytes=VMEM_LIMIT,
        ),
        name="exchange_last" if last else "exchange_first",
    )(frame_sums, point_sums, state, links, own)


def emit_kernel(state, own, poses, points):
    for pair in range(state.shape[0] // 2):
        here = slice(pair * 128, (pair + 1) * 128)
        poses[:, here] = jnp.concatenate(
            [state[2 * pair, 0:6, :], state[2 * pair + 1, 0:6, :]], axis=1
        )
    for pair in range(own.shape[0] // 2):
        here = slice(pair * 128, (pair + 1) * 128)
        for k in range(3):
            part = own[2 * pair : 2 * pair + 2, k * TILE : (k + 1) * TILE]
            points[k : k + 1, here] = jnp.concatenate([part[0:1], part[1:2]], axis=1)


def emit(state, own):
    vmem = pl.BlockSpec(memory_space=pltpu.VMEM)
    return pl.pallas_call(
        emit_kernel,
        in_specs=[vmem] * 2,
        out_specs=[vmem] * 2,
        out_shape=[
            jax.ShapeDtypeStruct((6, state.shape[0] * TILE), jnp.float32),
            jax.ShapeDtypeStruct((3, own.shape[0] * TILE), jnp.float32),
        ],
        compiler_params=pltpu.CompilerParams(vmem_limit_bytes=VMEM_LIMIT),
        name="emit",
    )(state, own)


def on_device(
    camera_poses,
    landmarks,
    odometry,
    odometry_info,
    observations,
    tile_frame,
    tile_block,
    tile_count,
    block_slot,
):
    rows, count = lax.axis_size("tm"), lax.axis_size("lm")
    state, links, own, window, packed = prepare(
        camera_poses, odometry, odometry_info, landmarks, observations, count
    )
    for iteration in range(ITERS - 1):
        sums = tile_sums(state, window, packed, tile_frame, tile_block, tile_count, block_slot)
        state, own, window = exchange(*sums, state, links, own, count, rows, False)
    sums = tile_sums(state, window, packed, tile_frame, tile_block, tile_count, block_slot)
    state, own = exchange(*sums, state, links, own, count, rows, True)
    return tuple(emit(state, own))


def solution(mesh):
    return jax.shard_map(
        on_device,
        mesh=mesh,
        in_specs=(
            P(None, "tm"),
            P(None, ("tm", "lm")),
            P(None, "tm"),
            P("tm"),
            P(("tm", "lm"), None, None, None),
            P(("tm", "lm")),
            P(("tm", "lm")),
            P(("tm", "lm")),
            P("tm", None),
        ),
        out_specs=(P(None, "tm"), P(None, ("tm", "lm"))),
        check_vma=False,
    )
```
